32 devices in a mesh: seq: 8 (over z, y), head: 4 (over x, core).
Axes of the slice: x: 2, y: 2, z: 4, core: 2. Of those that a mesh axis runs over, the one named last changes fastest.
Arguments:
- inputs: bfloat16 [4, 4096, 1024], P(None, 'seq'), may hold values from -6 to 6
- cotangent: bfloat16 [4, 4096, 1024], P(None, 'seq'), may hold values from -6 to 6
- lengths: int32 [4], replicated, may hold values from 1024 to 4096, as said below
- norm_gain: float32 [1024], replicated, may hold values from 0.5 to 1.5
- norm_gain_mean: float32 [1024], replicated, may hold values from -40 to 40
- norm_gain_square: float32 [1024], replicated, may hold values from 216.2688 to 861.7984
- proj_zx: float32 [1024, 2, 2048], P(None, None, 'head'), may hold values from -2 to 2
- proj_zx_mean: float32 [1024, 2, 2048], P(None, None, 'head'), may hold values from -24 to 24
- proj_zx_square: float32 [1024, 2, 2048], P(None, None, 'head'), may hold values from 77.66016 to 311.296
- proj_bc: float32 [1024, 256], replicated, may hold values from -0.1875 to 0.1875
- proj_bc_mean: float32 [1024, 256], replicated, may hold values from -24 to 24
- proj_bc_square: float32 [1024, 256], replicated, may hold values from 77.66016 to 311.296
- proj_step: float32 [1024, 32], P(None, 'head'), may hold values from -0.1875 to 0.1875
- proj_step_mean: float32 [1024, 32], P(None, 'head'), may hold values from -24 to 24
- proj_step_square: float32 [1024, 32], P(None, 'head'), may hold values from 77.66016 to 311.296
- conv_inner: float32 [5, 2048], P(None, 'head'), may hold values from -3 to 3
- conv_inner_mean: float32 [5, 2048], P(None, 'head'), may hold values from -24 to 24
- conv_inner_square: float32 [5, 2048], P(None, 'head'), may hold values from 77.66016 to 311.296
- conv_bc: float32 [5, 256], replicated, may hold values from -3 to 3
- conv_bc_mean: float32 [5, 256], replicated, may hold values from -24 to 24
- conv_bc_square: float32 [5, 256], replicated, may hold values from 77.66016 to 311.296
- head_params: float32 [3, 32], P(None, 'head'), may hold values from -16 to 16
- head_params_mean: float32 [3, 32], P(None, 'head'), may hold values from -160 to 160
- head_params_square: float32 [3, 32], P(None, 'head'), may hold values from 3440.64 to 13762.56
- gate_gain: float32 [2048], P('head'), may hold values from 0.5 to 1.5
- gate_gain_mean: float32 [2048], P('head'), may hold values from -40 to 40
- gate_gain_square: float32 [2048], P('head'), may hold values from 216.2688 to 861.7984
- proj_out: float32 [1024, 2048], P(None, 'head'), may hold values from -0.125 to 0.125
- proj_out_mean: float32 [1024, 2048], P(None, 'head'), may hold values from -64 to 64
- proj_out_square: float32 [1024, 2048], P(None, 'head'), may hold values from 552.1408 to 2211.84
Outputs:
- block_out: bfloat16 [4, 4096, 1024], P(None, 'seq')
- input_grad: float32 [4, 4096, 1024], P(None, 'seq')
- norm_gain_mean_new: float32 [1024], replicated
- norm_gain_square_new: float32 [1024], replicated
- norm_gain_new: float32 [1024], replicated
- proj_zx_mean_new: float32 [1024, 2, 2048], P(None, None, 'head')
- proj_zx_square_new: float32 [1024, 2, 2048], P(None, None, 'head')
- proj_zx_new: float32 [1024, 2, 2048], P(None, None, 'head')
- proj_bc_mean_new: float32 [1024, 256], replicated
- proj_bc_square_new: float32 [1024, 256], replicated
- proj_bc_new: float32 [1024, 256], replicated
- proj_step_mean_new: float32 [1024, 32], P(None, 'head')
- proj_step_square_new: float32 [1024, 32], P(None, 'head')
- proj_step_new: float32 [1024, 32], P(None, 'head')
- conv_inner_mean_new: float32 [5, 2048], P(None, 'head')
- conv_inner_square_new: float32 [5, 2048], P(None, 'head')
- conv_inner_new: float32 [5, 2048], P(None, 'head')
- conv_bc_mean_new: float32 [5, 256], replicated
- conv_bc_square_new: float32 [5, 256], replicated
- conv_bc_new: float32 [5, 256], replicated
- head_params_mean_new: float32 [3, 32], P(None, 'head')
- head_params_square_new: float32 [3, 32], P(None, 'head')
- head_params_new: float32 [3, 32], P(None, 'head')
- gate_gain_mean_new: float32 [2048], P('head')
- gate_gain_square_new: float32 [2048], P('head')
- gate_gain_new: float32 [2048], P('head')
- proj_out_mean_new: float32 [1024, 2048], P(None, 'head')
- proj_out_square_new: float32 [1024, 2048], P(None, 'head')
- proj_out_new: float32 [1024, 2048], P(None, 'head')
The draws below stay inside these ranges and needn't reach their ends.
Inputs may be any that keep to these rules, and one draw needn't show every extreme that they name: `lengths`: one sequence has length 4096 and another has length 1024.
All inputs are finite; a program needn't handle non-finite values.
Results may differ from the reference program's by a relative error of at most 0.012.
The reference program's roundings to bfloat16 on the way count: a program that leaves them out, or rounds other values in their place, can miss the bound.
Values may be sent and summed in bfloat16 or wider, within the bound.
No kernel may reach another device: no remote copies, remote signals or barrier semaphores. Data moves between devices by JAX's collectives and lax.ppermute only.
A program may use at most 192 MiB of HBM per device.

```python
import math
import jax
import jax.numpy as jnp
from jax import lax

D = 1024
HEADS = 32
INNER = 2048
STATE = 128
CONV = 4
BLOCK_LEN = 256
STEP = 7
SEQS = 4
SEQ_LEN = 4096


def draw_lengths(key, part):
    key = jax.random.fold_in(key, 11)
    first_key, second_key = jax.random.split(key)
    seq_lengths = jax.random.randint(first_key, (SEQS,), SEQ_LEN // 4, SEQ_LEN + 1)
    ranking = jax.random.permutation(second_key, SEQS)
    seq_lengths = seq_lengths.at[ranking[0]].set(SEQ_LEN)
    seq_lengths = seq_lengths.at[ranking[1]].set(SEQ_LEN // 4)
    return seq_lengths.astype(jnp.int32)


def draw_proj_zx(key, part):
    key = jax.random.fold_in(key, 12)
    column = jnp.arange(INNER).astype(jnp.float32) / INNER
    random_part = jnp.clip(jax.random.normal(key, (D, 2, INNER), jnp.float32), -6.0, 6.0)
    column_scale = 0.6 * 3.0 ** column
    return random_part * column_scale / jnp.sqrt(jnp.float32(D))


def draw_head_params(key, part):
    key = jax.random.fold_in(key, 13)
    key_list = jax.random.split(key, 5)
    decay_log = jax.random.uniform(key_list[0], (HEADS,), jnp.float32, 0.0, 2.7)
    slow_share = 0.5
    is_slow = jax.random.uniform(key_list[1], (HEADS,), jnp.float32) < slow_share
    slow_rate = jnp.exp(jax.random.uniform(key_list[2], (HEADS,), jnp.float32, jnp.log(0.1 / SEQ_LEN), jnp.log(1.0 / SEQ_LEN)))
    fast_rate = jnp.exp(jax.random.uniform(key_list[3], (HEADS,), jnp.float32, jnp.log(1.0 / 50.0), jnp.log(1.0 / 30.0)))
    decay_rate = jnp.where(is_slow, slow_rate, fast_rate)
    step_target = decay_rate / jnp.exp(decay_log)
    step_bias = jnp.log(jnp.expm1(step_target))
    skip_gain = jax.random.uniform(key_list[4], (HEADS,), jnp.float32, 0.5, 1.5)
    return jnp.stack([decay_log, step_bias, skip_gain])


def block_levels(key, shape, cuts, smallest, top_value):
    loudness = 1.0
    for dim, parts in cuts:
        heights = jax.random.uniform(jax.random.fold_in(jax.random.fold_in(key, 6), dim), (parts,), jnp.float32, smallest / len(cuts), top_value / len(cuts))
        loudness = loudness * jnp.repeat(jnp.exp(heights), shape[dim] // parts).reshape((-1,) + (1,) * (len(shape) - 1 - dim))
    return loudness


def scatter_about(stream_key, dims, spread, bound, shards=(), dtype=jnp.bfloat16):
    loudness = block_levels(stream_key, dims, shards, -0.22, 0.18) if shards else 1.0
    array = jax.random.normal(stream_key, dims, jnp.float32) * spread * loudness
    return jnp.minimum(jnp.maximum(array, -bound), bound).astype(dtype)


def setup_inputs(seed: int = 0) -> dict:
    arg_keys = jax.random.split(jax.random.key(seed), 31)
    return {
        "inputs": scatter_about(arg_keys[0], (SEQS, SEQ_LEN, D), 1.0, 6.0, ((1, 8),)),
        "cotangent": scatter_about(arg_keys[1], (SEQS, SEQ_LEN, D), 1.0, 6.0, ((1, 8),)),
        "lengths": draw_lengths(jax.random.fold_in(arg_keys[30], 71), 0),
        "norm_gain": jnp.clip(1.0 + 0.1 * jax.random.normal(arg_keys[3], (D,), jnp.float32), 0.5, 1.5),
        "norm_gain_mean": scatter_about(arg_keys[4], (D,), (0.056 * (SEQS * SEQ_LEN) ** 0.5), 40.0, (), jnp.float32),
        "norm_gain_square": jnp.clip(jnp.exp(jax.random.uniform(arg_keys[5], (D,), jnp.float32, math.log(216.2688), math.log(861.7984))), 216.2688, 861.7984),
        "proj_zx": draw_proj_zx(jax.random.fold_in(arg_keys[30], 71), 0),
        "proj_zx_mean": scatter_about(arg_keys[7], (D, 2, INNER), (0.033 * (SEQS * SEQ_LEN) ** 0.5), 24.0, ((2, 4),), jnp.float32),
        "proj_zx_square": jnp.clip(jnp.exp(math.log(311.296) - 1.3884019 * jax.random.uniform(arg_keys[8], (D, 2, INNER), jnp.float32) ** block_levels(arg_keys[8], (D, 2, INNER), ((2, 4),), -0.2, 0.2)), 77.66016, 311.296),
        "proj_bc": scatter_about(arg_keys[9], (D, 2 * STATE), D ** -0.5, 0.1875, (), jnp.float32),
        "proj_bc_mean": scatter_about(arg_keys[10], (D, 2 * STATE), (0.033 * (SEQS * SEQ_LEN) ** 0.5), 24.0, (), jnp.float32),
        "proj_bc_square": jnp.clip(jnp.exp(jax.random.uniform(arg_keys[11], (D, 2 * STATE), jnp.float32, math.log(77.66016), math.log(311.296))), 77.66016, 311.296),
        "proj_step": scatter_about(arg_keys[12], (D, HEADS), D ** -0.5, 0.1875, ((1, 4),), jnp.float32),
        "proj_step_mean": scatter_about(arg_keys[13], (D, HEADS), (0.033 * (SEQS * SEQ_LEN) ** 0.5), 24.0, ((1, 4),), jnp.float32),
        "proj_step_square": jnp.clip(jnp.exp(math.log(311.296) - 1.3884019 * jax.random.uniform(arg_keys[14], (D, HEADS), jnp.float32) ** block_levels(arg_keys[14], (D, HEADS), ((1, 4),), -0.2, 0.2)), 77.66016, 311.296),
        "conv_inner": scatter_about(arg_keys[15], (CONV + 1, INNER), CONV ** -0.5, 3.0, ((1, 4),), jnp.float32),
        "conv_inner_mean": scatter_about(arg_keys[16], (CONV + 1, INNER), (0.033 * (SEQS * SEQ_LEN) ** 0.5), 24.0, ((1, 4),), jnp.float32),
        "conv_inner_square": jnp.clip(jnp.exp(math.log(311.296) - 1.3884019 * jax.random.uniform(arg_keys[17], (CONV + 1, INNER), jnp.float32) ** block_levels(arg_keys[17], (CONV + 1, INNER), ((1, 4),), -0.2, 0.2)), 77.66016, 311.296),
        "conv_bc": scatter_about(arg_keys[18], (CONV + 1, 2 * STATE), CONV ** -0.5, 3.0, (), jnp.float32),
        "conv_bc_mean": scatter_about(arg_keys[19], (CONV + 1, 2 * STATE), (0.033 * (SEQS * SEQ_LEN) ** 0.5), 24.0, (), jnp.float32),
        "conv_bc_square": jnp.clip(jnp.exp(jax.random.uniform(arg_keys[20], (CONV + 1, 2 * STATE), jnp.float32, math.log(77.66016), math.log(311.296))), 77.66016, 311.296),
        "head_params": draw_head_params(jax.random.fold_in(arg_keys[30], 71), 0),
        "head_params_mean": scatter_about(arg_keys[22], (3, HEADS), (0.22 * (SEQS * SEQ_LEN) ** 0.5), 160.0, ((1, 4),), jnp.float32),
        "head_params_square": jnp.clip(jnp.exp(math.log(13762.56) - 1.3862944 * jax.random.uniform(arg_keys[23], (3, HEADS), jnp.float32) ** block_levels(arg_keys[23], (3, HEADS), ((1, 4),), -0.2, 0.2)), 3440.64, 13762.56),
        "gate_gain": jnp.clip(1.0 + 0.1 * jax.random.normal(arg_keys[24], (INNER,), jnp.float32), 0.5, 1.5),
        "gate_gain_mean": scatter_about(arg_keys[25], (INNER,), (0.056 * (SEQS * SEQ_LEN) ** 0.5), 40.0, ((0, 4),), jnp.float32),
        "gate_gain_square": jnp.clip(jnp.exp(math.log(861.7984) - 1.3824993 * jax.random.uniform(arg_keys[26], (INNER,), jnp.float32) ** block_levels(arg_keys[26], (INNER,), ((0, 4),), -0.2, 0.2)), 216.2688, 861.7984),
        "proj_out": scatter_about(arg_keys[27], (D, INNER), INNER ** -0.5, 0.125, ((1, 4),), jnp.float32),
        "proj_out_mean": scatter_about(arg_keys[28], (D, INNER), (0.089 * (SEQS * SEQ_LEN) ** 0.5), 64.0, ((1, 4),), jnp.float32),
        "proj_out_square": jnp.clip(jnp.exp(math.log(2211.84) - 1.387777 * jax.random.uniform(arg_keys[29], (D, INNER), jnp.float32) ** block_levels(arg_keys[29], (D, INNER), ((1, 4),), -0.2, 0.2)), 552.1408, 2211.84),
    }


EPS = 1e-05
BETA_ONE = 0.9
BETA_TWO = 0.95
ADAM_EPS = 1e-08
LEARNING_RATES = (0.6, 0.09, 0.09, 0.09, 0.9, 0.9, 0.9, 0.6, 0.06)
WEIGHT_DECAYS = (0.0, 0.1, 0.1, 0.1, 0.0, 0.0, 0.0, 0.0, 0.1)
HIGHEST_PREC = lax.Precision.HIGHEST

@jax.custom_vjp
def low(v):
    return lax.optimization_barrier(v.astype(jnp.bfloat16)).astype(jnp.float32)

@jax.custom_vjp
def low_back(v):
    return v

def low_keep(v):
    return (low(v), None)

def low_pass(kept, grad):
    return (grad,)

def back_keep(v):
    return (v, None)

def back_low(kept, grad):
    return (low(grad),)
low.defvjp(low_keep, low_pass)
low_back.defvjp(back_keep, back_low)

def block_step(carried_state, block_inputs):
    x_block, b_block, c_block, decay_block, step_block = block_inputs
    cumulative = jnp.cumsum(decay_block, axis=-1)
    length = cumulative.shape[-1]
    causal = jnp.arange(length)[:, None] >= jnp.arange(length)[None, :]
    between = jnp.where(causal, cumulative[..., :, None] - cumulative[..., None, :], 0.0)
    scores = jnp.einsum('btn,bsn->bts', c_block, b_block, precision=HIGHEST_PREC)
    mixing = jnp.where(causal, jnp.exp(between), 0.0) * scores[:, None] * step_block[..., None, :]
    within = jnp.einsum('bhts,bhsp->bhtp', mixing, x_block, precision=HIGHEST_PREC)
    from_state = jnp.exp(cumulative)[..., None] * jnp.einsum('btn,bhpn->bhtp', c_block, carried_state, precision=HIGHEST_PREC)
    total_decay = cumulative[..., -1]
    weighted = x_block * (jnp.exp(total_decay[..., None] - cumulative) * step_block)[..., None]
    next_state = jnp.exp(total_decay)[..., None, None] * carried_state + jnp.einsum('bhsp,bsn->bhpn', weighted, b_block, precision=HIGHEST_PREC)
    return (next_state, within + from_state)

def scan_blocks(x_heads, b_values, c_values, log_decay, step_size, first_state):
    batch_size, head_count, token_count, head_width = x_heads.shape
    block_count = token_count // BLOCK_LEN
    x_parts = x_heads.reshape(batch_size, head_count, block_count, BLOCK_LEN, head_width).transpose(2, 0, 1, 3, 4)
    b_parts = b_values.reshape(batch_size, block_count, BLOCK_LEN, -1).transpose(1, 0, 2, 3)
    c_parts = c_values.reshape(batch_size, block_count, BLOCK_LEN, -1).transpose(1, 0, 2, 3)
    decay_parts = log_decay.reshape(batch_size, head_count, block_count, BLOCK_LEN).transpose(2, 0, 1, 3)
    step_parts = step_size.reshape(batch_size, head_count, block_count, BLOCK_LEN).transpose(2, 0, 1, 3)
    final_state, outputs = lax.scan(jax.checkpoint(block_step), first_state, (x_parts, b_parts, c_parts, decay_parts, step_parts))
    outputs = outputs.transpose(1, 2, 0, 3, 4).reshape(batch_size, head_count, token_count, head_width)
    return (outputs, final_state)

def forward(params, tokens):
    norm_gain, proj_zx, proj_bc, proj_step, conv_inner, conv_bc, head_params, gate_gain, proj_out = params
    batch_size, token_count, model_width = tokens.shape
    inner_width = proj_zx.shape[2]
    state_width = proj_bc.shape[1] // 2
    head_count = proj_step.shape[1]
    head_width = inner_width // head_count
    normed = low(tokens * lax.rsqrt(lax.optimization_barrier(jnp.mean(tokens * tokens, axis=-1, keepdims=True)) + EPS) * norm_gain)
    zx_values = low_back(jnp.einsum('btd,dki->btki', normed, low(proj_zx), precision=HIGHEST_PREC))
    bc_raw = low_back(jnp.einsum('btd,dc->btc', normed, low(proj_bc), precision=HIGHEST_PREC))
    raw_step = low_back(jnp.einsum('btd,dh->bth', normed, low(proj_step), precision=HIGHEST_PREC))
    gate_input = zx_values[:, :, 0]
    mixed_in = low(jnp.concatenate([zx_values[:, :, 1], bc_raw], axis=-1))
    conv_weight = jnp.concatenate([conv_inner, conv_bc], axis=-1)
    padded = jnp.pad(mixed_in, ((0, 0), (CONV - 1, 0), (0, 0)))
    convolved = conv_weight[CONV] + jnp.zeros_like(mixed_in)
    for tap_index in range(CONV):
        convolved = convolved + conv_weight[tap_index] * padded[:, tap_index:tap_index + token_count]
    activated = low(jax.nn.silu(convolved))
    x_values = activated[..., :inner_width]
    b_values = activated[..., inner_width:inner_width + state_width]
    c_values = activated[..., inner_width + state_width:]
    step_size = jax.nn.softplus(raw_step + head_params[1])
    log_decay = -step_size * jnp.exp(head_params[0])
    x_heads = x_values.reshape(batch_size, token_count, head_count, head_width).transpose(0, 2, 1, 3)
    first_state = jnp.zeros((batch_size, head_count, head_width, state_width), jnp.float32)
    outputs, final_state = scan_blocks(x_heads, b_values, c_values, log_decay.transpose(0, 2, 1), step_size.transpose(0, 2, 1), first_state)
    outputs = outputs + head_params[2][None, :, None, None] * x_heads
    scanned = outputs.transpose(0, 2, 1, 3).reshape(batch_size, token_count, inner_width)
    gated_values = scanned * jax.nn.silu(gate_input)
    out_scale = lax.rsqrt(lax.optimization_barrier(jnp.mean(gated_values * gated_values, axis=-1, keepdims=True)) + EPS)
    scaled = low(gated_values * gate_gain)
    projected = low_back(jnp.einsum('bti,di->btd', scaled, low(proj_out), precision=HIGHEST_PREC))
    return tokens + out_scale * projected

def adam_update(weight, mean_old, square_old, gradient, step_rate, decay_weight):
    mean_new = BETA_ONE * mean_old + (1.0 - BETA_ONE) * gradient
    square_new = BETA_TWO * square_old + (1.0 - BETA_TWO) * gradient * gradient
    corrected_mean = mean_new / (1.0 - BETA_ONE ** STEP)
    corrected_square = square_new / (1.0 - BETA_TWO ** STEP)
    weight_new = weight - step_rate * (corrected_mean / (jnp.sqrt(corrected_square) + ADAM_EPS) + decay_weight * weight)
    return (mean_new, square_new, weight_new)

def reference(inputs, cotangent, lengths, norm_gain, norm_gain_mean, norm_gain_square, proj_zx, proj_zx_mean, proj_zx_square, proj_bc, proj_bc_mean, proj_bc_square, proj_step, proj_step_mean, proj_step_square, conv_inner, conv_inner_mean, conv_inner_square, conv_bc, conv_bc_mean, conv_bc_square, head_params, head_params_mean, head_params_square, gate_gain, gate_gain_mean, gate_gain_square, proj_out, proj_out_mean, proj_out_square):
    params = (norm_gain, proj_zx, proj_bc, proj_step, conv_inner, conv_bc, head_params, gate_gain, proj_out)
    means = (norm_gain_mean, proj_zx_mean, proj_bc_mean, proj_step_mean, conv_inner_mean, conv_bc_mean, head_params_mean, gate_gain_mean, proj_out_mean)
    squares = (norm_gain_square, proj_zx_square, proj_bc_square, proj_step_square, conv_inner_square, conv_bc_square, head_params_square, gate_gain_square, proj_out_square)
    positions = jnp.arange(SEQ_LEN).astype(jnp.int32)

    def one_sequence(totals, sequence_items):
        tokens, seq_cotangent, seq_length = sequence_items
        tokens = tokens.astype(jnp.float32)[None]
        is_valid = (positions < seq_length).astype(jnp.float32)
        out_cotangent = seq_cotangent.astype(jnp.float32)[None] * is_valid[None, :, None]
        result, pullback = jax.vjp(forward, params, tokens)
        param_grads, token_grads = pullback(out_cotangent)
        totals = jax.tree.map(jnp.add, totals, param_grads)
        return (totals, (result[0].astype(jnp.bfloat16), token_grads[0]))
    zero_grads = jax.tree.map(jnp.zeros_like, params)
    summed_grads, (block_out, input_grad) = lax.scan(one_sequence, zero_grads, (inputs, cotangent, lengths))
    results = [block_out, input_grad]
    for weight, mean_old, square_old, gradient, step_rate, decay_weight in zip(params, means, squares, summed_grads, LEARNING_RATES, WEIGHT_DECAYS):
        results.extend(adam_update(weight, mean_old, square_old, gradient, step_rate, decay_weight))
    return tuple(results)
```

```python
import functools

import jax
import jax.numpy as jnp
from jax import lax
from jax.experimental import pallas as pl
from jax.experimental.pallas import tpu as pltpu
from jax.sharding import PartitionSpec as P

INNER = 2048
CONV = 4
CHUNK = 128
STEP = 7


EPS = 1e-05
BETA_ONE = 0.9
BETA_TWO = 0.95
ADAM_EPS = 1e-08
LEARNING_RATES = (0.6, 0.09, 0.09, 0.09, 0.9, 0.9, 0.9, 0.6, 0.06)
WEIGHT_DECAYS = (0.0, 0.1, 0.1, 0.1, 0.0, 0.0, 0.0, 0.0, 0.1)
HIGHEST_PREC = lax.Precision.HIGHEST
F32 = jnp.float32
BF16 = jnp.bfloat16


def passed_along(block, axis, distance):
    devices = range(lax.axis_size(axis))
    route = [(i - distance, i) for i in devices if i - distance in devices]
    return lax.ppermute(block, axis, route)


def swapped(block, axis, mask):
    return lax.ppermute(block, axis, [(i, i ^ mask) for i in range(lax.axis_size(axis))])


def halving_sum(part, axis):
    index = lax.axis_index(axis)
    masks = [1 << k for k in range(lax.axis_size(axis).bit_length() - 1)]
    rest = part.shape[1:]
    for mask in masks[:-1]:
        bit = (index // mask) % 2
        halves = part.reshape((2, part.shape[0] // 2) + rest)
        sent = lax.dynamic_index_in_dim(halves, 1 - bit, 0, keepdims=False)
        kept = lax.dynamic_index_in_dim(halves, bit, 0, keepdims=False)
        got = swapped(sent, axis, mask)
        part = (kept.astype(F32) + got.astype(F32)).astype(BF16)
    got = swapped(part, axis, masks[-1])
    part = (part.astype(F32) + got.astype(F32)).astype(BF16)
    for mask in reversed(masks[:-1]):
        bit = (index // mask) % 2
        got = swapped(part, axis, mask)
        first = jnp.where(bit == 0, part, got)
        second = jnp.where(bit == 0, got, part)
        part = jnp.concatenate([first, second], axis=0)
    return part


def dot(a, b, dims=((1,), (0,)), precision=None):
    return lax.dot_general(a, b, (dims, ((), ())), precision=precision, preferred_element_type=F32)


def expander(heads, width):
    row = lax.broadcasted_iota(jnp.int32, (heads, heads * width), 0)
    column = lax.broadcasted_iota(jnp.int32, (heads, heads * width), 1)
    inside = (column >= row * width) & (column < (row + 1) * width)
    return jnp.where(inside, 1.0, 0.0).astype(BF16)


def split_dot(a, b, dims):
    high = a.astype(BF16)
    low = (a - high.astype(F32)).astype(BF16)
    return dot(high, b, dims) + dot(low, b, dims)


def spread(a, expand):
    return split_dot(a, expand, ((1,), (0,)))


def head_sums(a, expand):
    return split_dot(a, expand, ((1,), (1,)))


def pair_rows(a):
    lane = lax.broadcasted_iota(jnp.int32, a.shape, 1)
    first = lane < a.shape[1] // 2
    zero = jnp.zeros_like(a)
    return jnp.concatenate([jnp.where(first, a, zero), jnp.where(first, zero, a)], axis=0)


def chunk_decays(decay, decay_t):
    q = decay.shape[0]
    row = lax.broadcasted_iota(jnp.int32, (q, q), 0)
    column = lax.broadcasted_iota(jnp.int32, (q, q), 1)
    lower = jnp.where(row >= column, 1.0, 0.0).astype(F32)
    cum = dot(lower, decay, precision=HIGHEST_PREC)
    cum_t = dot(decay_t, lower, ((1,), (1,)), precision=HIGHEST_PREC)
    return cum, cum_t, row, column


def scan_kernel(x_ref, b_ref, c_ref, step_ref, decay_ref, decay_t_ref, enter_ref, y_ref, in_ref, state):
    heads = step_ref.shape[2]
    width = x_ref.shape[2] // heads

    @pl.when(pl.program_id(1) == 0)
    def _():
        state[...] = enter_ref[0]

    expand = expander(heads, width)
    cum, cum_t, row, column = chunk_decays(decay_ref[0], decay_t_ref[0])
    causal = row >= column
    q = cum.shape[0]
    total = cum[q - 1 : q, :]
    b, c = b_ref[0], c_ref[0]
    x = x_ref[0].astype(F32)
    step = step_ref[0]
    xs = (x * spread(step, expand)).astype(BF16)
    grown = spread(jnp.exp(cum), expand)
    xw = (x * spread(step * jnp.exp(total - cum), expand)).astype(BF16)
    scores = dot(c, b, ((1,), (1,)))
    before = state[...]
    in_ref[0, 0] = before
    from_state = grown * dot(c, before.astype(BF16))
    for pair in range(heads // 2):
        lanes = slice(pair * 2 * width, (pair + 1) * 2 * width)
        mixing = []
        for h in (2 * pair, 2 * pair + 1):
            between = cum[:, h : h + 1] - cum_t[h : h + 1, :]
            mixing.append((jnp.exp(jnp.where(causal, between, -1e30)) * scores).astype(BF16))
        within = dot(jnp.concatenate(mixing, axis=1), pair_rows(xs[:, lanes]))
        y_ref[0, :, lanes] = within + from_state[:, lanes]
    state[...] = grown[q - 1 : q, :] * before + dot(b, xw, ((0,), (0,)))


def back_kernel(
    x_ref, b_ref, c_ref, step_ref, decay_ref, decay_t_ref, skip_ref, dy_ref, y_ref, in_ref, leave_ref,
    dx_ref, dbc_ref, ldg_ref, dstep_ref, dskip_ref, grad
):
    heads = step_ref.shape[2]
    width = x_ref.shape[2] // heads

    @pl.when(pl.program_id(1) == 0)
    def _():
        grad[...] = leave_ref[0]

    expand = expander(heads, width)
    cum, cum_t, row, column = chunk_decays(decay_ref[0], decay_t_ref[0])
    later = column >= row
    q = cum.shape[0]
    total = cum[q - 1 : q, :]
    b, c = b_ref[0], c_ref[0]
    x = x_ref[0].astype(F32)
    step = step_ref[0]
    step_wide = spread(step, expand)
    xs = (x * step_wide).astype(BF16)
    grown = spread(jnp.exp(cum), expand)
    waned = spread(jnp.exp(total - cum), expand)
    xw = (x * step_wide * waned).astype(BF16)
    dy = dy_ref[0]
    dy_low = dy.astype(BF16)
    edy = (dy * grown).astype(BF16)
    before = in_ref[0, 0]
    after_grad = grad[...]
    after_low = after_grad.astype(BF16)
    scores_t = dot(b, c, ((1,), (1,)))
    v_state = waned * dot(b, after_low)
    dscores_t = jnp.zeros((q, q), F32)
    v_parts = []
    for pair in range(heads // 2):
        lanes = slice(pair * 2 * width, (pair + 1) * 2 * width)
        dy_pair = pair_rows(dy_low[:, lanes])
        xs_pair = pair_rows(xs[:, lanes])
        dmix = dot(xs_pair, dy_low[:, lanes], ((1,), (1,)))
        mixing = []
        for k, h in enumerate((2 * pair, 2 * pair + 1)):
            between = cum_t[h : h + 1, :] - cum[:, h : h + 1]
            fade = jnp.exp(jnp.where(later, between, -1e30))
            mixing.append((fade * scores_t).astype(BF16))
            dscores_t = dscores_t + fade * dmix[k * q : (k + 1) * q]
        v_parts.append(dot(jnp.concatenate(mixing, axis=1), dy_pair))
    v = jnp.concatenate(v_parts, axis=1) + v_state
    xs_wide = xs.astype(F32)
    etotal = grown[q - 1 : q, :]
    dx_ref[0] = step_wide * v + skip_ref[0] * dy
    end_row = jnp.sum(xs_wide * v_state, axis=0, keepdims=True) + jnp.sum(
        etotal * before * after_grad, axis=0, keepdims=True
    )
    crossing = dy_low.astype(F32) * y_ref[0] - xs_wide * v
    last = lax.broadcasted_iota(jnp.int32, crossing.shape, 0) == q - 1
    crossing = crossing + jnp.where(last, end_row, 0.0)
    upper = jnp.where(column >= row, 1.0, 0.0).astype(F32)
    ldg_ref[0] = dot(upper, head_sums(crossing, expand), precision=HIGHEST_PREC)
    dstep_ref[0] = head_sums(x * v, expand)
    dskip_ref[0] = head_sums(x * dy, expand)
    dscores_low = dscores_t.astype(BF16)
    state = b.shape[1]
    dbc_ref[0, :, :state] = (
        dot(dscores_low, c) + dot(xw, after_low, ((1,), (1,)))
    ).astype(BF16)
    dbc_ref[0, :, state:] = (
        dot(dscores_low, b, ((0,), (0,))) + dot(edy, before.astype(BF16), ((1,), (1,)))
    ).astype(BF16)
    grad[...] = etotal * after_grad + dot(c, edy, ((0,), (0,)))


def scan_forward(x, b, c, step, decay, decay_t, enter):
    seqs, length, inner = x.shape
    state, heads = b.shape[2], step.shape[2]
    chunks = length // CHUNK

    def block(lanes):
        return pl.BlockSpec((1, CHUNK, lanes), lambda s, k: (s, k, 0))

    return pl.pallas_call(
        scan_kernel,
        grid=(seqs, chunks),
        in_specs=[
            block(inner),
            block(state),
            block(state),
            block(heads),
            block(heads),
            pl.BlockSpec((1, heads, CHUNK), lambda s, k: (s, 0, k)),
            pl.BlockSpec((1, state, inner), lambda s, k: (s, 0, 0)),
        ],
        out_specs=[
            block(inner),
            pl.BlockSpec((1, 1, state, inner), lambda s, k: (s, k, 0, 0)),
        ],
        out_shape=[
            jax.ShapeDtypeStruct((seqs, length, inner), F32),
            jax.ShapeDtypeStruct((seqs, chunks, state, inner), F32),
        ],
        scratch_shapes=[pltpu.VMEM((state, inner), F32)],
        compiler_params=pltpu.CompilerParams(vmem_limit_bytes=40 << 20),
    )(x, b, c, step, decay, decay_t, enter)


def scan_backward(x, b, c, step, decay, decay_t, skip, dy, y, states, leave):
    seqs, length, inner = x.shape
    state, heads = b.shape[2], step.shape[2]
    chunks = length // CHUNK

    def block(lanes):
        return pl.BlockSpec((1, CHUNK, lanes), lambda s, k: (s, chunks - 1 - k, 0))

    return pl.pallas_call(
        back_kernel,
        grid=(seqs, chunks),
        in_specs=[
            block(inner),
            block(state),
            block(state),
            block(heads),
            block(heads),
            pl.BlockSpec((1, heads, CHUNK), lambda s, k: (s, 0, chunks - 1 - k)),
            pl.BlockSpec((1, 1, inner), lambda s, k: (0, 0, 0)),
            block(inner),
            block(inner),
            pl.BlockSpec((1, 1, state, inner), lambda s, k: (s, chunks - 1 - k, 0, 0)),
            pl.BlockSpec((1, state, inner), lambda s, k: (s, 0, 0)),
        ],
        out_specs=[block(inner), block(2 * state), block(heads), block(heads), block(heads)],
        out_shape=[
            jax.ShapeDtypeStruct((seqs, length, inner), F32),
            jax.ShapeDtypeStruct((seqs, length, 2 * state), BF16),
            jax.ShapeDtypeStruct((seqs, length, heads), F32),
            jax.ShapeDtypeStruct((seqs, length, heads), F32),
            jax.ShapeDtypeStruct((seqs, length, heads), F32),
        ],
        scratch_shapes=[pltpu.VMEM((state, inner), F32)],
        compiler_params=pltpu.CompilerParams(vmem_limit_bytes=40 << 20),
    )(x, b, c, step, decay, decay_t, skip, dy, y, states, leave)


def silu_slope(values):
    sigmoid_part = jax.nn.sigmoid(values)
    return sigmoid_part * (1.0 + values * (1.0 - sigmoid_part))


def adam_update(weight, mean_old, square_old, gradient, step_rate, decay_weight):
    mean_new = BETA_ONE * mean_old + (1.0 - BETA_ONE) * gradient
    square_new = BETA_TWO * square_old + (1.0 - BETA_TWO) * gradient * gradient
    corrected_mean = mean_new / (1.0 - BETA_ONE**STEP)
    corrected_square = square_new / (1.0 - BETA_TWO**STEP)
    weight_new = weight - step_rate * (
        corrected_mean / (jnp.sqrt(corrected_square) + ADAM_EPS) + decay_weight * weight
    )
    return (mean_new, square_new, weight_new)


def shards(
    inputs,
    cotangent,
    lengths,
    norm_gain,
    norm_gain_mean,
    norm_gain_square,
    proj_zx,
    proj_zx_mean,
    proj_zx_square,
    proj_bc,
    proj_bc_mean,
    proj_bc_square,
    proj_step,
    proj_step_mean,
    proj_step_square,
    conv_inner,
    conv_inner_mean,
    conv_inner_square,
    conv_bc,
    conv_bc_mean,
    conv_bc_square,
    head_params,
    head_params_mean,
    head_params_square,
    gate_gain,
    gate_gain_mean,
    gate_gain_square,
    proj_out,
    proj_out_mean,
    proj_out_square,
):
    seq_count, local_len, model_width = inputs.shape
    local_inner = proj_zx.shape[2]
    state_width = proj_bc.shape[1] // 2
    local_heads = proj_step.shape[1]
    head_width = local_inner // local_heads
    rows = seq_count * local_len
    seq_size, seq_index = lax.axis_size("seq"), lax.axis_index("seq")

    def wide(a):
        selector = jnp.repeat(jnp.eye(local_heads, dtype=F32), head_width, axis=1)
        return jnp.einsum("...h,hc->...c", a, selector, precision=HIGHEST_PREC)

    positions = seq_index * local_len + jnp.arange(local_len)
    is_valid = (positions[None, :] < lengths[:, None]).astype(F32)
    tokens = inputs.astype(F32)
    inverse_rms = lax.rsqrt(jnp.mean(tokens * tokens, axis=-1, keepdims=True) + EPS)
    unit_tokens = tokens * inverse_rms
    normed = (unit_tokens * norm_gain).astype(BF16)
    z_weight = proj_zx[:, 0].astype(BF16)
    x_weight = proj_zx[:, 1].astype(BF16)
    bc_weight = proj_bc.astype(BF16)
    step_weight = proj_step.astype(BF16)
    out_weight = proj_out.astype(BF16)
    xbc_weight = jnp.concatenate([x_weight, bc_weight], axis=1)
    mixed_in = jnp.einsum("btd,dc->btc", normed, xbc_weight, preferred_element_type=F32).astype(BF16)
    edge_in = passed_along(mixed_in[:, local_len - CONV + 1 :], "seq", 1)
    raw_step = jnp.einsum("btd,dh->bth", normed, step_weight, preferred_element_type=F32)
    gate_input = jnp.einsum("btd,dc->btc", normed, z_weight, preferred_element_type=F32)
    padded = jnp.concatenate([edge_in, mixed_in], axis=1)
    conv_weight = jnp.concatenate([conv_inner, conv_bc], axis=-1)
    convolved = conv_weight[CONV] + jnp.zeros(mixed_in.shape, F32)
    for tap_index in range(CONV):
        convolved = (
            convolved + conv_weight[tap_index] * padded[:, tap_index : tap_index + local_len]
        )
    activated = jax.nn.silu(convolved).astype(BF16)
    x_values = activated[..., :local_inner]
    b_values = activated[..., local_inner : local_inner + state_width]
    c_values = activated[..., local_inner + state_width :]
    decay_log, step_bias, skip_gain = head_params[0], head_params[1], head_params[2]
    step_size = jax.nn.softplus(raw_step + step_bias)
    log_decay = -step_size * jnp.exp(decay_log)
    earlier = jnp.tril(jnp.ones((local_len, local_len), F32))
    running = jnp.einsum("ts,bsh->bth", earlier, log_decay, precision=HIGHEST_PREC)
    device_decay = running[:, -1]
    decay_t = log_decay.transpose(0, 2, 1)

    weighted = x_values.astype(F32) * wide(jnp.exp(device_decay[:, None] - running) * step_size)
    local_state = jnp.einsum(
        "btn,btc->bnc", b_values, weighted.astype(BF16), preferred_element_type=F32
    )
    unit_decay = wide(jnp.exp(device_decay))[:, None]
    decay_high = unit_decay.astype(BF16)
    decay_low = (unit_decay - decay_high.astype(F32)).astype(BF16)
    packed = jnp.concatenate(
        [
            local_state.astype(BF16),
            decay_high,
            decay_low,
            jnp.zeros((seq_count, 14, local_inner), BF16),
        ],
        axis=1,
    )
    gathered = lax.all_gather(packed, "seq")
    all_decays = gathered[:, :, state_width : state_width + 1].astype(F32) + gathered[
        :, :, state_width + 1 : state_width + 2
    ].astype(F32)
    entering = jnp.zeros_like(local_state)
    for k in range(seq_size - 1):
        state_k = gathered[k, :, :state_width].astype(F32)
        entering = jnp.where(k < seq_index, all_decays[k] * entering + state_k, entering)

    scanned_raw, states = scan_forward(
        x_values, b_values, c_values, step_size, log_decay, decay_t, entering
    )
    skip_wide = jnp.repeat(skip_gain, head_width)[None, None]
    scanned = scanned_raw + skip_wide * x_values.astype(F32)
    gate_act = jax.nn.silu(gate_input)
    gated_values = scanned * gate_act
    square_sum = jnp.sum(gated_values * gated_values, axis=-1)
    scaled = (gated_values * gate_gain).astype(BF16)
    partial_out = jnp.einsum("bti,di->btd", scaled, out_weight, preferred_element_type=F32)
    out_cotangent = cotangent.astype(F32) * is_valid[..., None]
    partial_scale_grad = jnp.sum(out_cotangent * partial_out, axis=-1)
    square_total, scale_grad = lax.psum(jnp.stack([square_sum, partial_scale_grad]), "head")
    projected = halving_sum(partial_out.astype(BF16).reshape(rows, model_width), "head")
    projected = projected.reshape(inputs.shape).astype(F32)
    out_scale = lax.rsqrt(square_total / INNER + EPS)
    block_out = (tokens + out_scale[..., None] * projected).astype(BF16)
    proj_grad = (out_scale[..., None] * out_cotangent).astype(BF16)
    square_grad = -0.5 * scale_grad * out_scale * out_scale * out_scale / INNER
    out_weight_grad = jnp.einsum("btd,bti->di", proj_grad, scaled, preferred_element_type=F32)
    scaled_grad = jnp.einsum("btd,di->bti", proj_grad, out_weight, preferred_element_type=F32)
    gate_gain_grad = jnp.sum(scaled_grad * gated_values, axis=(0, 1))
    gated_grad = scaled_grad * gate_gain + 2.0 * gated_values * square_grad[..., None]
    scanned_grad = gated_grad * gate_act
    gate_grad = (gated_grad * scanned * silu_slope(gate_input)).astype(BF16)
    local_back = jnp.einsum(
        "btn,btc->bnc",
        c_values,
        (scanned_grad * wide(jnp.exp(running))).astype(BF16),
        preferred_element_type=F32,
    )
    gathered_back = lax.all_gather(local_back.astype(BF16), "seq")
    z_weight_grad = jnp.einsum("btd,btc->dc", normed, gate_grad, preferred_element_type=F32)
    early_sums = lax.psum((out_weight_grad.astype(BF16), z_weight_grad.astype(BF16)), "seq")
    leaving = jnp.zeros_like(local_back)
    for k in range(seq_size - 1, 0, -1):
        back_k = gathered_back[k].astype(F32)
        leaving = jnp.where(k > seq_index, all_decays[k] * leaving + back_k, leaving)

    x_grad, bc_grad, decay_grad, step_grad, skip_terms = scan_backward(
        x_values,
        b_values,
        c_values,
        step_size,
        log_decay,
        decay_t,
        skip_wide,
        scanned_grad,
        scanned_raw,
        states,
        leaving,
    )
    bc_total = halving_sum(bc_grad.reshape(rows, 2 * state_width), "head")
    bc_total = bc_total.reshape(bc_grad.shape).astype(F32)

    def conv_back(activated_grad, first, last):
        convolved_grad = activated_grad * silu_slope(convolved[..., first:last])
        taps = conv_weight[:, first:last]
        tap_grads = []
        padded_grad = jnp.zeros((seq_count, local_len + CONV - 1, last - first), F32)
        for tap_index in range(CONV):
            tap_grads.append(
                jnp.sum(
                    convolved_grad * padded[:, tap_index : tap_index + local_len, first:last],
                    axis=(0, 1),
                )
            )
            padded_grad = padded_grad + jnp.pad(
                taps[tap_index] * convolved_grad,
                ((0, 0), (tap_index, CONV - 1 - tap_index), (0, 0)),
            )
        tap_grads.append(jnp.sum(convolved_grad, axis=(0, 1)))
        edge_grad = passed_along(padded_grad[:, : CONV - 1], "seq", -1)
        mixed_grad = padded_grad[:, CONV - 1 :] + jnp.pad(
            edge_grad, ((0, 0), (local_len - CONV + 1, 0), (0, 0))
        )
        return mixed_grad.astype(BF16), jnp.stack(tap_grads)

    x_in_grad, conv_inner_grad = conv_back(x_grad, 0, local_inner)
    step_total = step_grad - jnp.exp(decay_log) * decay_grad
    pre_grad = step_total * jax.nn.sigmoid(raw_step + step_bias)
    head_grad = jnp.stack(
        [
            jnp.sum(decay_grad * log_decay, axis=(0, 1)),
            jnp.sum(pre_grad, axis=(0, 1)),
            jnp.sum(skip_terms, axis=(0, 1)),
        ]
    )
    step_in_grad = pre_grad.astype(BF16)
    normed_partial = (
        jnp.einsum("btc,dc->btd", gate_grad, z_weight, preferred_element_type=F32)
        + jnp.einsum("btc,dc->btd", x_in_grad, x_weight, preferred_element_type=F32)
        + jnp.einsum("bth,dh->btd", step_in_grad, step_weight, preferred_element_type=F32)
    )
    normed_sum = halving_sum(normed_partial.astype(BF16).reshape(rows, model_width), "head")
    norm_gain_partial = lax.psum(jnp.sum(normed_partial * unit_tokens, axis=(0, 1)), "head")
    bc_in_grad, conv_bc_grad = conv_back(bc_total, local_inner, local_inner + 2 * state_width)
    bc_normed = jnp.einsum("btc,dc->btd", bc_in_grad, bc_weight, preferred_element_type=F32)
    norm_gain_grad = norm_gain_partial + jnp.sum(bc_normed * unit_tokens, axis=(0, 1))
    x_weight_grad = jnp.einsum("btd,btc->dc", normed, x_in_grad, preferred_element_type=F32)
    bc_weight_grad = jnp.einsum("btd,btc->dc", normed, bc_in_grad, preferred_element_type=F32)
    step_weight_grad = jnp.einsum("btd,bth->hd", normed, step_in_grad, preferred_element_type=F32)
    late_sums = lax.psum((x_weight_grad.astype(BF16), bc_weight_grad.astype(BF16)), "seq")
    small_grads = (
        norm_gain_grad,
        step_weight_grad,
        conv_inner_grad,
        conv_bc_grad,
        head_grad,
        gate_gain_grad,
    )
    flat = jnp.concatenate([part.reshape(-1) for part in small_grads])
    count = flat.shape[0]
    flat = jnp.pad(flat, (0, -count % 1024)).reshape(-1, 128)
    flat = lax.psum(flat, "seq").reshape(-1)
    small_sums, at = [], 0
    for part in small_grads:
        small_sums.append(flat[at : at + part.size].reshape(part.shape))
        at += part.size

    normed_grad = normed_sum.reshape(inputs.shape).astype(F32) + bc_normed
    unit_grad = normed_grad * norm_gain
    input_grad = out_cotangent + inverse_rms * (
        unit_grad - unit_tokens * jnp.mean(unit_grad * unit_tokens, axis=-1, keepdims=True)
    )
    zx_sum = jnp.stack([early_sums[1], late_sums[0]], axis=1).astype(F32)
    summed_grads = (
        small_sums[0],
        zx_sum,
        late_sums[1].astype(F32),
        small_sums[1].T,
        small_sums[2],
        small_sums[3],
        small_sums[4],
        small_sums[5],
        early_sums[0].astype(F32),
    )
    params = (
        norm_gain,
        proj_zx,
        proj_bc,
        proj_step,
        conv_inner,
        conv_bc,
        head_params,
        gate_gain,
        proj_out,
    )
    means = (
        norm_gain_mean,
        proj_zx_mean,
        proj_bc_mean,
        proj_step_mean,
        conv_inner_mean,
        conv_bc_mean,
        head_params_mean,
        gate_gain_mean,
        proj_out_mean,
    )
    squares = (
        norm_gain_square,
        proj_zx_square,
        proj_bc_square,
        proj_step_square,
        conv_inner_square,
        conv_bc_square,
        head_params_square,
        gate_gain_square,
        proj_out_square,
    )
    results = [block_out, input_grad]
    for weight, mean_old, square_old, gradient, step_rate, decay_weight in zip(
        params, means, squares, summed_grads, LEARNING_RATES, WEIGHT_DECAYS
    ):
        results.extend(adam_update(weight, mean_old, square_old, gradient, step_rate, decay_weight))
    return tuple(results)


def solution(mesh):
    in_specs = (
        P(None, "seq", None),
        P(None, "seq", None),
        P(),
        P(),
        P(),
        P(),
        P(None, None, "head"),
        P(None, None, "head"),
        P(None, None, "head"),
        P(),
        P(),
        P(),
        P(None, "head"),
        P(None, "head"),
        P(None, "head"),
        P(None, "head"),
        P(None, "head"),
        P(None, "head"),
        P(),
        P(),
        P(),
        P(None, "head"),
        P(None, "head"),
        P(None, "head"),
        P("head"),
        P("head"),
        P("head"),
        P(None, "head"),
        P(None, "head"),
        P(None, "head"),
    )
    out_specs = (
        P(None, "seq", None),
        P(None, "seq", None),
        P(),
        P(),
        P(),
        P(None, None, "head"),
        P(None, None, "head"),
        P(None, None, "head"),
        P(),
        P(),
        P(),
        P(None, "head"),
        P(None, "head"),
        P(None, "head"),
        P(None, "head"),
        P(None, "head"),
        P(None, "head"),
        P(),
        P(),
        P(),
        P(None, "head"),
        P(None, "head"),
        P(None, "head"),
        P("head"),
        P("head"),
        P("head"),
        P(None, "head"),
        P(None, "head"),
        P(None, "head"),
    )
    return jax.shard_map(shards, mesh=mesh, in_specs=in_specs, out_specs=out_specs, check_vma=False)
```

```python
import functools

import jax
import jax.numpy as jnp
from jax import lax
from jax.experimental import pallas as pl
from jax.experimental.pallas import tpu as pltpu
from jax.sharding import PartitionSpec as P

INNER = 2048
CONV = 4
CHUNK = 128
STEP = 7


EPS = 1e-05
BETA_ONE = 0.9
BETA_TWO = 0.95
ADAM_EPS = 1e-08
LEARNING_RATES = (0.6, 0.09, 0.09, 0.09, 0.9, 0.9, 0.9, 0.6, 0.06)
WEIGHT_DECAYS = (0.0, 0.1, 0.1, 0.1, 0.0, 0.0, 0.0, 0.0, 0.1)
HIGHEST_PREC = lax.Precision.HIGHEST
F32 = jnp.float32
BF16 = jnp.bfloat16


def passed_along(block, axis, distance):
    devices = range(lax.axis_size(axis))
    route = [(i - distance, i) for i in devices if i - distance in devices]
    return lax.ppermute(block, axis, route)


def swapped(block, axis, mask):
    return lax.ppermute(block, axis, [(i, i ^ mask) for i in range(lax.axis_size(axis))])


def doubling_sum(part, axis):
    for k in range(lax.axis_size(axis).bit_length() - 1):
        part = part + swapped(part, axis, 1 << k)
    return part


def halving_sum(part, axis, after=None):
    index = lax.axis_index(axis)
    masks = [1 << k for k in range(lax.axis_size(axis).bit_length() - 1)]
    rest = part.shape[1:]
    for mask in masks[:-1]:
        bit = (index // mask) % 2
        halves = part.reshape((2, part.shape[0] // 2) + rest)
        sent = lax.dynamic_index_in_dim(halves, 1 - bit, 0, keepdims=False)
        kept = lax.dynamic_index_in_dim(halves, bit, 0, keepdims=False)
        got = swapped(sent, axis, mask)
        part = (kept.astype(F32) + got.astype(F32)).astype(BF16)
    got = swapped(part, axis, masks[-1])
    if after is not None:
        got, _ = lax.optimization_barrier((got, after))
    part = (part.astype(F32) + got.astype(F32)).astype(BF16)
    for mask in reversed(masks[:-1]):
        bit = (index // mask) % 2
        got = swapped(part, axis, mask)
        first = jnp.where(bit == 0, part, got)
        second = jnp.where(bit == 0, got, part)
        part = jnp.concatenate([first, second], axis=0)
    return part


def exchanged(blocks, axis):
    return lax.all_to_all(blocks, axis, 0, 0, tiled=True)


def to_blocks(state, count):
    return state.astype(BF16).reshape(count, -1, state.shape[-1])


def states_before(state, decay, axis):
    size = lax.axis_size(axis)
    blocks = to_blocks(state, size)
    height = blocks.shape[1]
    high = decay.astype(BF16)
    low = (decay - high.astype(F32)).astype(BF16)
    empty = jnp.zeros((decay.shape[0], 14, decay.shape[2]), BF16)
    extra = jnp.concatenate([high, low, empty], axis=1)
    extra = jnp.repeat(extra, size // decay.shape[0], axis=0)
    got = exchanged(jnp.concatenate([blocks, extra], axis=1), axis).astype(F32)
    decays = got[:, height : height + 1] + got[:, height + 1 : height + 2]
    entering = [jnp.zeros(got[0, :height].shape, F32)]
    for k in range(size - 1):
        entering.append(decays[k] * entering[-1] + got[k, :height])
    back = exchanged(jnp.stack(entering).astype(BF16), axis)
    return back.reshape(state.shape).astype(F32), decays


def states_after(state, decays, axis):
    size = lax.axis_size(axis)
    got = exchanged(to_blocks(state, size), axis).astype(F32)
    leaving = [jnp.zeros(got[0].shape, F32)]
    for k in range(size - 1, 0, -1):
        leaving.append(decays[k] * leaving[-1] + got[k])
    back = exchanged(jnp.stack(leaving[::-1]).astype(BF16), axis)
    return back.reshape(state.shape).astype(F32)


def lane_tiles(a):
    rows, two, columns = a.shape
    return a.reshape(rows, two, columns // 128, 128).transpose(0, 2, 1, 3).reshape(-1, 128)


def from_lane_tiles(a, shape):
    rows, two, columns = shape
    return a.reshape(rows, columns // 128, two, 128).transpose(0, 2, 1, 3).reshape(shape)


def dot(a, b, dims=((1,), (0,)), precision=None):
    return lax.dot_general(a, b, (dims, ((), ())), precision=precision, preferred_element_type=F32)


def expander(heads, width):
    row = lax.broadcasted_iota(jnp.int32, (heads, heads * width), 0)
    column = lax.broadcasted_iota(jnp.int32, (heads, heads * width), 1)
    inside = (column >= row * width) & (column < (row + 1) * width)
    return jnp.where(inside, 1.0, 0.0).astype(BF16)


def split_dot(a, b, dims):
    high = a.astype(BF16)
    low = (a - high.astype(F32)).astype(BF16)
    return dot(high, b, dims) + dot(low, b, dims)


def spread(a, expand):
    return split_dot(a, expand, ((1,), (0,)))


def head_sums(a, expand):
    return split_dot(a, expand, ((1,), (1,)))


def pair_rows(a):
    lane = lax.broadcasted_iota(jnp.int32, a.shape, 1)
    first = lane < a.shape[1] // 2
    zero = jnp.zeros_like(a)
    return jnp.concatenate([jnp.where(first, a, zero), jnp.where(first, zero, a)], axis=0)


def chunk_decays(decay, decay_t):
    q = decay.shape[0]
    row = lax.broadcasted_iota(jnp.int32, (q, q), 0)
    column = lax.broadcasted_iota(jnp.int32, (q, q), 1)
    lower = jnp.where(row >= column, 1.0, 0.0).astype(F32)
    cum = dot(lower, decay, precision=HIGHEST_PREC)
    cum_t = dot(decay_t, lower, ((1,), (1,)), precision=HIGHEST_PREC)
    return cum, cum_t, row, column


def scan_kernel(x_ref, b_ref, c_ref, step_ref, decay_ref, decay_t_ref, enter_ref, y_ref, in_ref, state):
    heads = step_ref.shape[2]
    width = x_ref.shape[2] // heads

    @pl.when(pl.program_id(1) == 0)
    def _():
        state[...] = enter_ref[0]

    expand = expander(heads, width)
    cum, cum_t, row, column = chunk_decays(decay_ref[0], decay_t_ref[0])
    causal = row >= column
    q = cum.shape[0]
    total = cum[q - 1 : q, :]
    b, c = b_ref[0], c_ref[0]
    x = x_ref[0].astype(F32)
    step = step_ref[0]
    xs = (x * spread(step, expand)).astype(BF16)
    grown = spread(jnp.exp(cum), expand)
    xw = (x * spread(step * jnp.exp(total - cum), expand)).astype(BF16)
    scores = dot(c, b, ((1,), (1,)))
    before = state[...]
    in_ref[0, 0] = before
    from_state = grown * dot(c, before.astype(BF16))
    for pair in range(heads // 2):
        lanes = slice(pair * 2 * width, (pair + 1) * 2 * width)
        mixing = []
        for h in (2 * pair, 2 * pair + 1):
            between = cum[:, h : h + 1] - cum_t[h : h + 1, :]
            mixing.append((jnp.exp(jnp.where(causal, between, -1e30)) * scores).astype(BF16))
        within = dot(jnp.concatenate(mixing, axis=1), pair_rows(xs[:, lanes]))
        y_ref[0, :, lanes] = within + from_state[:, lanes]
    state[...] = grown[q - 1 : q, :] * before + dot(b, xw, ((0,), (0,)))


def back_kernel(
    x_ref, b_ref, c_ref, step_ref, decay_ref, decay_t_ref, skip_ref, dy_ref, y_ref, in_ref, leave_ref,
    dx_ref, dbc_ref, ldg_ref, dstep_ref, dskip_ref, grad
):
    heads = step_ref.shape[2]
    width = x_ref.shape[2] // heads

    @pl.when(pl.program_id(1) == 0)
    def _():
        grad[...] = leave_ref[0]

    expand = expander(heads, width)
    cum, cum_t, row, column = chunk_decays(decay_ref[0], decay_t_ref[0])
    later = column >= row
    q = cum.shape[0]
    total = cum[q - 1 : q, :]
    b, c = b_ref[0], c_ref[0]
    x = x_ref[0].astype(F32)
    step = step_ref[0]
    step_wide = spread(step, expand)
    xs = (x * step_wide).astype(BF16)
    grown = spread(jnp.exp(cum), expand)
    waned = spread(jnp.exp(total - cum), expand)
    xw = (x * step_wide * waned).astype(BF16)
    dy = dy_ref[0]
    dy_low = dy.astype(BF16)
    edy = (dy * grown).astype(BF16)
    before = in_ref[0, 0]
    after_grad = grad[...]
    after_low = after_grad.astype(BF16)
    scores_t = dot(b, c, ((1,), (1,)))
    v_state = waned * dot(b, after_low)
    dscores_t = jnp.zeros((q, q), F32)
    v_parts = []
    for pair in range(heads // 2):
        lanes = slice(pair * 2 * width, (pair + 1) * 2 * width)
        dy_pair = pair_rows(dy_low[:, lanes])
        xs_pair = pair_rows(xs[:, lanes])
        dmix = dot(xs_pair, dy_low[:, lanes], ((1,), (1,)))
        mixing = []
        for k, h in enumerate((2 * pair, 2 * pair + 1)):
            between = cum_t[h : h + 1, :] - cum[:, h : h + 1]
            fade = jnp.exp(jnp.where(later, between, -1e30))
            mixing.append((fade * scores_t).astype(BF16))
            dscores_t = dscores_t + fade * dmix[k * q : (k + 1) * q]
        v_parts.append(dot(jnp.concatenate(mixing, axis=1), dy_pair))
    v = jnp.concatenate(v_parts, axis=1) + v_state
    xs_wide = xs.astype(F32)
    etotal = grown[q - 1 : q, :]
    dx_ref[0] = step_wide * v + skip_ref[0] * dy
    end_row = jnp.sum(xs_wide * v_state, axis=0, keepdims=True) + jnp.sum(
        etotal * before * after_grad, axis=0, keepdims=True
    )
    crossing = dy_low.astype(F32) * y_ref[0] - xs_wide * v
    last = lax.broadcasted_iota(jnp.int32, crossing.shape, 0) == q - 1
    crossing = crossing + jnp.where(last, end_row, 0.0)
    upper = jnp.where(column >= row, 1.0, 0.0).astype(F32)
    ldg_ref[0] = dot(upper, head_sums(crossing, expand), precision=HIGHEST_PREC)
    dstep_ref[0] = head_sums(x * v, expand)
    dskip_ref[0] = head_sums(x * dy, expand)
    dscores_low = dscores_t.astype(BF16)
    state = b.shape[1]
    dbc_ref[0, :, :state] = (
        dot(dscores_low, c) + dot(xw, after_low, ((1,), (1,)))
    ).astype(BF16)
    dbc_ref[0, :, state:] = (
        dot(dscores_low, b, ((0,), (0,))) + dot(edy, before.astype(BF16), ((1,), (1,)))
    ).astype(BF16)
    grad[...] = etotal * after_grad + dot(c, edy, ((0,), (0,)))


def scan_forward(x, b, c, step, decay, decay_t, enter):
    seqs, length, inner = x.shape
    state, heads = b.shape[2], step.shape[2]
    chunks = length // CHUNK

    def block(lanes):
        return pl.BlockSpec((1, CHUNK, lanes), lambda s, k: (s, k, 0))

    return pl.pallas_call(
        scan_kernel,
        grid=(seqs, chunks),
        in_specs=[
            block(inner),
            block(state),
            block(state),
            block(heads),
            block(heads),
            pl.BlockSpec((1, heads, CHUNK), lambda s, k: (s, 0, k)),
            pl.BlockSpec((1, state, inner), lambda s, k: (s, 0, 0)),
        ],
        out_specs=[
            block(inner),
            pl.BlockSpec((1, 1, state, inner), lambda s, k: (s, k, 0, 0)),
        ],
        out_shape=[
            jax.ShapeDtypeStruct((seqs, length, inner), F32),
            jax.ShapeDtypeStruct((seqs, chunks, state, inner), F32),
        ],
        scratch_shapes=[pltpu.VMEM((state, inner), F32)],
        compiler_params=pltpu.CompilerParams(vmem_limit_bytes=40 << 20),
    )(x, b, c, step, decay, decay_t, enter)


def scan_backward(x, b, c, step, decay, decay_t, skip, dy, y, states, leave):
    seqs, length, inner = x.shape
    state, heads = b.shape[2], step.shape[2]
    chunks = length // CHUNK

    def block(lanes):
        return pl.BlockSpec((1, CHUNK, lanes), lambda s, k: (s, chunks - 1 - k, 0))

    return pl.pallas_call(
        back_kernel,
        grid=(seqs, chunks),
        in_specs=[
            block(inner),
            block(state),
            block(state),
            block(heads),
            block(heads),
            pl.BlockSpec((1, heads, CHUNK), lambda s, k: (s, 0, chunks - 1 - k)),
            pl.BlockSpec((1, 1, inner), lambda s, k: (0, 0, 0)),
            block(inner),
            block(inner),
            pl.BlockSpec((1, 1, state, inner), lambda s, k: (s, chunks - 1 - k, 0, 0)),
            pl.BlockSpec((1, state, inner), lambda s, k: (s, 0, 0)),
        ],
        out_specs=[block(inner), block(2 * state), block(heads), block(heads), block(heads)],
        out_shape=[
            jax.ShapeDtypeStruct((seqs, length, inner), F32),
            jax.ShapeDtypeStruct((seqs, length, 2 * state), BF16),
            jax.ShapeDtypeStruct((seqs, length, heads), F32),
            jax.ShapeDtypeStruct((seqs, length, heads), F32),
            jax.ShapeDtypeStruct((seqs, length, heads), F32),
        ],
        scratch_shapes=[pltpu.VMEM((state, inner), F32)],
        compiler_params=pltpu.CompilerParams(vmem_limit_bytes=40 << 20),
    )(x, b, c, step, decay, decay_t, skip, dy, y, states, leave)


def silu_slope(values):
    sigmoid_part = jax.nn.sigmoid(values)
    return sigmoid_part * (1.0 + values * (1.0 - sigmoid_part))


def adam_update(weight, mean_old, square_old, gradient, step_rate, decay_weight):
    mean_new = BETA_ONE * mean_old + (1.0 - BETA_ONE) * gradient
    square_new = BETA_TWO * square_old + (1.0 - BETA_TWO) * gradient * gradient
    corrected_mean = mean_new / (1.0 - BETA_ONE**STEP)
    corrected_square = square_new / (1.0 - BETA_TWO**STEP)
    weight_new = weight - step_rate * (
        corrected_mean / (jnp.sqrt(corrected_square) + ADAM_EPS) + decay_weight * weight
    )
    return (mean_new, square_new, weight_new)


def shards(
    inputs,
    cotangent,
    lengths,
    norm_gain,
    norm_gain_mean,
    norm_gain_square,
    proj_zx,
    proj_zx_mean,
    proj_zx_square,
    proj_bc,
    proj_bc_mean,
    proj_bc_square,
    proj_step,
    proj_step_mean,
    proj_step_square,
    conv_inner,
    conv_inner_mean,
    conv_inner_square,
    conv_bc,
    conv_bc_mean,
    conv_bc_square,
    head_params,
    head_params_mean,
    head_params_square,
    gate_gain,
    gate_gain_mean,
    gate_gain_square,
    proj_out,
    proj_out_mean,
    proj_out_square,
):
    seq_count, local_len, model_width = inputs.shape
    local_inner = proj_zx.shape[2]
    state_width = proj_bc.shape[1] // 2
    local_heads = proj_step.shape[1]
    head_width = local_inner // local_heads
    rows = seq_count * local_len
    seq_size, seq_index = lax.axis_size("seq"), lax.axis_index("seq")

    def wide(a):
        selector = jnp.repeat(jnp.eye(local_heads, dtype=F32), head_width, axis=1)
        return jnp.einsum("...h,hc->...c", a, selector, precision=HIGHEST_PREC)

    positions = seq_index * local_len + jnp.arange(local_len)
    is_valid = (positions[None, :] < lengths[:, None]).astype(F32)
    tokens = inputs.astype(F32)
    inverse_rms = lax.rsqrt(jnp.mean(tokens * tokens, axis=-1, keepdims=True) + EPS)
    unit_tokens = tokens * inverse_rms
    normed = (unit_tokens * norm_gain).astype(BF16)
    z_weight = proj_zx[:, 0].astype(BF16)
    x_weight = proj_zx[:, 1].astype(BF16)
    bc_weight = proj_bc.astype(BF16)
    step_weight = proj_step.astype(BF16)
    out_weight = proj_out.astype(BF16)
    xbc_weight = jnp.concatenate([x_weight, bc_weight], axis=1)
    mixed_in = jnp.einsum("btd,dc->btc", normed, xbc_weight, preferred_element_type=F32).astype(BF16)
    edge_in = passed_along(mixed_in[:, local_len - CONV + 1 :], "seq", 1)
    raw_step = jnp.einsum("btd,dh->bth", normed, step_weight, preferred_element_type=F32)
    gate_input = jnp.einsum("btd,dc->btc", normed, z_weight, preferred_element_type=F32)
    padded = jnp.concatenate([edge_in, mixed_in], axis=1)
    conv_weight = jnp.concatenate([conv_inner, conv_bc], axis=-1)
    convolved = conv_weight[CONV] + jnp.zeros(mixed_in.shape, F32)
    for tap_index in range(CONV):
        convolved = (
            convolved + conv_weight[tap_index] * padded[:, tap_index : tap_index + local_len]
        )
    activated = jax.nn.silu(convolved).astype(BF16)
    x_values = activated[..., :local_inner]
    b_values = activated[..., local_inner : local_inner + state_width]
    c_values = activated[..., local_inner + state_width :]
    decay_log, step_bias, skip_gain = head_params[0], head_params[1], head_params[2]
    step_size = jax.nn.softplus(raw_step + step_bias)
    log_decay = -step_size * jnp.exp(decay_log)
    earlier = jnp.tril(jnp.ones((local_len, local_len), F32))
    running = jnp.einsum("ts,bsh->bth", earlier, log_decay, precision=HIGHEST_PREC)
    device_decay = running[:, -1]
    decay_t = log_decay.transpose(0, 2, 1)

    weighted = x_values.astype(F32) * wide(jnp.exp(device_decay[:, None] - running) * step_size)
    local_state = jnp.einsum(
        "btn,btc->bnc", b_values, weighted.astype(BF16), preferred_element_type=F32
    )
    unit_decay = wide(jnp.exp(device_decay))[:, None]
    entering, block_decays = states_before(local_state, unit_decay, "seq")

    scanned_raw, states = scan_forward(
        x_values, b_values, c_values, step_size, log_decay, decay_t, entering
    )
    skip_wide = jnp.repeat(skip_gain, head_width)[None, None]
    scanned = scanned_raw + skip_wide * x_values.astype(F32)
    gate_act = jax.nn.silu(gate_input)
    gated_values = scanned * gate_act
    square_sum = jnp.sum(gated_values * gated_values, axis=-1)
    scaled = (gated_values * gate_gain).astype(BF16)
    partial_out = jnp.einsum("bti,di->btd", scaled, out_weight, preferred_element_type=F32)
    out_cotangent = cotangent.astype(F32) * is_valid[..., None]
    partial_scale_grad = jnp.sum(out_cotangent * partial_out, axis=-1)
    square_total, scale_grad = lax.psum(jnp.stack([square_sum, partial_scale_grad]), "head")
    out_scale = lax.rsqrt(square_total / INNER + EPS)
    proj_grad = (out_scale[..., None] * out_cotangent).astype(BF16)
    square_grad = -0.5 * scale_grad * out_scale * out_scale * out_scale / INNER
    out_weight_grad = jnp.einsum("btd,bti->di", proj_grad, scaled, preferred_element_type=F32)
    scaled_grad = jnp.einsum("btd,di->bti", proj_grad, out_weight, preferred_element_type=F32)
    gate_gain_grad = jnp.sum(scaled_grad * gated_values, axis=(0, 1))
    gated_grad = scaled_grad * gate_gain + 2.0 * gated_values * square_grad[..., None]
    scanned_grad = gated_grad * gate_act
    gate_grad = (gated_grad * scanned * silu_slope(gate_input)).astype(BF16)
    local_back = jnp.einsum(
        "btn,btc->bnc",
        c_values,
        (scanned_grad * wide(jnp.exp(running))).astype(BF16),
        preferred_element_type=F32,
    )
    leaving = states_after(local_back, block_decays, "seq")
    z_weight_grad = jnp.einsum("btd,btc->dc", normed, gate_grad, preferred_element_type=F32)
    early_grads = (out_weight_grad.astype(BF16), z_weight_grad.astype(BF16))
    early_grads, _ = lax.optimization_barrier((early_grads, leaving))
    early_sums = lax.psum(early_grads, "seq")
    x_grad, bc_grad, decay_grad, step_grad, skip_terms = scan_backward(
        x_values,
        b_values,
        c_values,
        step_size,
        log_decay,
        decay_t,
        skip_wide,
        scanned_grad,
        scanned_raw,
        states,
        leaving,
    )
    projected = halving_sum(
        partial_out.astype(BF16).reshape(rows, model_width), "head", after=bc_grad
    )
    projected = projected.reshape(inputs.shape).astype(F32)
    block_out = (tokens + out_scale[..., None] * projected).astype(BF16)
    bc_total = halving_sum(bc_grad.reshape(rows, 2 * state_width), "head")
    bc_total = bc_total.reshape(bc_grad.shape).astype(F32)

    def conv_back(activated_grad, first, last):
        convolved_grad = activated_grad * silu_slope(convolved[..., first:last])
        taps = conv_weight[:, first:last]
        tap_grads = []
        padded_grad = jnp.zeros((seq_count, local_len + CONV - 1, last - first), F32)
        for tap_index in range(CONV):
            tap_grads.append(
                jnp.sum(
                    convolved_grad * padded[:, tap_index : tap_index + local_len, first:last],
                    axis=(0, 1),
                )
            )
            padded_grad = padded_grad + jnp.pad(
                taps[tap_index] * convolved_grad,
                ((0, 0), (tap_index, CONV - 1 - tap_index), (0, 0)),
            )
        tap_grads.append(jnp.sum(convolved_grad, axis=(0, 1)))
        edge_grad = passed_along(padded_grad[:, : CONV - 1], "seq", -1)
        mixed_grad = padded_grad[:, CONV - 1 :] + jnp.pad(
            edge_grad, ((0, 0), (local_len - CONV + 1, 0), (0, 0))
        )
        return mixed_grad.astype(BF16), jnp.stack(tap_grads)

    x_in_grad, conv_inner_grad = conv_back(x_grad, 0, local_inner)
    step_total = step_grad - jnp.exp(decay_log) * decay_grad
    pre_grad = step_total * jax.nn.sigmoid(raw_step + step_bias)
    head_grad = jnp.stack(
        [
            jnp.sum(decay_grad * log_decay, axis=(0, 1)),
            jnp.sum(pre_grad, axis=(0, 1)),
            jnp.sum(skip_terms, axis=(0, 1)),
        ]
    )
    step_in_grad = pre_grad.astype(BF16)
    normed_partial = (
        jnp.einsum("btc,dc->btd", gate_grad, z_weight, preferred_element_type=F32)
        + jnp.einsum("btc,dc->btd", x_in_grad, x_weight, preferred_element_type=F32)
        + jnp.einsum("bth,dh->btd", step_in_grad, step_weight, preferred_element_type=F32)
    )
    normed_sum = halving_sum(normed_partial.astype(BF16).reshape(rows, model_width), "head")
    norm_gain_partial = doubling_sum(jnp.sum(normed_partial * unit_tokens, axis=(0, 1)), "head")
    bc_in_grad, conv_bc_grad = conv_back(bc_total, local_inner, local_inner + 2 * state_width)
    bc_normed = jnp.einsum("btc,dc->btd", bc_in_grad, bc_weight, preferred_element_type=F32)
    norm_gain_grad = norm_gain_partial + jnp.sum(bc_normed * unit_tokens, axis=(0, 1))
    x_weight_grad = jnp.einsum("btd,btc->dc", normed, x_in_grad, preferred_element_type=F32)
    bc_weight_grad = jnp.einsum("btd,btc->dc", normed, bc_in_grad, preferred_element_type=F32)
    step_weight_grad = jnp.einsum("btd,bth->hd", normed, step_in_grad, preferred_element_type=F32)
    late_grads = (x_weight_grad.astype(BF16), bc_weight_grad.astype(BF16))
    late_grads, early_sums = lax.optimization_barrier((late_grads, early_sums))
    late_sums = lax.psum(late_grads, "seq")
    small_grads = (
        norm_gain_grad,
        step_weight_grad,
        conv_inner_grad,
        conv_bc_grad,
        head_grad,
        gate_gain_grad,
    )
    flat = jnp.concatenate([part.reshape(-1) for part in small_grads])
    count = flat.shape[0]
    flat = jnp.pad(flat, (0, -count % 1024)).reshape(-1, 128)
    flat = doubling_sum(flat, "seq").reshape(-1)
    small_sums, at = [], 0
    for part in small_grads:
        small_sums.append(flat[at : at + part.size].reshape(part.shape))
        at += part.size

    normed_grad = normed_sum.reshape(inputs.shape).astype(F32) + bc_normed
    unit_grad = normed_grad * norm_gain
    input_grad = out_cotangent + inverse_rms * (
        unit_grad - unit_tokens * jnp.mean(unit_grad * unit_tokens, axis=-1, keepdims=True)
    )
    zx_sum = lane_tiles(jnp.stack([early_sums[1], late_sums[0]], axis=1)).astype(F32)
    summed_grads = (
        small_sums[0],
        zx_sum,
        late_sums[1].astype(F32),
        small_sums[1].T,
        small_sums[2],
        small_sums[3],
        small_sums[4],
        small_sums[5],
        early_sums[0].astype(F32),
    )
    params = (
        norm_gain,
        proj_zx,
        proj_bc,
        proj_step,
        conv_inner,
        conv_bc,
        head_params,
        gate_gain,
        proj_out,
    )
    means = (
        norm_gain_mean,
        proj_zx_mean,
        proj_bc_mean,
        proj_step_mean,
        conv_inner_mean,
        conv_bc_mean,
        head_params_mean,
        gate_gain_mean,
        proj_out_mean,
    )
    squares = (
        norm_gain_square,
        proj_zx_square,
        proj_bc_square,
        proj_step_square,
        conv_inner_square,
        conv_bc_square,
        head_params_square,
        gate_gain_square,
        proj_out_square,
    )
    results = [block_out, input_grad]
    for weight, mean_old, square_old, gradient, step_rate, decay_weight in zip(
        params, means, squares, summed_grads, LEARNING_RATES, WEIGHT_DECAYS
    ):
        shape = weight.shape
        if len(shape) == 3:
            weight, mean_old, square_old = map(lane_tiles, (weight, mean_old, square_old))
        updated = adam_update(weight, mean_old, square_old, gradient, step_rate, decay_weight)
        if len(shape) == 3:
            updated = [from_lane_tiles(part, shape) for part in updated]
        results.extend(updated)
    return tuple(results)


def solution(mesh):
    in_specs = (
        P(None, "seq", None),
        P(None, "seq", None),
        P(),
        P(),
        P(),
        P(),
        P(None, None, "head"),
        P(None, None, "head"),
        P(None, None, "head"),
        P(),
        P(),
        P(),
        P(None, "head"),
        P(None, "head"),
        P(None, "head"),
        P(None, "head"),
        P(None, "head"),
        P(None, "head"),
        P(),
        P(),
        P(),
        P(None, "head"),
        P(None, "head"),
        P(None, "head"),
        P("head"),
        P("head"),
        P("head"),
        P(None, "head"),
        P(None, "head"),
        P(None, "head"),
    )
    out_specs = (
        P(None, "seq", None),
        P(None, "seq", None),
        P(),
        P(),
        P(),
        P(None, None, "head"),
        P(None, None, "head"),
        P(None, None, "head"),
        P(),
        P(),
        P(),
        P(None, "head"),
        P(None, "head"),
        P(None, "head"),
        P(None, "head"),
        P(None, "head"),
        P(None, "head"),
        P(),
        P(),
        P(),
        P(None, "head"),
        P(None, "head"),
        P(None, "head"),
        P("head"),
        P("head"),
        P("head"),
        P(None, "head"),
        P(None, "head"),
        P(None, "head"),
    )
    return jax.shard_map(shards, mesh=mesh, in_specs=in_specs, out_specs=out_specs, check_vma=False)
```

```python
import functools

import jax
import jax.numpy as jnp
from jax import lax
from jax.experimental import pallas as pl
from jax.experimental.pallas import tpu as pltpu
from jax.sharding import PartitionSpec as P

INNER = 2048
CONV = 4
CHUNK = 128
STEP = 7


EPS = 1e-05
BETA_ONE = 0.9
BETA_TWO = 0.95
ADAM_EPS = 1e-08
LEARNING_RATES = (0.6, 0.09, 0.09, 0.09, 0.9, 0.9, 0.9, 0.6, 0.06)
WEIGHT_DECAYS = (0.0, 0.1, 0.1, 0.1, 0.0, 0.0, 0.0, 0.0, 0.1)
HIGHEST_PREC = lax.Precision.HIGHEST
F32 = jnp.float32
BF16 = jnp.bfloat16


def passed_along(block, axis, distance):
    devices = range(lax.axis_size(axis))
    route = [(i - distance, i) for i in devices if i - distance in devices]
    return lax.ppermute(block, axis, route)


def swapped(block, axis, mask):
    return lax.ppermute(block, axis, [(i, i ^ mask) for i in range(lax.axis_size(axis))])


def doubling_sum(part, axis):
    for k in range(lax.axis_size(axis).bit_length() - 1):
        part = part + swapped(part, axis, 1 << k)
    return part


def axis_masks(axis):
    return [1 << k for k in range(lax.axis_size(axis).bit_length() - 1)]


def near_bit(axis, mask):
    return (lax.axis_index(axis) // mask) % 2


def added(a, b):
    return (a.astype(F32) + b.astype(F32)).astype(BF16)


def halved(part, axis):
    for mask in axis_masks(axis)[:-1]:
        bit = near_bit(axis, mask)
        halves = part.reshape((2, part.shape[0] // 2) + part.shape[1:])
        sent = lax.dynamic_index_in_dim(halves, 1 - bit, 0, keepdims=False)
        kept = lax.dynamic_index_in_dim(halves, bit, 0, keepdims=False)
        part = added(kept, swapped(sent, axis, mask))
    return part


def joined(part, got, bit):
    first = jnp.where(bit == 0, part, got)
    second = jnp.where(bit == 0, got, part)
    return jnp.concatenate([first, second], axis=0)


def regathered(part, axis):
    masks = axis_masks(axis)[:-1]
    for mask in reversed(masks[1:]):
        part = joined(part, swapped(part, axis, mask), near_bit(axis, mask))
    return part, swapped(part, axis, masks[0])


def halving_sum(part, axis):
    part = halved(part, axis)
    part = added(part, swapped(part, axis, axis_masks(axis)[-1]))
    part, other = regathered(part, axis)
    return joined(part, other, near_bit(axis, 1))


def exchanged(blocks, axis):
    return lax.all_to_all(blocks, axis, 0, 0, tiled=True)


def to_blocks(state, count):
    return state.astype(BF16).reshape(count, -1, state.shape[-1])


def states_before(state, decay, axis):
    size = lax.axis_size(axis)
    blocks = to_blocks(state, size)
    height = blocks.shape[1]
    high = decay.astype(BF16)
    low = (decay - high.astype(F32)).astype(BF16)
    empty = jnp.zeros((decay.shape[0], 14, decay.shape[2]), BF16)
    extra = jnp.concatenate([high, low, empty], axis=1)
    extra = jnp.repeat(extra, size // decay.shape[0], axis=0)
    got = exchanged(jnp.concatenate([blocks, extra], axis=1), axis).astype(F32)
    decays = got[:, height : height + 1] + got[:, height + 1 : height + 2]
    entering = [jnp.zeros(got[0, :height].shape, F32)]
    for k in range(size - 1):
        entering.append(decays[k] * entering[-1] + got[k, :height])
    back = exchanged(jnp.stack(entering).astype(BF16), axis)
    return back.reshape(state.shape).astype(F32), decays


def states_after(state, decays, axis):
    size = lax.axis_size(axis)
    got = exchanged(to_blocks(state, size), axis).astype(F32)
    leaving = [jnp.zeros(got[0].shape, F32)]
    for k in range(size - 1, 0, -1):
        leaving.append(decays[k] * leaving[-1] + got[k])
    back = exchanged(jnp.stack(leaving[::-1]).astype(BF16), axis)
    return back.reshape(state.shape).astype(F32)


def lane_tiles(a):
    rows, two, columns = a.shape
    return a.reshape(rows, two, columns // 128, 128).transpose(0, 2, 1, 3).reshape(rows, -1, 128)


def from_lane_tiles(a, shape):
    rows, two, columns = shape
    return a.reshape(rows, columns // 128, two, 128).transpose(0, 2, 1, 3).reshape(shape)


def dot(a, b, dims=((1,), (0,)), precision=None):
    return lax.dot_general(a, b, (dims, ((), ())), precision=precision, preferred_element_type=F32)


def expander(heads, width):
    row = lax.broadcasted_iota(jnp.int32, (heads, heads * width), 0)
    column = lax.broadcasted_iota(jnp.int32, (heads, heads * width), 1)
    inside = (column >= row * width) & (column < (row + 1) * width)
    return jnp.where(inside, 1.0, 0.0).astype(BF16)


def split_dot(a, b, dims):
    high = a.astype(BF16)
    low = (a - high.astype(F32)).astype(BF16)
    return dot(high, b, dims) + dot(low, b, dims)


def spread(a, expand):
    return split_dot(a, expand, ((1,), (0,)))


def head_sums(a, expand):
    return split_dot(a, expand, ((1,), (1,)))


def pair_rows(a):
    lane = lax.broadcasted_iota(jnp.int32, a.shape, 1)
    first = lane < a.shape[1] // 2
    zero = jnp.zeros_like(a)
    return jnp.concatenate([jnp.where(first, a, zero), jnp.where(first, zero, a)], axis=0)


def chunk_decays(decay, decay_t):
    q = decay.shape[0]
    row = lax.broadcasted_iota(jnp.int32, (q, q), 0)
    column = lax.broadcasted_iota(jnp.int32, (q, q), 1)
    lower = jnp.where(row >= column, 1.0, 0.0).astype(F32)
    cum = dot(lower, decay, precision=HIGHEST_PREC)
    cum_t = dot(decay_t, lower, ((1,), (1,)), precision=HIGHEST_PREC)
    return cum, cum_t, row, column


def scan_kernel(x_ref, b_ref, c_ref, step_ref, decay_ref, decay_t_ref, enter_ref, y_ref, in_ref, state):
    heads = step_ref.shape[2]
    width = x_ref.shape[2] // heads

    @pl.when(pl.program_id(1) == 0)
    def _():
        state[...] = enter_ref[0]

    expand = expander(heads, width)
    cum, cum_t, row, column = chunk_decays(decay_ref[0], decay_t_ref[0])
    causal = row >= column
    q = cum.shape[0]
    total = cum[q - 1 : q, :]
    b, c = b_ref[0], c_ref[0]
    x = x_ref[0].astype(F32)
    step = step_ref[0]
    xs = (x * spread(step, expand)).astype(BF16)
    grown = spread(jnp.exp(cum), expand)
    xw = (x * spread(step * jnp.exp(total - cum), expand)).astype(BF16)
    scores = dot(c, b, ((1,), (1,)))
    before = state[...]
    in_ref[0, 0] = before
    from_state = grown * dot(c, before.astype(BF16))
    for pair in range(heads // 2):
        lanes = slice(pair * 2 * width, (pair + 1) * 2 * width)
        mixing = []
        for h in (2 * pair, 2 * pair + 1):
            between = cum[:, h : h + 1] - cum_t[h : h + 1, :]
            mixing.append((jnp.exp(jnp.where(causal, between, -1e30)) * scores).astype(BF16))
        within = dot(jnp.concatenate(mixing, axis=1), pair_rows(xs[:, lanes]))
        y_ref[0, :, lanes] = within + from_state[:, lanes]
    state[...] = grown[q - 1 : q, :] * before + dot(b, xw, ((0,), (0,)))


def back_kernel(
    x_ref, b_ref, c_ref, step_ref, decay_ref, decay_t_ref, skip_ref, dy_ref, y_ref, in_ref, leave_ref,
    dx_ref, dbc_ref, ldg_ref, dstep_ref, dskip_ref, grad
):
    heads = step_ref.shape[2]
    width = x_ref.shape[2] // heads

    @pl.when(pl.program_id(1) == 0)
    def _():
        grad[...] = leave_ref[0]

    expand = expander(heads, width)
    cum, cum_t, row, column = chunk_decays(decay_ref[0], decay_t_ref[0])
    later = column >= row
    q = cum.shape[0]
    total = cum[q - 1 : q, :]
    b, c = b_ref[0], c_ref[0]
    x = x_ref[0].astype(F32)
    step = step_ref[0]
    step_wide = spread(step, expand)
    xs = (x * step_wide).astype(BF16)
    grown = spread(jnp.exp(cum), expand)
    waned = spread(jnp.exp(total - cum), expand)
    xw = (x * step_wide * waned).astype(BF16)
    dy = dy_ref[0]
    dy_low = dy.astype(BF16)
    edy = (dy * grown).astype(BF16)
    before = in_ref[0, 0]
    after_grad = grad[...]
    after_low = after_grad.astype(BF16)
    scores_t = dot(b, c, ((1,), (1,)))
    v_state = waned * dot(b, after_low)
    dscores_t = jnp.zeros((q, q), F32)
    v_parts = []
    for pair in range(heads // 2):
        lanes = slice(pair * 2 * width, (pair + 1) * 2 * width)
        dy_pair = pair_rows(dy_low[:, lanes])
        xs_pair = pair_rows(xs[:, lanes])
        dmix = dot(xs_pair, dy_low[:, lanes], ((1,), (1,)))
        mixing = []
        for k, h in enumerate((2 * pair, 2 * pair + 1)):
            between = cum_t[h : h + 1, :] - cum[:, h : h + 1]
            fade = jnp.exp(jnp.where(later, between, -1e30))
            mixing.append((fade * scores_t).astype(BF16))
            dscores_t = dscores_t + fade * dmix[k * q : (k + 1) * q]
        v_parts.append(dot(jnp.concatenate(mixing, axis=1), dy_pair))
    v = jnp.concatenate(v_parts, axis=1) + v_state
    xs_wide = xs.astype(F32)
    etotal = grown[q - 1 : q, :]
    dx_ref[0] = step_wide * v + skip_ref[0] * dy
    end_row = jnp.sum(xs_wide * v_state, axis=0, keepdims=True) + jnp.sum(
        etotal * before * after_grad, axis=0, keepdims=True
    )
    crossing = dy_low.astype(F32) * y_ref[0] - xs_wide * v
    last = lax.broadcasted_iota(jnp.int32, crossing.shape, 0) == q - 1
    crossing = crossing + jnp.where(last, end_row, 0.0)
    upper = jnp.where(column >= row, 1.0, 0.0).astype(F32)
    ldg_ref[0] = dot(upper, head_sums(crossing, expand), precision=HIGHEST_PREC)
    dstep_ref[0] = head_sums(x * v, expand)
    dskip_ref[0] = head_sums(x * dy, expand)
    dscores_low = dscores_t.astype(BF16)
    state = b.shape[1]
    dbc_ref[0, :, :state] = (
        dot(dscores_low, c) + dot(xw, after_low, ((1,), (1,)))
    ).astype(BF16)
    dbc_ref[0, :, state:] = (
        dot(dscores_low, b, ((0,), (0,))) + dot(edy, before.astype(BF16), ((1,), (1,)))
    ).astype(BF16)
    grad[...] = etotal * after_grad + dot(c, edy, ((0,), (0,)))


def scan_forward(x, b, c, step, decay, decay_t, enter):
    seqs, length, inner = x.shape
    state, heads = b.shape[2], step.shape[2]
    chunks = length // CHUNK

    def block(lanes):
        return pl.BlockSpec((1, CHUNK, lanes), lambda s, k: (s, k, 0))

    return pl.pallas_call(
        scan_kernel,
        grid=(seqs, chunks),
        in_specs=[
            block(inner),
            block(state),
            block(state),
            block(heads),
            block(heads),
            pl.BlockSpec((1, heads, CHUNK), lambda s, k: (s, 0, k)),
            pl.BlockSpec((1, state, inner), lambda s, k: (s, 0, 0)),
        ],
        out_specs=[
            block(inner),
            pl.BlockSpec((1, 1, state, inner), lambda s, k: (s, k, 0, 0)),
        ],
        out_shape=[
            jax.ShapeDtypeStruct((seqs, length, inner), F32),
            jax.ShapeDtypeStruct((seqs, chunks, state, inner), F32),
        ],
        scratch_shapes=[pltpu.VMEM((state, inner), F32)],
        compiler_params=pltpu.CompilerParams(vmem_limit_bytes=40 << 20),
        cost_estimate=load(13),
    )(x, b, c, step, decay, decay_t, enter)


def scan_backward(x, b, c, step, decay, decay_t, skip, dy, y, states, leave):
    seqs, length, inner = x.shape
    state, heads = b.shape[2], step.shape[2]
    chunks = length // CHUNK

    def block(lanes):
        return pl.BlockSpec((1, CHUNK, lanes), lambda s, k: (s, chunks - 1 - k, 0))

    return pl.pallas_call(
        back_kernel,
        grid=(seqs, chunks),
        in_specs=[
            block(inner),
            block(state),
            block(state),
            block(heads),
            block(heads),
            pl.BlockSpec((1, heads, CHUNK), lambda s, k: (s, 0, chunks - 1 - k)),
            pl.BlockSpec((1, 1, inner), lambda s, k: (0, 0, 0)),
            block(inner),
            block(inner),
            pl.BlockSpec((1, 1, state, inner), lambda s, k: (s, chunks - 1 - k, 0, 0)),
            pl.BlockSpec((1, state, inner), lambda s, k: (s, 0, 0)),
        ],
        out_specs=[block(inner), block(2 * state), block(heads), block(heads), block(heads)],
        out_shape=[
            jax.ShapeDtypeStruct((seqs, length, inner), F32),
            jax.ShapeDtypeStruct((seqs, length, 2 * state), BF16),
            jax.ShapeDtypeStruct((seqs, length, heads), F32),
            jax.ShapeDtypeStruct((seqs, length, heads), F32),
            jax.ShapeDtypeStruct((seqs, length, heads), F32),
        ],
        scratch_shapes=[pltpu.VMEM((state, inner), F32)],
        compiler_params=pltpu.CompilerParams(vmem_limit_bytes=40 << 20),
        cost_estimate=load(27),
    )(x, b, c, step, decay, decay_t, skip, dy, y, states, leave)


def picked(scalars_ref, part_ref, got_ref):
    bit = scalars_ref[scalars_ref.shape[0] - 1]
    half = pl.num_programs(0) // 2
    own = (pl.program_id(0) // half) == bit
    return jnp.where(own, part_ref[...].astype(F32), got_ref[...].astype(F32))


def out_kernel(scalars_ref, part_ref, got_ref, tokens_ref, scale_ref, out_ref):
    projected = picked(scalars_ref, part_ref, got_ref)
    out_ref[...] = (tokens_ref[...].astype(F32) + scale_ref[...] * projected).astype(BF16)


def tail_kernel(
    local_len, scalars_ref, part_ref, got_ref, bc_ref, weight_ref, tokens_ref, back_ref, gain_ref,
    out_ref, gain_grad_ref
):
    step = pl.program_id(0)
    height = tokens_ref.shape[0]
    normed_grad = picked(scalars_ref, part_ref, got_ref) + dot(
        bc_ref[...], weight_ref[...], ((1,), (1,))
    )
    tokens = tokens_ref[...].astype(F32)
    inverse_rms = lax.rsqrt(jnp.mean(tokens * tokens, axis=-1, keepdims=True) + EPS)
    unit = tokens * inverse_rms

    @pl.when(step == 0)
    def _():
        gain_grad_ref[...] = jnp.zeros_like(gain_grad_ref)

    gain_grad_ref[...] += jnp.sum(normed_grad * unit, axis=0, keepdims=True)
    unit_grad = normed_grad * gain_ref[...]
    along = jnp.mean(unit_grad * unit, axis=-1, keepdims=True)
    row = step * height
    length = scalars_ref[row // local_len]
    start = scalars_ref[scalars_ref.shape[0] - 2] + row % local_len
    position = start + lax.broadcasted_iota(jnp.int32, tokens.shape, 0)
    back = jnp.where(position < length, back_ref[...].astype(F32), 0.0)
    out_ref[...] = back + inverse_rms * (unit_grad - unit * along)


ROWS = 256


def load(microseconds):
    return pl.CostEstimate(flops=0, transcendentals=0, bytes_accessed=int(microseconds * 3.69e6))


def merge_call(kernel, scalars, part, got, others, other_specs, out_specs, out_shape):
    rows, width = 2 * part.shape[0], part.shape[1]
    blocks = rows // ROWS
    half = pl.BlockSpec((ROWS, width), lambda i, s: (i % (blocks // 2), 0))
    return pl.pallas_call(
        kernel,
        grid_spec=pltpu.PrefetchScalarGridSpec(
            num_scalar_prefetch=1,
            grid=(blocks,),
            in_specs=[half, half] + other_specs,
            out_specs=out_specs,
        ),
        out_shape=out_shape,
        compiler_params=pltpu.CompilerParams(vmem_limit_bytes=40 << 20),
        cost_estimate=load(8),
    )(scalars, part, got, *others)


def row_block(lanes):
    return pl.BlockSpec((ROWS, lanes), lambda i, s: (i, 0))


def whole_block(shape):
    return pl.BlockSpec(shape, lambda i, s: (0, 0))


def adam_kernel(
    step_rate, decay_weight, first_ref, second_ref, weight_ref, mean_ref, square_ref,
    mean_out, square_out, weight_out
):
    for r in range(weight_ref.shape[1]):
        source = first_ref if r % 2 == 0 else second_ref
        gradient = source[:, (r // 2) * 128 : (r // 2 + 1) * 128].astype(F32)
        updated = adam_update(
            weight_ref[:, r], mean_ref[:, r], square_ref[:, r], gradient, step_rate, decay_weight
        )
        mean_out[:, r], square_out[:, r], weight_out[:, r] = updated


def adam_pair(weight, mean_old, square_old, first, second, step_rate, decay_weight):
    rows, _, columns = weight.shape
    height = 128
    narrow = pl.BlockSpec((height, columns), lambda i: (i, 0))
    tiles = pl.BlockSpec((height, columns // 64, 128), lambda i: (i, 0, 0))
    updated = pl.pallas_call(
        functools.partial(adam_kernel, step_rate, decay_weight),
        grid=(rows // height,),
        in_specs=[narrow, narrow, tiles, tiles, tiles],
        out_specs=[tiles, tiles, tiles],
        out_shape=[jax.ShapeDtypeStruct((rows, columns // 64, 128), F32)] * 3,
        compiler_params=pltpu.CompilerParams(vmem_limit_bytes=40 << 20),
        cost_estimate=load(9),
    )(first, second, lane_tiles(weight), lane_tiles(mean_old), lane_tiles(square_old))
    return [from_lane_tiles(part, weight.shape) for part in updated]


def silu_slope(values):
    sigmoid_part = jax.nn.sigmoid(values)
    return sigmoid_part * (1.0 + values * (1.0 - sigmoid_part))


def adam_update(weight, mean_old, square_old, gradient, step_rate, decay_weight):
    mean_new = BETA_ONE * mean_old + (1.0 - BETA_ONE) * gradient
    square_new = BETA_TWO * square_old + (1.0 - BETA_TWO) * gradient * gradient
    corrected_mean = mean_new / (1.0 - BETA_ONE**STEP)
    corrected_square = square_new / (1.0 - BETA_TWO**STEP)
    weight_new = weight - step_rate * (
        corrected_mean / (jnp.sqrt(corrected_square) + ADAM_EPS) + decay_weight * weight
    )
    return (mean_new, square_new, weight_new)


def shards(
    inputs,
    cotangent,
    lengths,
    norm_gain,
    norm_gain_mean,
    norm_gain_square,
    proj_zx,
    proj_zx_mean,
    proj_zx_square,
    proj_bc,
    proj_bc_mean,
    proj_bc_square,
    proj_step,
    proj_step_mean,
    proj_step_square,
    conv_inner,
    conv_inner_mean,
    conv_inner_square,
    conv_bc,
    conv_bc_mean,
    conv_bc_square,
    head_params,
    head_params_mean,
    head_params_square,
    gate_gain,
    gate_gain_mean,
    gate_gain_square,
    proj_out,
    proj_out_mean,
    proj_out_square,
):
    seq_count, local_len, model_width = inputs.shape
    local_inner = proj_zx.shape[2]
    state_width = proj_bc.shape[1] // 2
    local_heads = proj_step.shape[1]
    head_width = local_inner // local_heads
    rows = seq_count * local_len
    seq_size, seq_index = lax.axis_size("seq"), lax.axis_index("seq")

    def wide(a):
        selector = jnp.repeat(jnp.eye(local_heads, dtype=F32), head_width, axis=1)
        return jnp.einsum("...h,hc->...c", a, selector, precision=HIGHEST_PREC)

    positions = seq_index * local_len + jnp.arange(local_len)
    is_valid = (positions[None, :] < lengths[:, None]).astype(F32)
    tokens = inputs.astype(F32)
    inverse_rms = lax.rsqrt(jnp.mean(tokens * tokens, axis=-1, keepdims=True) + EPS)
    unit_tokens = tokens * inverse_rms
    normed = (unit_tokens * norm_gain).astype(BF16)
    z_weight = proj_zx[:, 0].astype(BF16)
    x_weight = proj_zx[:, 1].astype(BF16)
    bc_weight = proj_bc.astype(BF16)
    step_weight = proj_step.astype(BF16)
    out_weight = proj_out.astype(BF16)
    xbc_weight = jnp.concatenate([x_weight, bc_weight], axis=1)
    mixed_in = jnp.einsum("btd,dc->btc", normed, xbc_weight, preferred_element_type=F32).astype(BF16)
    edge_in = passed_along(mixed_in[:, local_len - CONV + 1 :], "seq", 1)
    raw_step = jnp.einsum("btd,dh->bth", normed, step_weight, preferred_element_type=F32)
    gate_input = jnp.einsum("btd,dc->btc", normed, z_weight, preferred_element_type=F32)
    padded = jnp.concatenate([edge_in, mixed_in], axis=1)
    conv_weight = jnp.concatenate([conv_inner, conv_bc], axis=-1)
    convolved = conv_weight[CONV] + jnp.zeros(mixed_in.shape, F32)
    for tap_index in range(CONV):
        convolved = (
            convolved + conv_weight[tap_index] * padded[:, tap_index : tap_index + local_len]
        )
    activated = jax.nn.silu(convolved).astype(BF16)
    x_values = activated[..., :local_inner]
    b_values = activated[..., local_inner : local_inner + state_width]
    c_values = activated[..., local_inner + state_width :]
    decay_log, step_bias, skip_gain = head_params[0], head_params[1], head_params[2]
    step_size = jax.nn.softplus(raw_step + step_bias)
    log_decay = -step_size * jnp.exp(decay_log)
    earlier = jnp.tril(jnp.ones((local_len, local_len), F32))
    running = jnp.einsum("ts,bsh->bth", earlier, log_decay, precision=HIGHEST_PREC)
    device_decay = running[:, -1]
    decay_t = log_decay.transpose(0, 2, 1)

    weighted = x_values.astype(F32) * wide(jnp.exp(device_decay[:, None] - running) * step_size)
    local_state = jnp.einsum(
        "btn,btc->bnc", b_values, weighted.astype(BF16), preferred_element_type=F32
    )
    unit_decay = wide(jnp.exp(device_decay))[:, None]
    entering, block_decays = states_before(local_state, unit_decay, "seq")

    scanned_raw, states = scan_forward(
        x_values, b_values, c_values, step_size, log_decay, decay_t, entering
    )
    skip_wide = jnp.repeat(skip_gain, head_width)[None, None]
    scanned = scanned_raw + skip_wide * x_values.astype(F32)
    gate_act = jax.nn.silu(gate_input)
    gated_values = scanned * gate_act
    square_sum = jnp.sum(gated_values * gated_values, axis=-1)
    scaled = (gated_values * gate_gain).astype(BF16)
    partial_out = jnp.einsum("bti,di->btd", scaled, out_weight, preferred_element_type=F32)
    out_cotangent = cotangent.astype(F32) * is_valid[..., None]
    partial_scale_grad = jnp.sum(out_cotangent * partial_out, axis=-1)
    square_total, scale_grad = lax.psum(jnp.stack([square_sum, partial_scale_grad]), "head")
    out_scale = lax.rsqrt(square_total / INNER + EPS)
    proj_grad = (out_scale[..., None] * out_cotangent).astype(BF16)
    square_grad = -0.5 * scale_grad * out_scale * out_scale * out_scale / INNER
    out_weight_grad = jnp.einsum("btd,bti->di", proj_grad, scaled, preferred_element_type=F32)
    scaled_grad = jnp.einsum("btd,di->bti", proj_grad, out_weight, preferred_element_type=F32)
    gate_gain_grad = jnp.sum(scaled_grad * gated_values, axis=(0, 1))
    gated_grad = scaled_grad * gate_gain + 2.0 * gated_values * square_grad[..., None]
    scanned_grad = gated_grad * gate_act
    gate_grad = (gated_grad * scanned * silu_slope(gate_input)).astype(BF16)
    local_back = jnp.einsum(
        "btn,btc->bnc",
        c_values,
        (scanned_grad * wide(jnp.exp(running))).astype(BF16),
        preferred_element_type=F32,
    )
    leaving = states_after(local_back, block_decays, "seq")
    z_weight_grad = jnp.einsum("btd,btc->dc", normed, gate_grad, preferred_element_type=F32)
    early_grads = jnp.concatenate([out_weight_grad, z_weight_grad], axis=0).astype(BF16)
    early_grads, _ = lax.optimization_barrier((early_grads, leaving))
    early_parts = exchanged(to_blocks(early_grads, seq_size), "seq")
    projected = halved(partial_out.astype(BF16).reshape(rows, model_width), "head")
    scanned_grad, projected = lax.optimization_barrier((scanned_grad, projected))
    projected_far = swapped(projected, "head", axis_masks("head")[-1])
    x_grad, bc_grad, decay_grad, step_grad, skip_terms = scan_backward(
        x_values,
        b_values,
        c_values,
        step_size,
        log_decay,
        decay_t,
        skip_wide,
        scanned_grad,
        scanned_raw,
        states,
        leaving,
    )
    x_grad_late, early_parts, projected_far = lax.optimization_barrier(
        (x_grad, early_parts, projected_far)
    )
    projected_half, projected_other = regathered(added(projected, projected_far), "head")
    early_own = jnp.sum(early_parts.astype(F32), axis=0).astype(BF16)
    early_all = exchanged(jnp.broadcast_to(early_own[None], early_parts.shape), "seq")
    bc_total = halving_sum(bc_grad.reshape(rows, 2 * state_width), "head")
    bc_total = bc_total.reshape(bc_grad.shape).astype(F32)

    def conv_back(activated_grad, activated_grad_late, first, last):
        convolved_grad = activated_grad * silu_slope(convolved[..., first:last])
        taps = conv_weight[:, first:last]
        tap_grads = []
        convolved_late = activated_grad_late * silu_slope(convolved[..., first:last])
        padded_grad = jnp.zeros((seq_count, local_len + CONV - 1, last - first), F32)
        for tap_index in range(CONV):
            tap_grads.append(
                jnp.sum(
                    convolved_grad * padded[:, tap_index : tap_index + local_len, first:last],
                    axis=(0, 1),
                )
            )
            padded_grad = padded_grad + jnp.pad(
                taps[tap_index] * convolved_late,
                ((0, 0), (tap_index, CONV - 1 - tap_index), (0, 0)),
            )
        tap_grads.append(jnp.sum(convolved_grad, axis=(0, 1)))
        edge_grad = passed_along(padded_grad[:, : CONV - 1], "seq", -1)
        mixed_grad = padded_grad[:, CONV - 1 :] + jnp.pad(
            edge_grad, ((0, 0), (local_len - CONV + 1, 0), (0, 0))
        )
        return mixed_grad.astype(BF16), jnp.stack(tap_grads)

    x_in_grad, conv_inner_grad = conv_back(x_grad, x_grad_late, 0, local_inner)
    step_total = step_grad - jnp.exp(decay_log) * decay_grad
    pre_grad = step_total * jax.nn.sigmoid(raw_step + step_bias)
    head_grad = jnp.stack(
        [
            jnp.sum(decay_grad * log_decay, axis=(0, 1)),
            jnp.sum(pre_grad, axis=(0, 1)),
            jnp.sum(skip_terms, axis=(0, 1)),
        ]
    )
    step_in_grad = pre_grad.astype(BF16)
    normed_partial = (
        jnp.einsum("btc,dc->btd", gate_grad, z_weight, preferred_element_type=F32)
        + jnp.einsum("btc,dc->btd", x_in_grad, x_weight, preferred_element_type=F32)
        + jnp.einsum("bth,dh->btd", step_in_grad, step_weight, preferred_element_type=F32)
    )
    normed_sum = halved(normed_partial.astype(BF16).reshape(rows, model_width), "head")
    normed_far = swapped(normed_sum, "head", axis_masks("head")[-1])
    normed_half, normed_other = regathered(added(normed_sum, normed_far), "head")
    bc_in_grad, conv_bc_grad = conv_back(
        bc_total, bc_total, local_inner, local_inner + 2 * state_width
    )
    x_in_late, early_all = lax.optimization_barrier((x_in_grad, early_all))
    early_sums = early_all.reshape(2, model_width, local_inner)
    x_weight_grad = jnp.einsum("btd,btc->dc", normed, x_in_late, preferred_element_type=F32)
    bc_weight_grad = jnp.einsum("btd,btc->dc", normed, bc_in_grad, preferred_element_type=F32)
    step_weight_grad = jnp.einsum("btd,bth->hd", normed, step_in_grad, preferred_element_type=F32)
    late_grads = (x_weight_grad.astype(BF16), bc_weight_grad.astype(BF16))
    late_sums = lax.psum(late_grads, "seq")
    scalars = jnp.concatenate(
        [lengths, jnp.stack([seq_index * local_len, near_bit("head", 1)]).astype(jnp.int32)]
    )
    flat_tokens = inputs.reshape(rows, model_width)
    input_grad, norm_gain_grad = merge_call(
        functools.partial(tail_kernel, local_len),
        scalars,
        normed_half,
        normed_other,
        (
            bc_in_grad.reshape(rows, 2 * state_width),
            bc_weight,
            flat_tokens,
            cotangent.reshape(rows, model_width),
            norm_gain[None],
        ),
        [
            row_block(2 * state_width),
            whole_block(bc_weight.shape),
            row_block(model_width),
            row_block(model_width),
            whole_block((1, model_width)),
        ],
        [row_block(model_width), whole_block((1, model_width))],
        [
            jax.ShapeDtypeStruct((rows, model_width), F32),
            jax.ShapeDtypeStruct((1, model_width), F32),
        ],
    )
    input_grad = input_grad.reshape(inputs.shape)
    block_out = merge_call(
        out_kernel,
        scalars,
        projected_half,
        projected_other,
        (flat_tokens, out_scale.reshape(rows, 1)),
        [row_block(model_width), row_block(1)],
        row_block(model_width),
        jax.ShapeDtypeStruct((rows, model_width), BF16),
    ).reshape(inputs.shape)
    late_sums, _, _ = lax.optimization_barrier((late_sums, input_grad, block_out))
    small_grads = (
        norm_gain_grad[0],
        step_weight_grad,
        conv_inner_grad,
        conv_bc_grad,
        head_grad,
        gate_gain_grad,
    )
    flat = jnp.concatenate([part.reshape(-1) for part in small_grads])
    count = flat.shape[0]
    flat = jnp.pad(flat, (0, -count % 1024)).reshape(-1, 128)
    flat = doubling_sum(flat, "seq").reshape(-1)
    small_sums, at = [], 0
    for part in small_grads:
        small_sums.append(flat[at : at + part.size].reshape(part.shape))
        at += part.size

    summed_grads = (
        small_sums[0],
        (early_sums[1], late_sums[0].reshape(model_width, local_inner)),
        late_sums[1].astype(F32),
        small_sums[1].T,
        small_sums[2],
        small_sums[3],
        small_sums[4],
        small_sums[5],
        early_sums[0].astype(F32),
    )
    params = (
        norm_gain,
        proj_zx,
        proj_bc,
        proj_step,
        conv_inner,
        conv_bc,
        head_params,
        gate_gain,
        proj_out,
    )
    means = (
        norm_gain_mean,
        proj_zx_mean,
        proj_bc_mean,
        proj_step_mean,
        conv_inner_mean,
        conv_bc_mean,
        head_params_mean,
        gate_gain_mean,
        proj_out_mean,
    )
    squares = (
        norm_gain_square,
        proj_zx_square,
        proj_bc_square,
        proj_step_square,
        conv_inner_square,
        conv_bc_square,
        head_params_square,
        gate_gain_square,
        proj_out_square,
    )
    results = [block_out, input_grad]
    for weight, mean_old, square_old, gradient, step_rate, decay_weight in zip(
        params, means, squares, summed_grads, LEARNING_RATES, WEIGHT_DECAYS
    ):
        if weight.ndim == 3:
            updated = adam_pair(weight, mean_old, square_old, *gradient, step_rate, decay_weight)
        else:
            updated = adam_update(weight, mean_old, square_old, gradient, step_rate, decay_weight)
        results.extend(updated)
    return tuple(results)


def solution(mesh):
    in_specs = (
        P(None, "seq", None),
        P(None, "seq", None),
        P(),
        P(),
        P(),
        P(),
        P(None, None, "head"),
        P(None, None, "head"),
        P(None, None, "head"),
        P(),
        P(),
        P(),
        P(None, "head"),
        P(None, "head"),
        P(None, "head"),
        P(None, "head"),
        P(None, "head"),
        P(None, "head"),
        P(),
        P(),
        P(),
        P(None, "head"),
        P(None, "head"),
        P(None, "head"),
        P("head"),
        P("head"),
        P("head"),
        P(None, "head"),
        P(None, "head"),
        P(None, "head"),
    )
    out_specs = (
        P(None, "seq", None),
        P(None, "seq", None),
        P(),
        P(),
        P(),
        P(None, None, "head"),
        P(None, None, "head"),
        P(None, None, "head"),
        P(),
        P(),
        P(),
        P(None, "head"),
        P(None, "head"),
        P(None, "head"),
        P(None, "head"),
        P(None, "head"),
        P(None, "head"),
        P(),
        P(),
        P(),
        P(None, "head"),
        P(None, "head"),
        P(None, "head"),
        P("head"),
        P("head"),
        P("head"),
        P(None, "head"),
        P(None, "head"),
        P(None, "head"),
    )
    return jax.shard_map(shards, mesh=mesh, in_specs=in_specs, out_specs=out_specs, check_vma=False)
```

```python
import functools

import jax
import jax.numpy as jnp
from jax import lax
from jax.experimental import pallas as pl
from jax.experimental.pallas import tpu as pltpu
from jax.sharding import PartitionSpec as P

INNER = 2048
CONV = 4
CHUNK = 128
STEP = 7


EPS = 1e-05
BETA_ONE = 0.9
BETA_TWO = 0.95
ADAM_EPS = 1e-08
LEARNING_RATES = (0.6, 0.09, 0.09, 0.09, 0.9, 0.9, 0.9, 0.6, 0.06)
WEIGHT_DECAYS = (0.0, 0.1, 0.1, 0.1, 0.0, 0.0, 0.0, 0.0, 0.1)
HIGHEST_PREC = lax.Precision.HIGHEST
F32 = jnp.float32
BF16 = jnp.bfloat16


def passed_along(block, axis, distance):
    devices = range(lax.axis_size(axis))
    route = [(i - distance, i) for i in devices if i - distance in devices]
    return lax.ppermute(block, axis, route)


def swapped(block, axis, mask):
    return lax.ppermute(block, axis, [(i, i ^ mask) for i in range(lax.axis_size(axis))])


def doubling_sum(part, axis):
    for k in range(lax.axis_size(axis).bit_length() - 1):
        part = part + swapped(part, axis, 1 << k)
    return part


def axis_masks(axis):
    return [1 << k for k in range(lax.axis_size(axis).bit_length() - 1)]


def near_bit(axis, mask):
    return (lax.axis_index(axis) // mask) % 2


def added(a, b):
    return (a.astype(F32) + b.astype(F32)).astype(BF16)


def halved(part, axis):
    for mask in axis_masks(axis)[:-1]:
        bit = near_bit(axis, mask)
        halves = part.reshape((2, part.shape[0] // 2) + part.shape[1:])
        sent = lax.dynamic_index_in_dim(halves, 1 - bit, 0, keepdims=False)
        kept = lax.dynamic_index_in_dim(halves, bit, 0, keepdims=False)
        part = added(kept, swapped(sent, axis, mask))
    return part


def joined(part, got, bit):
    first = jnp.where(bit == 0, part, got)
    second = jnp.where(bit == 0, got, part)
    return jnp.concatenate([first, second], axis=0)


def regathered(part, axis):
    masks = axis_masks(axis)[:-1]
    for mask in reversed(masks[1:]):
        part = joined(part, swapped(part, axis, mask), near_bit(axis, mask))
    return part, swapped(part, axis, masks[0])


def halving_sum(part, axis):
    part = halved(part, axis)
    part = added(part, swapped(part, axis, axis_masks(axis)[-1]))
    part, other = regathered(part, axis)
    return joined(part, other, near_bit(axis, 1))


def exchanged(blocks, axis):
    return lax.all_to_all(blocks, axis, 0, 0, tiled=True)


def to_blocks(state, count):
    return state.astype(BF16).reshape(count, -1, state.shape[-1])


def states_before(state, decay, axis):
    size = lax.axis_size(axis)
    blocks = to_blocks(state, size)
    height = blocks.shape[1]
    high = decay.astype(BF16)
    low = (decay - high.astype(F32)).astype(BF16)
    empty = jnp.zeros((decay.shape[0], 14, decay.shape[2]), BF16)
    extra = jnp.concatenate([high, low, empty], axis=1)
    extra = jnp.repeat(extra, size // decay.shape[0], axis=0)
    got = exchanged(jnp.concatenate([blocks, extra], axis=1), axis).astype(F32)
    decays = got[:, height : height + 1] + got[:, height + 1 : height + 2]
    entering = [jnp.zeros(got[0, :height].shape, F32)]
    for k in range(size - 1):
        entering.append(decays[k] * entering[-1] + got[k, :height])
    back = exchanged(jnp.stack(entering).astype(BF16), axis)
    return back.reshape(state.shape).astype(F32), decays


def states_after(state, decays, axis):
    size = lax.axis_size(axis)
    got = exchanged(to_blocks(state, size), axis).astype(F32)
    leaving = [jnp.zeros(got[0].shape, F32)]
    for k in range(size - 1, 0, -1):
        leaving.append(decays[k] * leaving[-1] + got[k])
    back = exchanged(jnp.stack(leaving[::-1]).astype(BF16), axis)
    return back.reshape(state.shape).astype(F32)


def lane_tiles(a):
    rows, two, columns = a.shape
    return a.reshape(rows, two, columns // 128, 128).transpose(0, 2, 1, 3).reshape(rows, -1, 128)


def from_lane_tiles(a, shape):
    rows, two, columns = shape
    return a.reshape(rows, columns // 128, two, 128).transpose(0, 2, 1, 3).reshape(shape)


def dot(a, b, dims=((1,), (0,)), precision=None):
    return lax.dot_general(a, b, (dims, ((), ())), precision=precision, preferred_element_type=F32)


def expander(heads, width):
    row = lax.broadcasted_iota(jnp.int32, (heads, heads * width), 0)
    column = lax.broadcasted_iota(jnp.int32, (heads, heads * width), 1)
    inside = (column >= row * width) & (column < (row + 1) * width)
    return jnp.where(inside, 1.0, 0.0).astype(BF16)


def split_dot(a, b, dims):
    high = a.astype(BF16)
    low = (a - high.astype(F32)).astype(BF16)
    return dot(high, b, dims) + dot(low, b, dims)


def spread(a, expand):
    return split_dot(a, expand, ((1,), (0,)))


def head_sums(a, expand):
    return split_dot(a, expand, ((1,), (1,)))


def pair_rows(a):
    lane = lax.broadcasted_iota(jnp.int32, a.shape, 1)
    first = lane < a.shape[1] // 2
    zero = jnp.zeros_like(a)
    return jnp.concatenate([jnp.where(first, a, zero), jnp.where(first, zero, a)], axis=0)


def chunk_decays(decay, decay_t):
    q = decay.shape[0]
    row = lax.broadcasted_iota(jnp.int32, (q, q), 0)
    column = lax.broadcasted_iota(jnp.int32, (q, q), 1)
    lower = jnp.where(row >= column, 1.0, 0.0).astype(F32)
    cum = dot(lower, decay, precision=HIGHEST_PREC)
    cum_t = dot(decay_t, lower, ((1,), (1,)), precision=HIGHEST_PREC)
    return cum, cum_t, row, column


def scan_kernel(x_ref, b_ref, c_ref, step_ref, decay_ref, decay_t_ref, enter_ref, y_ref, in_ref, state):
    heads = step_ref.shape[2]
    width = x_ref.shape[2] // heads

    @pl.when(pl.program_id(1) == 0)
    def _():
        state[...] = enter_ref[0]

    expand = expander(heads, width)
    cum, cum_t, row, column = chunk_decays(decay_ref[0], decay_t_ref[0])
    causal = row >= column
    q = cum.shape[0]
    total = cum[q - 1 : q, :]
    b, c = b_ref[0], c_ref[0]
    x = x_ref[0].astype(F32)
    step = step_ref[0]
    xs = (x * spread(step, expand)).astype(BF16)
    grown = spread(jnp.exp(cum), expand)
    xw = (x * spread(step * jnp.exp(total - cum), expand)).astype(BF16)
    scores = dot(c, b, ((1,), (1,)))
    before = state[...]
    in_ref[0, 0] = before
    from_state = grown * dot(c, before.astype(BF16))
    for pair in range(heads // 2):
        lanes = slice(pair * 2 * width, (pair + 1) * 2 * width)
        mixing = []
        for h in (2 * pair, 2 * pair + 1):
            between = cum[:, h : h + 1] - cum_t[h : h + 1, :]
            mixing.append((jnp.exp(jnp.where(causal, between, -1e30)) * scores).astype(BF16))
        within = dot(jnp.concatenate(mixing, axis=1), pair_rows(xs[:, lanes]))
        y_ref[0, :, lanes] = within + from_state[:, lanes]
    state[...] = grown[q - 1 : q, :] * before + dot(b, xw, ((0,), (0,)))


def conv_back_step(act_grad, mixed, previous, taps, after_ref):
    q = mixed.shape[0]
    window = jnp.concatenate([previous, mixed], axis=0)
    shifted = [window[8 - CONV + 1 + k : 8 - CONV + 1 + k + q] for k in range(CONV)]
    convolved = taps[CONV : CONV + 1]
    for k in range(CONV):
        convolved = convolved + taps[k : k + 1] * shifted[k]
    conv_grad = act_grad * silu_slope(convolved)
    extended = jnp.concatenate([conv_grad, after_ref[...]], axis=0)
    mixed_grad = taps[CONV - 1 : CONV] * conv_grad
    for k in range(CONV - 1):
        mixed_grad = mixed_grad + taps[k : k + 1] * extended[CONV - 1 - k : CONV - 1 - k + q]
    sums = [jnp.sum(conv_grad * part, axis=0, keepdims=True) for part in shifted]
    sums.append(jnp.sum(conv_grad, axis=0, keepdims=True))
    sums.append(jnp.zeros((8 - CONV - 1, mixed.shape[1]), F32))
    after_ref[...] = conv_grad[:8]
    return conv_grad, mixed_grad, jnp.concatenate(sums, axis=0)


def rows_before(edge_ref, previous_ref):
    first = pl.program_id(1) == pl.num_programs(1) - 1
    return jnp.where(first, edge_ref[0].astype(F32), previous_ref[0].astype(F32))[8:]


def back_kernel(
    x_ref, b_ref, c_ref, step_ref, decay_ref, decay_t_ref, skip_ref, dy_ref, y_ref, in_ref, leave_ref,
    mixed_ref, previous_ref, edge_ref, taps_ref, slope_ref, rate_ref,
    mixed_grad_ref, dbc_ref, pre_ref, first_ref, last_ref, tap_sums_ref, head_sums_ref,
    grad, after
):
    start = (pl.program_id(0) == 0) & (pl.program_id(1) == 0)

    @pl.when(start)
    def _():
        tap_sums_ref[...] = jnp.zeros_like(tap_sums_ref)
        head_sums_ref[...] = jnp.zeros_like(head_sums_ref)

    @pl.when(pl.program_id(1) == 0)
    def _():
        after[...] = jnp.zeros_like(after)

    heads = step_ref.shape[2]
    width = x_ref.shape[2] // heads

    @pl.when(pl.program_id(1) == 0)
    def _():
        grad[...] = leave_ref[0]

    expand = expander(heads, width)
    cum, cum_t, row, column = chunk_decays(decay_ref[0], decay_t_ref[0])
    later = column >= row
    q = cum.shape[0]
    total = cum[q - 1 : q, :]
    b, c = b_ref[0], c_ref[0]
    x = x_ref[0].astype(F32)
    step = step_ref[0]
    step_wide = spread(step, expand)
    xs = (x * step_wide).astype(BF16)
    grown = spread(jnp.exp(cum), expand)
    waned = spread(jnp.exp(total - cum), expand)
    xw = (x * step_wide * waned).astype(BF16)
    dy = dy_ref[0]
    dy_low = dy.astype(BF16)
    edy = (dy * grown).astype(BF16)
    before = in_ref[0, 0]
    after_grad = grad[...]
    after_low = after_grad.astype(BF16)
    scores_t = dot(b, c, ((1,), (1,)))
    v_state = waned * dot(b, after_low)
    dscores_t = jnp.zeros((q, q), F32)
    v_parts = []
    for pair in range(heads // 2):
        lanes = slice(pair * 2 * width, (pair + 1) * 2 * width)
        dy_pair = pair_rows(dy_low[:, lanes])
        xs_pair = pair_rows(xs[:, lanes])
        dmix = dot(xs_pair, dy_low[:, lanes], ((1,), (1,)))
        mixing = []
        for k, h in enumerate((2 * pair, 2 * pair + 1)):
            between = cum_t[h : h + 1, :] - cum[:, h : h + 1]
            fade = jnp.exp(jnp.where(later, between, -1e30))
            mixing.append((fade * scores_t).astype(BF16))
            dscores_t = dscores_t + fade * dmix[k * q : (k + 1) * q]
        v_parts.append(dot(jnp.concatenate(mixing, axis=1), dy_pair))
    v = jnp.concatenate(v_parts, axis=1) + v_state
    xs_wide = xs.astype(F32)
    etotal = grown[q - 1 : q, :]
    dx = step_wide * v + skip_ref[0] * dy
    conv_grad, mixed_grad, tap_sums = conv_back_step(
        dx, mixed_ref[0].astype(F32), rows_before(edge_ref, previous_ref), taps_ref[...], after
    )
    mixed_grad_ref[0] = mixed_grad.astype(BF16)
    first_ref[0] = conv_grad[:8]

    @pl.when(pl.program_id(1) == 0)
    def _():
        last_ref[0] = mixed_grad[q - 8 :]

    tap_sums_ref[...] += tap_sums
    end_row = jnp.sum(xs_wide * v_state, axis=0, keepdims=True) + jnp.sum(
        etotal * before * after_grad, axis=0, keepdims=True
    )
    crossing = dy_low.astype(F32) * y_ref[0] - xs_wide * v
    last = lax.broadcasted_iota(jnp.int32, crossing.shape, 0) == q - 1
    crossing = crossing + jnp.where(last, end_row, 0.0)
    upper = jnp.where(column >= row, 1.0, 0.0).astype(F32)
    decay_grad = dot(upper, head_sums(crossing, expand), precision=HIGHEST_PREC)
    pre_grad = (head_sums(x * v, expand) - rate_ref[...] * decay_grad) * slope_ref[0]
    pre_ref[0] = pre_grad.astype(BF16)
    sums = [
        jnp.sum(decay_grad * decay_ref[0], axis=0, keepdims=True),
        jnp.sum(pre_grad, axis=0, keepdims=True),
        jnp.sum(head_sums(x * dy, expand), axis=0, keepdims=True),
        jnp.zeros((5, heads), F32),
    ]
    head_sums_ref[...] += jnp.concatenate(sums, axis=0)
    dscores_low = dscores_t.astype(BF16)
    state = b.shape[1]
    dbc_ref[0, :, :state] = (
        dot(dscores_low, c) + dot(xw, after_low, ((1,), (1,)))
    ).astype(BF16)
    dbc_ref[0, :, state:] = (
        dot(dscores_low, b, ((0,), (0,))) + dot(edy, before.astype(BF16), ((1,), (1,)))
    ).astype(BF16)
    grad[...] = etotal * after_grad + dot(c, edy, ((0,), (0,)))


def act_blocks(inner, state, place):
    def part(lanes, at):
        return pl.BlockSpec((1, CHUNK, lanes), lambda s, k: (s, place(k), at))

    return [part(inner, 0), part(state, inner // state), part(state, inner // state + 1)]


def scan_forward(activated, step, decay, decay_t, enter):
    seqs, length, heads = step.shape
    state, inner = enter.shape[1:]
    chunks = length // CHUNK

    def block(lanes):
        return pl.BlockSpec((1, CHUNK, lanes), lambda s, k: (s, k, 0))

    return pl.pallas_call(
        scan_kernel,
        grid=(seqs, chunks),
        in_specs=act_blocks(inner, state, lambda k: k)
        + [
            block(heads),
            block(heads),
            pl.BlockSpec((1, heads, CHUNK), lambda s, k: (s, 0, k)),
            pl.BlockSpec((1, state, inner), lambda s, k: (s, 0, 0)),
        ],
        out_specs=[
            block(inner),
            pl.BlockSpec((1, 1, state, inner), lambda s, k: (s, k, 0, 0)),
        ],
        out_shape=[
            jax.ShapeDtypeStruct((seqs, length, inner), F32),
            jax.ShapeDtypeStruct((seqs, chunks, state, inner), F32),
        ],
        scratch_shapes=[pltpu.VMEM((state, inner), F32)],
        compiler_params=pltpu.CompilerParams(vmem_limit_bytes=40 << 20),
        cost_estimate=load(13),
    )(activated, activated, activated, step, decay, decay_t, enter)


def conv_blocks(chunks, lanes, at):
    tall = CHUNK // 16
    return [
        pl.BlockSpec((1, CHUNK, lanes), lambda s, k, *_: (s, chunks - 1 - k, at)),
        pl.BlockSpec(
            (1, 16, lanes), lambda s, k, *_: (s, jnp.maximum((chunks - 1 - k) * tall - 1, 0), at)
        ),
        pl.BlockSpec((1, 16, lanes), lambda s, k, *_: (s, 0, at)),
        pl.BlockSpec((8, lanes), lambda s, k, *_: (0, at)),
    ]


def conv_outs(seqs, chunks, lanes):
    specs = [
        pl.BlockSpec((1, CHUNK, lanes), lambda s, k, *_: (s, chunks - 1 - k, 0)),
        pl.BlockSpec((1, 8, lanes), lambda s, k, *_: (s, 0, 0)),
        pl.BlockSpec((1, 8, lanes), lambda s, k, *_: (s, 0, 0)),
        pl.BlockSpec((8, lanes), lambda s, k, *_: (0, 0)),
    ]
    shapes = [
        jax.ShapeDtypeStruct((seqs, chunks * CHUNK, lanes), BF16),
        jax.ShapeDtypeStruct((seqs, 8, lanes), F32),
        jax.ShapeDtypeStruct((seqs, 8, lanes), F32),
        jax.ShapeDtypeStruct((8, lanes), F32),
    ]
    return specs, shapes


def scan_backward(
    activated, step, decay, decay_t, skip, dy, y, states, leave, mixed, edge, taps, slope, rate
):
    seqs, length, heads = step.shape
    state, inner = leave.shape[1:]
    chunks = length // CHUNK

    def block(lanes):
        return pl.BlockSpec((1, CHUNK, lanes), lambda s, k: (s, chunks - 1 - k, 0))

    conv_specs, conv_shapes = conv_outs(seqs, chunks, inner)
    return pl.pallas_call(
        back_kernel,
        grid=(seqs, chunks),
        in_specs=act_blocks(inner, state, lambda k: chunks - 1 - k)
        + [
            block(heads),
            block(heads),
            pl.BlockSpec((1, heads, CHUNK), lambda s, k: (s, 0, chunks - 1 - k)),
            pl.BlockSpec((1, 1, inner), lambda s, k: (0, 0, 0)),
            block(inner),
            block(inner),
            pl.BlockSpec((1, 1, state, inner), lambda s, k: (s, chunks - 1 - k, 0, 0)),
            pl.BlockSpec((1, state, inner), lambda s, k: (s, 0, 0)),
        ]
        + conv_blocks(chunks, inner, 0)
        + [block(heads), pl.BlockSpec((1, heads), lambda s, k: (0, 0))],
        out_specs=[conv_specs[0], block(2 * state), block(heads)]
        + conv_specs[1:]
        + [pl.BlockSpec((8, heads), lambda s, k: (0, 0))],
        out_shape=[
            conv_shapes[0],
            jax.ShapeDtypeStruct((seqs, length, 2 * state), BF16),
            jax.ShapeDtypeStruct((seqs, length, heads), BF16),
        ]
        + conv_shapes[1:]
        + [jax.ShapeDtypeStruct((8, heads), F32)],
        scratch_shapes=[pltpu.VMEM((state, inner), F32), pltpu.VMEM((8, inner), F32)],
        compiler_params=pltpu.CompilerParams(vmem_limit_bytes=40 << 20),
        cost_estimate=load(30),
    )(
        activated, activated, activated, step, decay, decay_t, skip, dy, y, states, leave,
        mixed, mixed, edge, taps, slope, rate
    )


def bc_kernel(
    scalars_ref, part_ref, got_ref, mixed_ref, previous_ref, edge_ref, taps_ref,
    mixed_grad_ref, first_ref, last_ref, tap_sums_ref, after
):
    start = (pl.program_id(0) == 0) & (pl.program_id(1) == 0)

    @pl.when(start)
    def _():
        tap_sums_ref[...] = jnp.zeros_like(tap_sums_ref)

    @pl.when(pl.program_id(1) == 0)
    def _():
        after[...] = jnp.zeros_like(after)

    q = mixed_ref.shape[1]
    act_grad = picked(scalars_ref, part_ref, got_ref)[0]
    conv_grad, mixed_grad, tap_sums = conv_back_step(
        act_grad, mixed_ref[0].astype(F32), rows_before(edge_ref, previous_ref), taps_ref[...], after
    )
    mixed_grad_ref[0] = mixed_grad.astype(BF16)
    first_ref[0] = conv_grad[:8]

    @pl.when(pl.program_id(1) == 0)
    def _():
        last_ref[0] = mixed_grad[q - 8 :]

    tap_sums_ref[...] += tap_sums


def bc_backward(scalars, part, got, mixed, edge, taps):
    seqs, length, lanes = mixed.shape
    chunks = length // CHUNK
    half = pl.BlockSpec((1, CHUNK, lanes), lambda s, k, _: (s % (seqs // 2), chunks - 1 - k, 0))
    conv_specs, conv_shapes = conv_outs(seqs, chunks, lanes)
    return pl.pallas_call(
        bc_kernel,
        grid_spec=pltpu.PrefetchScalarGridSpec(
            num_scalar_prefetch=1,
            grid=(seqs, chunks),
            in_specs=[half, half] + conv_blocks(chunks, lanes, 0),
            out_specs=conv_specs,
            scratch_shapes=[pltpu.VMEM((8, lanes), F32)],
        ),
        out_shape=conv_shapes,
        compiler_params=pltpu.CompilerParams(vmem_limit_bytes=40 << 20),
        cost_estimate=load(5),
    )(
        scalars,
        part.reshape(seqs // 2, length, lanes),
        got.reshape(seqs // 2, length, lanes),
        mixed,
        mixed,
        edge,
        taps,
    )


def joined_edges(mixed_grad, first, last, taps):
    rows = []
    for j in range(CONV - 1):
        rows.append(sum(taps[k] * first[:, j - k] for k in range(j + 1)))
    edge_grad = passed_along(jnp.stack(rows, axis=1), "seq", -1)
    fixed = last + jnp.pad(edge_grad, ((0, 0), (8 - CONV + 1, 0), (0, 0)))
    return lax.dynamic_update_slice(mixed_grad, fixed.astype(BF16), (0, mixed_grad.shape[1] - 8, 0))


def normed_kernel(gate_ref, x_ref, step_ref, z_weight_ref, x_weight_ref, step_weight_ref, out_ref):
    nt = ((1,), (1,))
    total = dot(gate_ref[...], z_weight_ref[...], nt) + dot(x_ref[...], x_weight_ref[...], nt)
    out_ref[...] = (total + dot(step_ref[...], step_weight_ref[...], nt)).astype(BF16)


def normed_products(gate_grad, x_grad, step_grad, z_weight, x_weight, step_weight):
    rows, width = gate_grad.shape[0], z_weight.shape[0]

    def block(a):
        return pl.BlockSpec((ROWS, a.shape[1]), lambda i: (i, 0))

    def whole(a):
        return pl.BlockSpec(a.shape, lambda i: (0, 0))

    args = (gate_grad, x_grad, step_grad, z_weight, x_weight, step_weight)
    return pl.pallas_call(
        normed_kernel,
        grid=(rows // ROWS,),
        in_specs=[block(a) for a in args[:3]] + [whole(a) for a in args[3:]],
        out_specs=pl.BlockSpec((ROWS, width), lambda i: (i, 0)),
        out_shape=jax.ShapeDtypeStruct((rows, width), BF16),
        compiler_params=pltpu.CompilerParams(vmem_limit_bytes=40 << 20),
        cost_estimate=load(6),
    )(*args)


def picked(scalars_ref, part_ref, got_ref):
    bit = scalars_ref[scalars_ref.shape[0] - 1]
    half = pl.num_programs(0) // 2
    own = (pl.program_id(0) // half) == bit
    return jnp.where(own, part_ref[...].astype(F32), got_ref[...].astype(F32))


def out_kernel(scalars_ref, part_ref, got_ref, tokens_ref, scale_ref, out_ref):
    projected = picked(scalars_ref, part_ref, got_ref)
    out_ref[...] = (tokens_ref[...].astype(F32) + scale_ref[...] * projected).astype(BF16)


def tail_kernel(
    local_len, scalars_ref, part_ref, got_ref, bc_ref, weight_ref, tokens_ref, back_ref, gain_ref,
    out_ref, gain_grad_ref
):
    step = pl.program_id(0)
    height = tokens_ref.shape[0]
    normed_grad = picked(scalars_ref, part_ref, got_ref) + dot(
        bc_ref[...], weight_ref[...], ((1,), (1,))
    )
    tokens = tokens_ref[...].astype(F32)
    inverse_rms = lax.rsqrt(jnp.mean(tokens * tokens, axis=-1, keepdims=True) + EPS)
    unit = tokens * inverse_rms

    @pl.when(step == 0)
    def _():
        gain_grad_ref[...] = jnp.zeros_like(gain_grad_ref)

    gain_grad_ref[...] += jnp.sum(normed_grad * unit, axis=0, keepdims=True)
    unit_grad = normed_grad * gain_ref[...]
    along = jnp.mean(unit_grad * unit, axis=-1, keepdims=True)
    row = step * height
    length = scalars_ref[row // local_len]
    start = scalars_ref[scalars_ref.shape[0] - 2] + row % local_len
    position = start + lax.broadcasted_iota(jnp.int32, tokens.shape, 0)
    back = jnp.where(position < length, back_ref[...].astype(F32), 0.0)
    out_ref[...] = back + inverse_rms * (unit_grad - unit * along)


ROWS = 256


def load(microseconds):
    return pl.CostEstimate(flops=0, transcendentals=0, bytes_accessed=int(microseconds * 3.69e6))


def merge_call(kernel, scalars, part, got, others, other_specs, out_specs, out_shape):
    rows, width = 2 * part.shape[0], part.shape[1]
    blocks = rows // ROWS
    half = pl.BlockSpec((ROWS, width), lambda i, s: (i % (blocks // 2), 0))
    return pl.pallas_call(
        kernel,
        grid_spec=pltpu.PrefetchScalarGridSpec(
            num_scalar_prefetch=1,
            grid=(blocks,),
            in_specs=[half, half] + other_specs,
            out_specs=out_specs,
        ),
        out_shape=out_shape,
        compiler_params=pltpu.CompilerParams(vmem_limit_bytes=40 << 20),
        cost_estimate=load(8),
    )(scalars, part, got, *others)


def row_block(lanes):
    return pl.BlockSpec((ROWS, lanes), lambda i, s: (i, 0))


def whole_block(shape):
    return pl.BlockSpec(shape, lambda i, s: (0, 0))


def adam_kernel(
    step_rate, decay_weight, gradient_ref, weight_ref, mean_ref, square_ref,
    mean_out, square_out, weight_out
):
    mean_out[...], square_out[...], weight_out[...] = adam_update(
        weight_ref[...],
        mean_ref[...],
        square_ref[...],
        gradient_ref[...].astype(F32),
        step_rate,
        decay_weight,
    )


def adam_tiles(weight, mean_old, square_old, gradient, step_rate, decay_weight):
    rows, _, columns = weight.shape
    tiles = pl.BlockSpec((128, columns // 64, 128), lambda i: (i, 0, 0))
    updated = pl.pallas_call(
        functools.partial(adam_kernel, step_rate, decay_weight),
        grid=(rows // 128,),
        in_specs=[tiles] * 4,
        out_specs=[tiles] * 3,
        out_shape=[jax.ShapeDtypeStruct((rows, columns // 64, 128), F32)] * 3,
        compiler_params=pltpu.CompilerParams(vmem_limit_bytes=40 << 20),
        cost_estimate=load(9),
    )(*map(lane_tiles, (gradient, weight, mean_old, square_old)))
    return [from_lane_tiles(part, weight.shape) for part in updated]


def silu_slope(values):
    sigmoid_part = jax.nn.sigmoid(values)
    return sigmoid_part * (1.0 + values * (1.0 - sigmoid_part))


def adam_update(weight, mean_old, square_old, gradient, step_rate, decay_weight):
    mean_new = BETA_ONE * mean_old + (1.0 - BETA_ONE) * gradient
    square_new = BETA_TWO * square_old + (1.0 - BETA_TWO) * gradient * gradient
    corrected_mean = mean_new / (1.0 - BETA_ONE**STEP)
    corrected_square = square_new / (1.0 - BETA_TWO**STEP)
    weight_new = weight - step_rate * (
        corrected_mean / (jnp.sqrt(corrected_square) + ADAM_EPS) + decay_weight * weight
    )
    return (mean_new, square_new, weight_new)


def shards(
    inputs,
    cotangent,
    lengths,
    norm_gain,
    norm_gain_mean,
    norm_gain_square,
    proj_zx,
    proj_zx_mean,
    proj_zx_square,
    proj_bc,
    proj_bc_mean,
    proj_bc_square,
    proj_step,
    proj_step_mean,
    proj_step_square,
    conv_inner,
    conv_inner_mean,
    conv_inner_square,
    conv_bc,
    conv_bc_mean,
    conv_bc_square,
    head_params,
    head_params_mean,
    head_params_square,
    gate_gain,
    gate_gain_mean,
    gate_gain_square,
    proj_out,
    proj_out_mean,
    proj_out_square,
):
    seq_count, local_len, model_width = inputs.shape
    local_inner = proj_zx.shape[2]
    state_width = proj_bc.shape[1] // 2
    local_heads = proj_step.shape[1]
    head_width = local_inner // local_heads
    rows = seq_count * local_len
    seq_size, seq_index = lax.axis_size("seq"), lax.axis_index("seq")

    def wide(a):
        selector = jnp.repeat(jnp.eye(local_heads, dtype=F32), head_width, axis=1)
        return jnp.einsum("...h,hc->...c", a, selector, precision=HIGHEST_PREC)

    positions = seq_index * local_len + jnp.arange(local_len)
    is_valid = (positions[None, :] < lengths[:, None]).astype(F32)
    tokens = inputs.astype(F32)
    inverse_rms = lax.rsqrt(jnp.mean(tokens * tokens, axis=-1, keepdims=True) + EPS)
    unit_tokens = tokens * inverse_rms
    normed = (unit_tokens * norm_gain).astype(BF16)
    z_weight = proj_zx[:, 0].astype(BF16)
    x_weight = proj_zx[:, 1].astype(BF16)
    bc_weight = proj_bc.astype(BF16)
    step_weight = proj_step.astype(BF16)
    out_weight = proj_out.astype(BF16)
    xbc_weight = jnp.concatenate([x_weight, bc_weight], axis=1)
    mixed_in = jnp.einsum("btd,dc->btc", normed, xbc_weight, preferred_element_type=F32).astype(BF16)
    edge_in = passed_along(mixed_in[:, local_len - CONV + 1 :], "seq", 1)
    raw_step = jnp.einsum("btd,dh->bth", normed, step_weight, preferred_element_type=F32)
    gate_input = jnp.einsum("btd,dc->btc", normed, z_weight, preferred_element_type=F32)
    padded = jnp.concatenate([edge_in, mixed_in], axis=1)
    conv_weight = jnp.concatenate([conv_inner, conv_bc], axis=-1)
    convolved = conv_weight[CONV] + jnp.zeros(mixed_in.shape, F32)
    for tap_index in range(CONV):
        convolved = (
            convolved + conv_weight[tap_index] * padded[:, tap_index : tap_index + local_len]
        )
    activated = jax.nn.silu(convolved).astype(BF16)
    x_values = activated[..., :local_inner]
    b_values = activated[..., local_inner : local_inner + state_width]
    c_values = activated[..., local_inner + state_width :]
    decay_log, step_bias, skip_gain = head_params[0], head_params[1], head_params[2]
    step_size = jax.nn.softplus(raw_step + step_bias)
    log_decay = -step_size * jnp.exp(decay_log)
    earlier = jnp.tril(jnp.ones((local_len, local_len), F32))
    running = jnp.einsum("ts,bsh->bth", earlier, log_decay, precision=HIGHEST_PREC)
    device_decay = running[:, -1]
    decay_t = log_decay.transpose(0, 2, 1)

    weighted = x_values.astype(F32) * wide(jnp.exp(device_decay[:, None] - running) * step_size)
    local_state = jnp.einsum(
        "btn,btc->bnc", b_values, weighted.astype(BF16), preferred_element_type=F32
    )
    unit_decay = wide(jnp.exp(device_decay))[:, None]
    entering, block_decays = states_before(local_state, unit_decay, "seq")

    scanned_raw, states = scan_forward(activated, step_size, log_decay, decay_t, entering)
    skip_wide = jnp.repeat(skip_gain, head_width)[None, None]
    scanned = scanned_raw + skip_wide * x_values.astype(F32)
    gate_act = jax.nn.silu(gate_input)
    gated_values = scanned * gate_act
    square_sum = jnp.sum(gated_values * gated_values, axis=-1)
    scaled = (gated_values * gate_gain).astype(BF16)
    partial_out = jnp.einsum("bti,di->btd", scaled, out_weight, preferred_element_type=F32)
    out_cotangent = cotangent.astype(F32) * is_valid[..., None]
    partial_scale_grad = jnp.sum(out_cotangent * partial_out, axis=-1)
    square_total, scale_grad = lax.psum(jnp.stack([square_sum, partial_scale_grad]), "head")
    out_scale = lax.rsqrt(square_total / INNER + EPS)
    proj_grad = (out_scale[..., None] * out_cotangent).astype(BF16)
    square_grad = -0.5 * scale_grad * out_scale * out_scale * out_scale / INNER
    out_weight_grad = jnp.einsum("btd,bti->di", proj_grad, scaled, preferred_element_type=F32)
    scaled_grad = jnp.einsum("btd,di->bti", proj_grad, out_weight, preferred_element_type=F32)
    gate_gain_grad = jnp.sum(scaled_grad * gated_values, axis=(0, 1))
    gated_grad = scaled_grad * gate_gain + 2.0 * gated_values * square_grad[..., None]
    scanned_grad = gated_grad * gate_act
    gate_grad = (gated_grad * scanned * silu_slope(gate_input)).astype(BF16)
    local_back = jnp.einsum(
        "btn,btc->bnc",
        c_values,
        (scanned_grad * wide(jnp.exp(running))).astype(BF16),
        preferred_element_type=F32,
    )
    leaving = states_after(local_back, block_decays, "seq")
    z_weight_grad = jnp.einsum("btd,btc->dc", normed, gate_grad, preferred_element_type=F32)
    early_grads = jnp.concatenate([out_weight_grad, z_weight_grad], axis=0).astype(BF16)
    early_grads, _ = lax.optimization_barrier((early_grads, leaving))
    early_parts = exchanged(to_blocks(early_grads, seq_size), "seq")
    projected = halved(partial_out.astype(BF16).reshape(rows, model_width), "head")
    scanned_grad, projected = lax.optimization_barrier((scanned_grad, projected))
    projected_far = swapped(projected, "head", axis_masks("head")[-1])
    taps = jnp.pad(conv_weight, ((0, 8 - CONV - 1), (0, 0)))
    edge_rows = jnp.pad(edge_in, ((0, 0), (16 - CONV + 1, 0), (0, 0)))
    x_raw, bc_grad, step_in_grad, x_first, x_last, x_tap_sums, head_totals = scan_backward(
        activated,
        step_size,
        log_decay,
        decay_t,
        skip_wide,
        scanned_grad,
        scanned_raw,
        states,
        leaving,
        mixed_in,
        edge_rows,
        taps,
        jax.nn.sigmoid(raw_step + step_bias),
        jnp.exp(decay_log)[None],
    )
    x_raw, early_parts, projected_far = lax.optimization_barrier(
        (x_raw, early_parts, projected_far)
    )
    projected_half, projected_other = regathered(added(projected, projected_far), "head")
    early_own = jnp.sum(early_parts.astype(F32), axis=0).astype(BF16)
    early_all = exchanged(jnp.broadcast_to(early_own[None], early_parts.shape), "seq")
    bc_sum = halved(bc_grad.reshape(rows, 2 * state_width), "head")
    bc_far = swapped(bc_sum, "head", axis_masks("head")[-1])

    x_in_grad = joined_edges(x_raw, x_first, x_last, conv_weight[:, :local_inner])
    x_in_grad, bc_far = lax.optimization_barrier((x_in_grad, bc_far))
    bc_half, bc_other = regathered(added(bc_sum, bc_far), "head")
    normed_partial = normed_products(
        gate_grad.reshape(rows, local_inner),
        x_in_grad.reshape(rows, local_inner),
        step_in_grad.reshape(rows, local_heads),
        z_weight,
        x_weight,
        step_weight,
    )
    x_weight_grad = jnp.einsum("btd,btc->dc", normed, x_in_grad, preferred_element_type=F32)
    x_parts = exchanged(to_blocks(x_weight_grad, seq_size), "seq")
    normed_sum = halved(normed_partial, "head")
    normed_far = swapped(normed_sum, "head", axis_masks("head")[-1])

    scalars = jnp.concatenate(
        [lengths, jnp.stack([seq_index * local_len, near_bit("head", 1)]).astype(jnp.int32)]
    )
    bc_half, early_all, _ = lax.optimization_barrier((bc_half, early_all, normed_sum))
    early_sums = early_all.reshape(2, model_width, local_inner)
    bc_raw_grad, bc_first, bc_last, bc_tap_sums = bc_backward(
        scalars,
        bc_half,
        bc_other,
        mixed_in[..., local_inner:],
        edge_rows[..., local_inner:],
        taps[:, local_inner:],
    )
    bc_in_grad = joined_edges(bc_raw_grad, bc_first, bc_last, conv_weight[:, local_inner:])
    bc_in_grad, x_parts = lax.optimization_barrier((bc_in_grad, x_parts))
    x_own = jnp.sum(x_parts.astype(F32), axis=0).astype(BF16)
    x_all = exchanged(jnp.broadcast_to(x_own[None], x_parts.shape), "seq")
    x_sum = x_all.reshape(model_width, local_inner)
    bc_weight_grad = jnp.einsum("btd,btc->dc", normed, bc_in_grad, preferred_element_type=F32)
    bc_blocks = to_blocks(bc_weight_grad, seq_size)
    bc_parts = exchanged(bc_blocks, "seq")
    flat_tokens = inputs.reshape(rows, model_width)
    block_out = merge_call(
        out_kernel,
        scalars,
        projected_half,
        projected_other,
        (flat_tokens, out_scale.reshape(rows, 1)),
        [row_block(model_width), row_block(1)],
        row_block(model_width),
        jax.ShapeDtypeStruct((rows, model_width), BF16),
    )
    out_updated = adam_update(
        proj_out,
        proj_out_mean,
        proj_out_square,
        early_sums[0].astype(F32),
        LEARNING_RATES[-1],
        WEIGHT_DECAYS[-1],
    )
    normed_far, block_out, out_updated, _ = lax.optimization_barrier(
        (normed_far, block_out, out_updated, bc_blocks)
    )
    block_out = block_out.reshape(inputs.shape)
    normed_half, normed_other = regathered(added(normed_sum, normed_far), "head")
    input_grad, norm_gain_grad = merge_call(
        functools.partial(tail_kernel, local_len),
        scalars,
        normed_half,
        normed_other,
        (
            bc_in_grad.reshape(rows, 2 * state_width),
            bc_weight,
            flat_tokens,
            cotangent.reshape(rows, model_width),
            norm_gain[None],
        ),
        [
            row_block(2 * state_width),
            whole_block(bc_weight.shape),
            row_block(model_width),
            row_block(model_width),
            whole_block((1, model_width)),
        ],
        [row_block(model_width), whole_block((1, model_width))],
        [
            jax.ShapeDtypeStruct((rows, model_width), F32),
            jax.ShapeDtypeStruct((1, model_width), F32),
        ],
    )
    input_grad = input_grad.reshape(inputs.shape)
    bc_own = jnp.sum(bc_parts.astype(F32), axis=0).astype(BF16)
    bc_all = exchanged(jnp.broadcast_to(bc_own[None], bc_parts.shape), "seq")
    step_weight_grad = jnp.einsum("btd,bth->hd", normed, step_in_grad, preferred_element_type=F32)
    conv_inner_grad = x_tap_sums[: CONV + 1]
    conv_bc_grad = bc_tap_sums[: CONV + 1]
    head_grad = head_totals[:3]
    small_grads = (
        norm_gain_grad[0],
        step_weight_grad,
        conv_inner_grad,
        conv_bc_grad,
        head_grad,
        gate_gain_grad,
    )
    flat = jnp.concatenate([part.reshape(-1) for part in small_grads])
    count = flat.shape[0]
    flat = jnp.pad(flat, (0, -count % 1024)).reshape(-1, 128)
    flat = doubling_sum(flat, "seq").reshape(-1)
    small_sums, at = [], 0
    for part in small_grads:
        small_sums.append(flat[at : at + part.size].reshape(part.shape))
        at += part.size

    summed_grads = (
        small_sums[0],
        jnp.stack([early_sums[1], x_sum], axis=1),
        bc_all.reshape(bc_weight_grad.shape).astype(F32),
        small_sums[1].T,
        small_sums[2],
        small_sums[3],
        small_sums[4],
        small_sums[5],
        None,
    )
    params = (
        norm_gain,
        proj_zx,
        proj_bc,
        proj_step,
        conv_inner,
        conv_bc,
        head_params,
        gate_gain,
        proj_out,
    )
    means = (
        norm_gain_mean,
        proj_zx_mean,
        proj_bc_mean,
        proj_step_mean,
        conv_inner_mean,
        conv_bc_mean,
        head_params_mean,
        gate_gain_mean,
        proj_out_mean,
    )
    squares = (
        norm_gain_square,
        proj_zx_square,
        proj_bc_square,
        proj_step_square,
        conv_inner_square,
        conv_bc_square,
        head_params_square,
        gate_gain_square,
        proj_out_square,
    )
    results = [block_out, input_grad]
    for weight, mean_old, square_old, gradient, step_rate, decay_weight in zip(
        params, means, squares, summed_grads, LEARNING_RATES, WEIGHT_DECAYS
    ):
        if gradient is None:
            updated = out_updated
        elif weight.ndim == 3:
            updated = adam_tiles(weight, mean_old, square_old, gradient, step_rate, decay_weight)
        else:
            updated = adam_update(weight, mean_old, square_old, gradient, step_rate, decay_weight)
        results.extend(updated)
    return tuple(results)


def solution(mesh):
    in_specs = (
        P(None, "seq", None),
        P(None, "seq", None),
        P(),
        P(),
        P(),
        P(),
        P(None, None, "head"),
        P(None, None, "head"),
        P(None, None, "head"),
        P(),
        P(),
        P(),
        P(None, "head"),
        P(None, "head"),
        P(None, "head"),
        P(None, "head"),
        P(None, "head"),
        P(None, "head"),
        P(),
        P(),
        P(),
        P(None, "head"),
        P(None, "head"),
        P(None, "head"),
        P("head"),
        P("head"),
        P("head"),
        P(None, "head"),
        P(None, "head"),
        P(None, "head"),
    )
    out_specs = (
        P(None, "seq", None),
        P(None, "seq", None),
        P(),
        P(),
        P(),
        P(None, None, "head"),
        P(None, None, "head"),
        P(None, None, "head"),
        P(),
        P(),
        P(),
        P(None, "head"),
        P(None, "head"),
        P(None, "head"),
        P(None, "head"),
        P(None, "head"),
        P(None, "head"),
        P(),
        P(),
        P(),
        P(None, "head"),
        P(None, "head"),
        P(None, "head"),
        P("head"),
        P("head"),
        P("head"),
        P(None, "head"),
        P(None, "head"),
        P(None, "head"),
    )
    return jax.shard_map(shards, mesh=mesh, in_specs=in_specs, out_specs=out_specs, check_vma=False)
```

```python
import functools

import jax
import jax.numpy as jnp
from jax import lax
from jax.experimental import pallas as pl
from jax.experimental.pallas import tpu as pltpu
from jax.sharding import PartitionSpec as P

INNER = 2048
CONV = 4
CHUNK = 128
STEP = 7


EPS = 1e-05
BETA_ONE = 0.9
BETA_TWO = 0.95
ADAM_EPS = 1e-08
LEARNING_RATES = (0.6, 0.09, 0.09, 0.09, 0.9, 0.9, 0.9, 0.6, 0.06)
WEIGHT_DECAYS = (0.0, 0.1, 0.1, 0.1, 0.0, 0.0, 0.0, 0.0, 0.1)
HIGHEST_PREC = lax.Precision.HIGHEST
F32 = jnp.float32
BF16 = jnp.bfloat16


def passed_along(block, axis, distance):
    devices = range(lax.axis_size(axis))
    route = [(i - distance, i) for i in devices if i - distance in devices]
    return lax.ppermute(block, axis, route)


def swapped(block, axis, mask):
    return lax.ppermute(block, axis, [(i, i ^ mask) for i in range(lax.axis_size(axis))])


def doubling_sum(part, axis):
    for k in range(lax.axis_size(axis).bit_length() - 1):
        part = part + swapped(part, axis, 1 << k)
    return part


def axis_masks(axis):
    return [1 << k for k in range(lax.axis_size(axis).bit_length() - 1)]


def near_bit(axis, mask):
    return (lax.axis_index(axis) // mask) % 2


def added(a, b):
    return (a.astype(F32) + b.astype(F32)).astype(BF16)


def halved(part, axis):
    for mask in axis_masks(axis)[:-1]:
        bit = near_bit(axis, mask)
        halves = part.reshape((2, part.shape[0] // 2) + part.shape[1:])
        sent = lax.dynamic_index_in_dim(halves, 1 - bit, 0, keepdims=False)
        kept = lax.dynamic_index_in_dim(halves, bit, 0, keepdims=False)
        part = added(kept, swapped(sent, axis, mask))
    return part


def joined(part, got, bit):
    first = jnp.where(bit == 0, part, got)
    second = jnp.where(bit == 0, got, part)
    return jnp.concatenate([first, second], axis=0)


def regathered(part, axis):
    masks = axis_masks(axis)[:-1]
    for mask in reversed(masks[1:]):
        part = joined(part, swapped(part, axis, mask), near_bit(axis, mask))
    return part, swapped(part, axis, masks[0])


def halving_sum(part, axis):
    part = halved(part, axis)
    part = added(part, swapped(part, axis, axis_masks(axis)[-1]))
    part, other = regathered(part, axis)
    return joined(part, other, near_bit(axis, 1))


def exchanged(blocks, axis):
    return lax.all_to_all(blocks, axis, 0, 0, tiled=True)


def to_blocks(state, count):
    return state.astype(BF16).reshape(count, -1, state.shape[-1])


def states_before(packed, height, axis):
    size = lax.axis_size(axis)
    got = exchanged(packed, axis).astype(F32)
    decays = got[:, height : height + 1] + got[:, height + 1 : height + 2]
    entering = [jnp.zeros(got[0, :height].shape, F32)]
    for k in range(size - 1):
        entering.append(decays[k] * entering[-1] + got[k, :height])
    return exchanged(jnp.stack(entering).astype(BF16), axis), decays


def states_after(state, decays, axis):
    size = lax.axis_size(axis)
    got = exchanged(to_blocks(state, size), axis).astype(F32)
    leaving = [jnp.zeros(got[0].shape, F32)]
    for k in range(size - 1, 0, -1):
        leaving.append(decays[k] * leaving[-1] + got[k])
    return exchanged(jnp.stack(leaving[::-1]).astype(BF16), axis)


def lane_tiles(a):
    rows, two, columns = a.shape
    return a.reshape(rows, two, columns // 128, 128).transpose(0, 2, 1, 3).reshape(rows, -1, 128)


def from_lane_tiles(a, shape):
    rows, two, columns = shape
    return a.reshape(rows, columns // 128, two, 128).transpose(0, 2, 1, 3).reshape(shape)


def dot(a, b, dims=((1,), (0,)), precision=None):
    return lax.dot_general(a, b, (dims, ((), ())), precision=precision, preferred_element_type=F32)


def expander(heads, width):
    row = lax.broadcasted_iota(jnp.int32, (heads, heads * width), 0)
    column = lax.broadcasted_iota(jnp.int32, (heads, heads * width), 1)
    inside = (column >= row * width) & (column < (row + 1) * width)
    return jnp.where(inside, 1.0, 0.0).astype(BF16)


def split_dot(a, b, dims):
    high = a.astype(BF16)
    low = (a - high.astype(F32)).astype(BF16)
    return dot(high, b, dims) + dot(low, b, dims)


def spread(a, expand):
    return split_dot(a, expand, ((1,), (0,)))


def head_sums(a, expand):
    return split_dot(a, expand, ((1,), (1,)))


def pair_rows(a):
    lane = lax.broadcasted_iota(jnp.int32, a.shape, 1)
    first = lane < a.shape[1] // 2
    zero = jnp.zeros_like(a)
    return jnp.concatenate([jnp.where(first, a, zero), jnp.where(first, zero, a)], axis=0)


def chunk_decays(decay):
    q = decay.shape[0]
    row = lax.broadcasted_iota(jnp.int32, (q, q), 0)
    column = lax.broadcasted_iota(jnp.int32, (q, q), 1)
    lower = jnp.where(row >= column, 1.0, 0.0).astype(F32)
    cum = dot(lower, decay, precision=HIGHEST_PREC)
    cum_t = dot(decay, lower, ((0,), (1,)), precision=HIGHEST_PREC)
    return cum, cum_t, row, column


def scan_kernel(x_ref, b_ref, c_ref, step_ref, decay_ref, enter_ref, y_ref, in_ref, state):
    heads = step_ref.shape[2]
    width = x_ref.shape[2] // heads

    @pl.when(pl.program_id(1) == 0)
    def _():
        state[...] = enter_ref[0].astype(F32)

    expand = expander(heads, width)
    cum, cum_t, row, column = chunk_decays(decay_ref[0])
    causal = row >= column
    q = cum.shape[0]
    total = cum[q - 1 : q, :]
    b, c = b_ref[0], c_ref[0]
    x = x_ref[0].astype(F32)
    step = step_ref[0]
    xs = (x * spread(step, expand)).astype(BF16)
    grown = spread(jnp.exp(cum), expand)
    xw = (x * spread(step * jnp.exp(total - cum), expand)).astype(BF16)
    scores = dot(c, b, ((1,), (1,)))
    before = state[...]
    in_ref[0, 0] = before
    from_state = grown * dot(c, before.astype(BF16))
    for pair in range(heads // 2):
        lanes = slice(pair * 2 * width, (pair + 1) * 2 * width)
        mixing = []
        for h in (2 * pair, 2 * pair + 1):
            between = cum[:, h : h + 1] - cum_t[h : h + 1, :]
            mixing.append((jnp.exp(jnp.where(causal, between, -1e30)) * scores).astype(BF16))
        within = dot(jnp.concatenate(mixing, axis=1), pair_rows(xs[:, lanes]))
        y_ref[0, :, lanes] = within + from_state[:, lanes]
    state[...] = grown[q - 1 : q, :] * before + dot(b, xw, ((0,), (0,)))


def conv_back_step(act_grad, mixed, previous, taps, after_ref):
    q = mixed.shape[0]
    shifted = conv_windows(mixed, previous)
    convolved = taps[CONV : CONV + 1]
    for k in range(CONV):
        convolved = convolved + taps[k : k + 1] * shifted[k]
    conv_grad = act_grad * silu_slope(convolved)
    extended = jnp.concatenate([conv_grad, after_ref[...]], axis=0)
    mixed_grad = taps[CONV - 1 : CONV] * conv_grad
    for k in range(CONV - 1):
        mixed_grad = mixed_grad + taps[k : k + 1] * extended[CONV - 1 - k : CONV - 1 - k + q]
    sums = [jnp.sum(conv_grad * part, axis=0, keepdims=True) for part in shifted]
    sums.append(jnp.sum(conv_grad, axis=0, keepdims=True))
    sums.append(jnp.zeros((8 - CONV - 1, mixed.shape[1]), F32))
    after_ref[...] = conv_grad[:8]
    return conv_grad, mixed_grad, jnp.concatenate(sums, axis=0)


def rows_before(edge_ref, previous_ref):
    first = pl.program_id(1) == pl.num_programs(1) - 1
    return jnp.where(first, edge_ref[0].astype(F32), previous_ref[0].astype(F32))[8:]


def back_kernel(
    x_ref, b_ref, c_ref, step_ref, decay_ref, skip_ref, dy_ref, y_ref, in_ref, leave_ref,
    mixed_ref, previous_ref, edge_ref, taps_ref, slope_ref, rate_ref,
    mixed_grad_ref, dbc_ref, pre_ref, first_ref, last_ref, tap_sums_ref, head_sums_ref,
    grad, after
):
    start = (pl.program_id(0) == 0) & (pl.program_id(1) == 0)

    @pl.when(start)
    def _():
        tap_sums_ref[...] = jnp.zeros_like(tap_sums_ref)
        head_sums_ref[...] = jnp.zeros_like(head_sums_ref)

    @pl.when(pl.program_id(1) == 0)
    def _():
        after[...] = jnp.zeros_like(after)

    heads = step_ref.shape[2]
    width = x_ref.shape[2] // heads

    @pl.when(pl.program_id(1) == 0)
    def _():
        grad[...] = leave_ref[0].astype(F32)

    expand = expander(heads, width)
    cum, cum_t, row, column = chunk_decays(decay_ref[0])
    later = column >= row
    q = cum.shape[0]
    total = cum[q - 1 : q, :]
    b, c = b_ref[0], c_ref[0]
    x = x_ref[0].astype(F32)
    step = step_ref[0]
    step_wide = spread(step, expand)
    xs = (x * step_wide).astype(BF16)
    grown = spread(jnp.exp(cum), expand)
    waned = spread(jnp.exp(total - cum), expand)
    xw = (x * step_wide * waned).astype(BF16)
    dy = dy_ref[0]
    dy_low = dy.astype(BF16)
    edy = (dy * grown).astype(BF16)
    before = in_ref[0, 0]
    after_grad = grad[...]
    after_low = after_grad.astype(BF16)
    scores_t = dot(b, c, ((1,), (1,)))
    v_state = waned * dot(b, after_low)
    dscores_t = jnp.zeros((q, q), F32)
    v_parts = []
    for pair in range(heads // 2):
        lanes = slice(pair * 2 * width, (pair + 1) * 2 * width)
        dy_pair = pair_rows(dy_low[:, lanes])
        xs_pair = pair_rows(xs[:, lanes])
        dmix = dot(xs_pair, dy_low[:, lanes], ((1,), (1,)))
        mixing = []
        for k, h in enumerate((2 * pair, 2 * pair + 1)):
            between = cum_t[h : h + 1, :] - cum[:, h : h + 1]
            fade = jnp.exp(jnp.where(later, between, -1e30))
            mixing.append((fade * scores_t).astype(BF16))
            dscores_t = dscores_t + fade * dmix[k * q : (k + 1) * q]
        v_parts.append(dot(jnp.concatenate(mixing, axis=1), dy_pair))
    v = jnp.concatenate(v_parts, axis=1) + v_state
    xs_wide = xs.astype(F32)
    etotal = grown[q - 1 : q, :]
    dx = step_wide * v + skip_ref[0] * dy
    conv_grad, mixed_grad, tap_sums = conv_back_step(
        dx, mixed_ref[0].astype(F32), rows_before(edge_ref, previous_ref), taps_ref[...], after
    )
    mixed_grad_ref[0] = mixed_grad.astype(BF16)
    first_ref[0] = conv_grad[:8]

    @pl.when(pl.program_id(1) == 0)
    def _():
        last_ref[0] = mixed_grad[q - 8 :]

    tap_sums_ref[...] += tap_sums
    end_row = jnp.sum(xs_wide * v_state, axis=0, keepdims=True) + jnp.sum(
        etotal * before * after_grad, axis=0, keepdims=True
    )
    crossing = dy_low.astype(F32) * y_ref[0] - xs_wide * v
    last = lax.broadcasted_iota(jnp.int32, crossing.shape, 0) == q - 1
    crossing = crossing + jnp.where(last, end_row, 0.0)
    upper = jnp.where(column >= row, 1.0, 0.0).astype(F32)
    decay_grad = dot(upper, head_sums(crossing, expand), precision=HIGHEST_PREC)
    pre_grad = (head_sums(x * v, expand) - rate_ref[...] * decay_grad) * slope_ref[0]
    pre_ref[0] = pre_grad.astype(BF16)
    sums = [
        jnp.sum(decay_grad * decay_ref[0], axis=0, keepdims=True),
        jnp.sum(pre_grad, axis=0, keepdims=True),
        jnp.sum(head_sums(x * dy, expand), axis=0, keepdims=True),
        jnp.zeros((5, heads), F32),
    ]
    head_sums_ref[...] += jnp.concatenate(sums, axis=0)
    dscores_low = dscores_t.astype(BF16)
    state = b.shape[1]
    dbc_ref[0, :, :state] = (
        dot(dscores_low, c) + dot(xw, after_low, ((1,), (1,)))
    ).astype(BF16)
    dbc_ref[0, :, state:] = (
        dot(dscores_low, b, ((0,), (0,))) + dot(edy, before.astype(BF16), ((1,), (1,)))
    ).astype(BF16)
    grad[...] = etotal * after_grad + dot(c, edy, ((0,), (0,)))


def act_blocks(inner, state, place):
    def part(lanes, at):
        return pl.BlockSpec((1, CHUNK, lanes), lambda s, k: (s, place(k), at))

    return [part(inner, 0), part(state, inner // state), part(state, inner // state + 1)]


def conv_windows(mixed, previous):
    q = mixed.shape[0]
    window = jnp.concatenate([previous, mixed], axis=0)
    return [window[8 - CONV + 1 + k : 8 - CONV + 1 + k + q] for k in range(CONV)]


def first_kernel(
    mixed_ref, previous_ref, edge_ref, taps_ref, step_ref, decay_ref, act_ref, packed_ref, state, total
):
    chunk = pl.program_id(1)

    @pl.when(chunk == 0)
    def _():
        state[...] = jnp.zeros_like(state)
        total[...] = jnp.zeros_like(total)

    previous = jnp.where(
        chunk == 0, edge_ref[0].astype(F32), previous_ref[0].astype(F32)
    )[8:]
    convolved = taps_ref[CONV : CONV + 1]
    for k, part in enumerate(conv_windows(mixed_ref[0].astype(F32), previous)):
        convolved = convolved + taps_ref[k : k + 1] * part
    activated = jax.nn.silu(convolved).astype(BF16)
    act_ref[0] = activated
    heads, (state_width, inner) = step_ref.shape[2], state.shape
    expand = expander(heads, inner // heads)
    cum = chunk_decays(decay_ref[0])[0]
    q = cum.shape[0]
    last = cum[q - 1 : q, :]
    weights = spread(step_ref[0] * jnp.exp(last - cum), expand)
    xw = (activated[:, :inner].astype(F32) * weights).astype(BF16)
    b = activated[:, inner : inner + state_width]
    kept = spread(jnp.exp(cum), expand)[q - 1 : q]
    state[...] = kept * state[...] + dot(b, xw, ((0,), (0,)))
    total[...] = total[...] + last

    @pl.when(chunk == pl.num_programs(1) - 1)
    def _():
        decay = spread(jnp.exp(jnp.broadcast_to(total[...], (8, heads))), expand)[:1]
        high = decay.astype(BF16).astype(F32)
        tail = jnp.concatenate([high, decay - high, jnp.zeros((14, inner), F32)], axis=0)
        height = packed_ref.shape[2] - 16
        for part in range(packed_ref.shape[1]):
            rows = state[part * height : (part + 1) * height]
            packed_ref[0, part] = jnp.concatenate([rows, tail], axis=0).astype(BF16)


def conv_forward(mixed, edge, taps, step, decay, state, parts):
    seqs, length, lanes = mixed.shape
    heads, inner = step.shape[2], lanes - 2 * state
    chunks, tall = length // CHUNK, CHUNK // 16
    height = state // parts + 16

    def block(width):
        return pl.BlockSpec((1, CHUNK, width), lambda s, k: (s, k, 0))

    return pl.pallas_call(
        first_kernel,
        grid=(seqs, chunks),
        in_specs=[
            block(lanes),
            pl.BlockSpec((1, 16, lanes), lambda s, k: (s, jnp.maximum(k * tall - 1, 0), 0)),
            pl.BlockSpec((1, 16, lanes), lambda s, k: (s, 0, 0)),
            pl.BlockSpec((8, lanes), lambda s, k: (0, 0)),
            block(heads),
            block(heads),
        ],
        out_specs=[
            block(lanes),
            pl.BlockSpec((1, parts, height, inner), lambda s, k: (s, 0, 0, 0)),
        ],
        out_shape=[
            jax.ShapeDtypeStruct(mixed.shape, BF16),
            jax.ShapeDtypeStruct((seqs, parts, height, inner), BF16),
        ],
        scratch_shapes=[pltpu.VMEM((state, inner), F32), pltpu.VMEM((1, heads), F32)],
        compiler_params=pltpu.CompilerParams(vmem_limit_bytes=40 << 20),
        cost_estimate=load(9),
    )(mixed, mixed, edge, taps, step, decay)


def scan_forward(activated, step, decay, enter):
    seqs, length, heads = step.shape
    state, inner = enter.shape[1:]
    chunks = length // CHUNK

    def block(lanes):
        return pl.BlockSpec((1, CHUNK, lanes), lambda s, k: (s, k, 0))

    return pl.pallas_call(
        scan_kernel,
        grid=(seqs, chunks),
        in_specs=act_blocks(inner, state, lambda k: k)
        + [
            block(heads),
            block(heads),
            pl.BlockSpec((1, state, inner), lambda s, k: (s, 0, 0)),
        ],
        out_specs=[
            block(inner),
            pl.BlockSpec((1, 1, state, inner), lambda s, k: (s, k, 0, 0)),
        ],
        out_shape=[
            jax.ShapeDtypeStruct((seqs, length, inner), F32),
            jax.ShapeDtypeStruct((seqs, chunks, state, inner), F32),
        ],
        scratch_shapes=[pltpu.VMEM((state, inner), F32)],
        compiler_params=pltpu.CompilerParams(vmem_limit_bytes=40 << 20),
        cost_estimate=load(13),
    )(activated, activated, activated, step, decay, enter)


def conv_blocks(chunks, lanes, at):
    tall = CHUNK // 16
    return [
        pl.BlockSpec((1, CHUNK, lanes), lambda s, k, *_: (s, chunks - 1 - k, at)),
        pl.BlockSpec(
            (1, 16, lanes), lambda s, k, *_: (s, jnp.maximum((chunks - 1 - k) * tall - 1, 0), at)
        ),
        pl.BlockSpec((1, 16, lanes), lambda s, k, *_: (s, 0, at)),
        pl.BlockSpec((8, lanes), lambda s, k, *_: (0, at)),
    ]


def conv_outs(seqs, chunks, lanes):
    specs = [
        pl.BlockSpec((1, CHUNK, lanes), lambda s, k, *_: (s, chunks - 1 - k, 0)),
        pl.BlockSpec((1, 8, lanes), lambda s, k, *_: (s, 0, 0)),
        pl.BlockSpec((1, 8, lanes), lambda s, k, *_: (s, 0, 0)),
        pl.BlockSpec((8, lanes), lambda s, k, *_: (0, 0)),
    ]
    shapes = [
        jax.ShapeDtypeStruct((seqs, chunks * CHUNK, lanes), BF16),
        jax.ShapeDtypeStruct((seqs, 8, lanes), F32),
        jax.ShapeDtypeStruct((seqs, 8, lanes), F32),
        jax.ShapeDtypeStruct((8, lanes), F32),
    ]
    return specs, shapes


def scan_backward(
    activated, step, decay, skip, dy, y, states, leave, mixed, edge, taps, slope, rate
):
    seqs, length, heads = step.shape
    state, inner = leave.shape[1:]
    chunks = length // CHUNK

    def block(lanes):
        return pl.BlockSpec((1, CHUNK, lanes), lambda s, k: (s, chunks - 1 - k, 0))

    conv_specs, conv_shapes = conv_outs(seqs, chunks, inner)
    return pl.pallas_call(
        back_kernel,
        grid=(seqs, chunks),
        in_specs=act_blocks(inner, state, lambda k: chunks - 1 - k)
        + [
            block(heads),
            block(heads),
            pl.BlockSpec((1, 1, inner), lambda s, k: (0, 0, 0)),
            block(inner),
            block(inner),
            pl.BlockSpec((1, 1, state, inner), lambda s, k: (s, chunks - 1 - k, 0, 0)),
            pl.BlockSpec((1, state, inner), lambda s, k: (s, 0, 0)),
        ]
        + conv_blocks(chunks, inner, 0)
        + [block(heads), pl.BlockSpec((1, heads), lambda s, k: (0, 0))],
        out_specs=[conv_specs[0], block(2 * state), block(heads)]
        + conv_specs[1:]
        + [pl.BlockSpec((8, heads), lambda s, k: (0, 0))],
        out_shape=[
            conv_shapes[0],
            jax.ShapeDtypeStruct((seqs, length, 2 * state), BF16),
            jax.ShapeDtypeStruct((seqs, length, heads), BF16),
        ]
        + conv_shapes[1:]
        + [jax.ShapeDtypeStruct((8, heads), F32)],
        scratch_shapes=[pltpu.VMEM((state, inner), F32), pltpu.VMEM((8, inner), F32)],
        compiler_params=pltpu.CompilerParams(vmem_limit_bytes=40 << 20),
        cost_estimate=load(30),
    )(
        activated, activated, activated, step, decay, skip, dy, y, states, leave,
        mixed, mixed, edge, taps, slope, rate
    )


def bc_kernel(
    scalars_ref, part_ref, got_ref, mixed_ref, previous_ref, edge_ref, taps_ref,
    mixed_grad_ref, first_ref, last_ref, tap_sums_ref, after
):
    start = (pl.program_id(0) == 0) & (pl.program_id(1) == 0)

    @pl.when(start)
    def _():
        tap_sums_ref[...] = jnp.zeros_like(tap_sums_ref)

    @pl.when(pl.program_id(1) == 0)
    def _():
        after[...] = jnp.zeros_like(after)

    q = mixed_ref.shape[1]
    act_grad = picked(scalars_ref, part_ref, got_ref)[0]
    conv_grad, mixed_grad, tap_sums = conv_back_step(
        act_grad, mixed_ref[0].astype(F32), rows_before(edge_ref, previous_ref), taps_ref[...], after
    )
    mixed_grad_ref[0] = mixed_grad.astype(BF16)
    first_ref[0] = conv_grad[:8]

    @pl.when(pl.program_id(1) == 0)
    def _():
        last_ref[0] = mixed_grad[q - 8 :]

    tap_sums_ref[...] += tap_sums


def bc_backward(scalars, part, got, mixed, edge, taps):
    seqs, length, lanes = mixed.shape
    chunks = length // CHUNK
    half = pl.BlockSpec((1, CHUNK, lanes), lambda s, k, _: (s % (seqs // 2), chunks - 1 - k, 0))
    conv_specs, conv_shapes = conv_outs(seqs, chunks, lanes)
    return pl.pallas_call(
        bc_kernel,
        grid_spec=pltpu.PrefetchScalarGridSpec(
            num_scalar_prefetch=1,
            grid=(seqs, chunks),
            in_specs=[half, half] + conv_blocks(chunks, lanes, 0),
            out_specs=conv_specs,
            scratch_shapes=[pltpu.VMEM((8, lanes), F32)],
        ),
        out_shape=conv_shapes,
        compiler_params=pltpu.CompilerParams(vmem_limit_bytes=40 << 20),
        cost_estimate=load(5),
    )(
        scalars,
        part.reshape(seqs // 2, length, lanes),
        got.reshape(seqs // 2, length, lanes),
        mixed,
        mixed,
        edge,
        taps,
    )


def joined_edges(mixed_grad, first, last, taps):
    rows = []
    for j in range(CONV - 1):
        rows.append(sum(taps[k] * first[:, j - k] for k in range(j + 1)))
    edge_grad = passed_along(jnp.stack(rows, axis=1), "seq", -1)
    fixed = last + jnp.pad(edge_grad, ((0, 0), (8 - CONV + 1, 0), (0, 0)))
    return lax.dynamic_update_slice(mixed_grad, fixed.astype(BF16), (0, mixed_grad.shape[1] - 8, 0))


def normed_kernel(gate_ref, x_ref, step_ref, z_weight_ref, x_weight_ref, step_weight_ref, out_ref):
    nt = ((1,), (1,))
    total = dot(gate_ref[...], z_weight_ref[...], nt) + dot(x_ref[...], x_weight_ref[...], nt)
    out_ref[...] = (total + dot(step_ref[...], step_weight_ref[...], nt)).astype(BF16)


def normed_products(gate_grad, x_grad, step_grad, z_weight, x_weight, step_weight):
    rows, width = gate_grad.shape[0], z_weight.shape[0]

    def block(a):
        return pl.BlockSpec((ROWS, a.shape[1]), lambda i: (i, 0))

    def whole(a):
        return pl.BlockSpec(a.shape, lambda i: (0, 0))

    args = (gate_grad, x_grad, step_grad, z_weight, x_weight, step_weight)
    return pl.pallas_call(
        normed_kernel,
        grid=(rows // ROWS,),
        in_specs=[block(a) for a in args[:3]] + [whole(a) for a in args[3:]],
        out_specs=pl.BlockSpec((ROWS, width), lambda i: (i, 0)),
        out_shape=jax.ShapeDtypeStruct((rows, width), BF16),
        compiler_params=pltpu.CompilerParams(vmem_limit_bytes=40 << 20),
        cost_estimate=load(6),
    )(*args)


def picked(scalars_ref, part_ref, got_ref):
    bit = scalars_ref[scalars_ref.shape[0] - 1]
    half = pl.num_programs(0) // 2
    own = (pl.program_id(0) // half) == bit
    return jnp.where(own, part_ref[...].astype(F32), got_ref[...].astype(F32))


def out_kernel(scalars_ref, part_ref, got_ref, tokens_ref, scale_ref, out_ref):
    projected = picked(scalars_ref, part_ref, got_ref)
    out_ref[...] = (tokens_ref[...].astype(F32) + scale_ref[...] * projected).astype(BF16)


def tail_kernel(
    local_len, scalars_ref, part_ref, got_ref, bc_ref, weight_ref, tokens_ref, back_ref, gain_ref,
    out_ref, gain_grad_ref
):
    step = pl.program_id(0)
    height = tokens_ref.shape[0]
    normed_grad = picked(scalars_ref, part_ref, got_ref) + dot(
        bc_ref[...], weight_ref[...], ((1,), (1,))
    )
    tokens = tokens_ref[...].astype(F32)
    inverse_rms = lax.rsqrt(jnp.mean(tokens * tokens, axis=-1, keepdims=True) + EPS)
    unit = tokens * inverse_rms

    @pl.when(step == 0)
    def _():
        gain_grad_ref[...] = jnp.zeros_like(gain_grad_ref)

    gain_grad_ref[...] += jnp.sum(normed_grad * unit, axis=0, keepdims=True)
    unit_grad = normed_grad * gain_ref[...]
    along = jnp.mean(unit_grad * unit, axis=-1, keepdims=True)
    row = step * height
    length = scalars_ref[row // local_len]
    start = scalars_ref[scalars_ref.shape[0] - 2] + row % local_len
    position = start + lax.broadcasted_iota(jnp.int32, tokens.shape, 0)
    back = jnp.where(position < length, back_ref[...].astype(F32), 0.0)
    out_ref[...] = back + inverse_rms * (unit_grad - unit * along)


ROWS = 256


def load(microseconds):
    return pl.CostEstimate(flops=0, transcendentals=0, bytes_accessed=int(microseconds * 3.69e6))


def merge_call(kernel, scalars, part, got, others, other_specs, out_specs, out_shape):
    rows, width = 2 * part.shape[0], part.shape[1]
    blocks = rows // ROWS
    half = pl.BlockSpec((ROWS, width), lambda i, s: (i % (blocks // 2), 0))
    return pl.pallas_call(
        kernel,
        grid_spec=pltpu.PrefetchScalarGridSpec(
            num_scalar_prefetch=1,
            grid=(blocks,),
            in_specs=[half, half] + other_specs,
            out_specs=out_specs,
        ),
        out_shape=out_shape,
        compiler_params=pltpu.CompilerParams(vmem_limit_bytes=40 << 20),
        cost_estimate=load(8),
    )(scalars, part, got, *others)


def row_block(lanes):
    return pl.BlockSpec((ROWS, lanes), lambda i, s: (i, 0))


def whole_block(shape):
    return pl.BlockSpec(shape, lambda i, s: (0, 0))


def adam_kernel(
    step_rate, decay_weight, gradient_ref, weight_ref, mean_ref, square_ref,
    mean_out, square_out, weight_out
):
    mean_out[...], square_out[...], weight_out[...] = adam_update(
        weight_ref[...],
        mean_ref[...],
        square_ref[...],
        gradient_ref[...].astype(F32),
        step_rate,
        decay_weight,
    )


def adam_tiles(weight, mean_old, square_old, gradient, step_rate, decay_weight):
    rows, _, columns = weight.shape
    tiles = pl.BlockSpec((128, columns // 64, 128), lambda i: (i, 0, 0))
    updated = pl.pallas_call(
        functools.partial(adam_kernel, step_rate, decay_weight),
        grid=(rows // 128,),
        in_specs=[tiles] * 4,
        out_specs=[tiles] * 3,
        out_shape=[jax.ShapeDtypeStruct((rows, columns // 64, 128), F32)] * 3,
        compiler_params=pltpu.CompilerParams(vmem_limit_bytes=40 << 20),
        cost_estimate=load(9),
    )(*map(lane_tiles, (gradient, weight, mean_old, square_old)))
    return [from_lane_tiles(part, weight.shape) for part in updated]


def silu_slope(values):
    sigmoid_part = jax.nn.sigmoid(values)
    return sigmoid_part * (1.0 + values * (1.0 - sigmoid_part))


def adam_update(weight, mean_old, square_old, gradient, step_rate, decay_weight):
    mean_new = BETA_ONE * mean_old + (1.0 - BETA_ONE) * gradient
    square_new = BETA_TWO * square_old + (1.0 - BETA_TWO) * gradient * gradient
    corrected_mean = mean_new / (1.0 - BETA_ONE**STEP)
    corrected_square = square_new / (1.0 - BETA_TWO**STEP)
    weight_new = weight - step_rate * (
        corrected_mean / (jnp.sqrt(corrected_square) + ADAM_EPS) + decay_weight * weight
    )
    return (mean_new, square_new, weight_new)


def shards(
    inputs,
    cotangent,
    lengths,
    norm_gain,
    norm_gain_mean,
    norm_gain_square,
    proj_zx,
    proj_zx_mean,
    proj_zx_square,
    proj_bc,
    proj_bc_mean,
    proj_bc_square,
    proj_step,
    proj_step_mean,
    proj_step_square,
    conv_inner,
    conv_inner_mean,
    conv_inner_square,
    conv_bc,
    conv_bc_mean,
    conv_bc_square,
    head_params,
    head_params_mean,
    head_params_square,
    gate_gain,
    gate_gain_mean,
    gate_gain_square,
    proj_out,
    proj_out_mean,
    proj_out_square,
):
    seq_count, local_len, model_width = inputs.shape
    local_inner = proj_zx.shape[2]
    state_width = proj_bc.shape[1] // 2
    local_heads = proj_step.shape[1]
    head_width = local_inner // local_heads
    rows = seq_count * local_len
    seq_size, seq_index = lax.axis_size("seq"), lax.axis_index("seq")

    def wide(a):
        selector = jnp.repeat(jnp.eye(local_heads, dtype=F32), head_width, axis=1)
        return jnp.einsum("...h,hc->...c", a, selector, precision=HIGHEST_PREC)

    positions = seq_index * local_len + jnp.arange(local_len)
    is_valid = (positions[None, :] < lengths[:, None]).astype(F32)
    tokens = inputs.astype(F32)
    inverse_rms = lax.rsqrt(jnp.mean(tokens * tokens, axis=-1, keepdims=True) + EPS)
    unit_tokens = tokens * inverse_rms
    normed = (unit_tokens * norm_gain).astype(BF16)
    z_weight = proj_zx[:, 0].astype(BF16)
    x_weight = proj_zx[:, 1].astype(BF16)
    bc_weight = proj_bc.astype(BF16)
    step_weight = proj_step.astype(BF16)
    out_weight = proj_out.astype(BF16)
    xbc_weight = jnp.concatenate([x_weight, bc_weight], axis=1)
    mixed_in = jnp.einsum("btd,dc->btc", normed, xbc_weight, preferred_element_type=F32).astype(BF16)
    edge_in = passed_along(mixed_in[:, local_len - CONV + 1 :], "seq", 1)
    raw_step = jnp.einsum("btd,dh->bth", normed, step_weight, preferred_element_type=F32)
    gate_input = jnp.einsum("btd,dc->btc", normed, z_weight, preferred_element_type=F32)
    conv_weight = jnp.concatenate([conv_inner, conv_bc], axis=-1)
    taps = jnp.pad(conv_weight, ((0, 8 - CONV - 1), (0, 0)))
    edge_rows = jnp.pad(edge_in, ((0, 0), (16 - CONV + 1, 0), (0, 0)))
    decay_log, step_bias, skip_gain = head_params[0], head_params[1], head_params[2]
    step_size = jax.nn.softplus(raw_step + step_bias)
    log_decay = -step_size * jnp.exp(decay_log)
    parts = seq_size // seq_count
    activated, packed = conv_forward(
        mixed_in, edge_rows, taps, step_size, log_decay, state_width, parts
    )
    entering, block_decays = states_before(
        packed.reshape((seq_size,) + packed.shape[2:]), state_width // parts, "seq"
    )
    entering = entering.reshape(seq_count, state_width, local_inner)
    x_values = activated[..., :local_inner]
    c_values = activated[..., local_inner + state_width :]
    earlier = jnp.tril(jnp.ones((local_len, local_len), F32))
    running = jnp.einsum("ts,bsh->bth", earlier, log_decay, precision=HIGHEST_PREC)

    scanned_raw, states = scan_forward(activated, step_size, log_decay, entering)
    skip_wide = jnp.repeat(skip_gain, head_width)[None, None]
    scanned = scanned_raw + skip_wide * x_values.astype(F32)
    gate_act = jax.nn.silu(gate_input)
    gated_values = scanned * gate_act
    square_sum = jnp.sum(gated_values * gated_values, axis=-1)
    scaled = (gated_values * gate_gain).astype(BF16)
    partial_out = jnp.einsum("bti,di->btd", scaled, out_weight, preferred_element_type=F32)
    out_cotangent = cotangent.astype(F32) * is_valid[..., None]
    partial_scale_grad = jnp.sum(out_cotangent * partial_out, axis=-1)
    square_total, scale_grad = lax.psum(jnp.stack([square_sum, partial_scale_grad]), "head")
    out_scale = lax.rsqrt(square_total / INNER + EPS)
    proj_grad = (out_scale[..., None] * out_cotangent).astype(BF16)
    square_grad = -0.5 * scale_grad * out_scale * out_scale * out_scale / INNER
    out_weight_grad = jnp.einsum("btd,bti->di", proj_grad, scaled, preferred_element_type=F32)
    scaled_grad = jnp.einsum("btd,di->bti", proj_grad, out_weight, preferred_element_type=F32)
    gate_gain_grad = jnp.sum(scaled_grad * gated_values, axis=(0, 1))
    gated_grad = scaled_grad * gate_gain + 2.0 * gated_values * square_grad[..., None]
    scanned_grad = gated_grad * gate_act
    gate_grad = (gated_grad * scanned * silu_slope(gate_input)).astype(BF16)
    local_back = jnp.einsum(
        "btn,btc->bnc",
        c_values,
        (scanned_grad * wide(jnp.exp(running))).astype(BF16),
        preferred_element_type=F32,
    )
    leaving = states_after(local_back, block_decays, "seq")
    projected = halved(partial_out.astype(BF16).reshape(rows, model_width), "head")
    leaving, projected = lax.optimization_barrier((leaving, projected))
    leaving = leaving.reshape(local_back.shape)
    z_weight_grad = jnp.einsum("btd,btc->dc", normed, gate_grad, preferred_element_type=F32)
    early_grads = jnp.concatenate([out_weight_grad, z_weight_grad], axis=0).astype(BF16)
    early_grads, _ = lax.optimization_barrier((early_grads, leaving))
    early_parts = exchanged(to_blocks(early_grads, seq_size), "seq")
    projected_far = swapped(projected, "head", axis_masks("head")[-1])
    x_raw, bc_grad, step_in_grad, x_first, x_last, x_tap_sums, head_totals = scan_backward(
        activated,
        step_size,
        log_decay,
        skip_wide,
        scanned_grad,
        scanned_raw,
        states,
        leaving,
        mixed_in,
        edge_rows,
        taps,
        jax.nn.sigmoid(raw_step + step_bias),
        jnp.exp(decay_log)[None],
    )
    x_raw, early_parts, projected_far = lax.optimization_barrier(
        (x_raw, early_parts, projected_far)
    )
    projected_half, projected_other = regathered(added(projected, projected_far), "head")
    early_own = jnp.sum(early_parts.astype(F32), axis=0).astype(BF16)
    early_all = lax.all_gather(early_own, "seq")
    bc_sum = halved(bc_grad.reshape(rows, 2 * state_width), "head")
    x_in_grad = joined_edges(x_raw, x_first, x_last, conv_weight[:, :local_inner])
    x_in_grad, bc_sum = lax.optimization_barrier((x_in_grad, bc_sum))
    bc_far = swapped(bc_sum, "head", axis_masks("head")[-1])
    normed_partial = normed_products(
        gate_grad.reshape(rows, local_inner),
        x_in_grad.reshape(rows, local_inner),
        step_in_grad.reshape(rows, local_heads),
        z_weight,
        x_weight,
        step_weight,
    )
    x_weight_grad = jnp.einsum("btd,btc->dc", normed, x_in_grad, preferred_element_type=F32)
    normed_sum = halved(normed_partial, "head")
    bc_added = added(bc_sum, bc_far)
    normed_sum, bc_added = lax.optimization_barrier((normed_sum, bc_added))
    bc_half, bc_other = regathered(bc_added, "head")
    x_blocks, _ = lax.optimization_barrier((to_blocks(x_weight_grad, seq_size), normed_sum))
    x_parts = exchanged(x_blocks, "seq")
    normed_far = swapped(normed_sum, "head", axis_masks("head")[-1])

    scalars = jnp.concatenate(
        [lengths, jnp.stack([seq_index * local_len, near_bit("head", 1)]).astype(jnp.int32)]
    )
    bc_half, early_all, _ = lax.optimization_barrier((bc_half, early_all, normed_sum))
    early_sums = early_all.reshape(2, model_width, local_inner)
    bc_raw_grad, bc_first, bc_last, bc_tap_sums = bc_backward(
        scalars,
        bc_half,
        bc_other,
        mixed_in[..., local_inner:],
        edge_rows[..., local_inner:],
        taps[:, local_inner:],
    )
    bc_in_grad = joined_edges(bc_raw_grad, bc_first, bc_last, conv_weight[:, local_inner:])
    bc_in_grad, x_parts = lax.optimization_barrier((bc_in_grad, x_parts))
    x_own = jnp.sum(x_parts.astype(F32), axis=0).astype(BF16)
    x_all = lax.all_gather(x_own, "seq")
    x_sum = x_all.reshape(model_width, local_inner)
    bc_weight_grad = jnp.einsum("btd,btc->dc", normed, bc_in_grad, preferred_element_type=F32)
    bc_blocks = to_blocks(bc_weight_grad, seq_size)
    bc_parts = exchanged(bc_blocks, "seq")
    flat_tokens = inputs.reshape(rows, model_width)
    block_out = merge_call(
        out_kernel,
        scalars,
        projected_half,
        projected_other,
        (flat_tokens, out_scale.reshape(rows, 1)),
        [row_block(model_width), row_block(1)],
        row_block(model_width),
        jax.ShapeDtypeStruct((rows, model_width), BF16),
    )
    out_updated = adam_update(
        proj_out,
        proj_out_mean,
        proj_out_square,
        early_sums[0].astype(F32),
        LEARNING_RATES[-1],
        WEIGHT_DECAYS[-1],
    )
    normed_far, block_out, out_updated, _ = lax.optimization_barrier(
        (normed_far, block_out, out_updated, bc_blocks)
    )
    block_out = block_out.reshape(inputs.shape)
    normed_half, normed_other = regathered(added(normed_sum, normed_far), "head")
    input_grad, norm_gain_grad = merge_call(
        functools.partial(tail_kernel, local_len),
        scalars,
        normed_half,
        normed_other,
        (
            bc_in_grad.reshape(rows, 2 * state_width),
            bc_weight,
            flat_tokens,
            cotangent.reshape(rows, model_width),
            norm_gain[None],
        ),
        [
            row_block(2 * state_width),
            whole_block(bc_weight.shape),
            row_block(model_width),
            row_block(model_width),
            whole_block((1, model_width)),
        ],
        [row_block(model_width), whole_block((1, model_width))],
        [
            jax.ShapeDtypeStruct((rows, model_width), F32),
            jax.ShapeDtypeStruct((1, model_width), F32),
        ],
    )
    input_grad = input_grad.reshape(inputs.shape)
    bc_own = jnp.sum(bc_parts.astype(F32), axis=0).astype(BF16)
    bc_all = lax.all_gather(bc_own, "seq")
    step_weight_grad = jnp.einsum("btd,bth->hd", normed, step_in_grad, preferred_element_type=F32)
    conv_inner_grad = x_tap_sums[: CONV + 1]
    conv_bc_grad = bc_tap_sums[: CONV + 1]
    head_grad = head_totals[:3]
    small_grads = (
        norm_gain_grad[0],
        step_weight_grad,
        conv_inner_grad,
        conv_bc_grad,
        head_grad,
        gate_gain_grad,
    )
    flat = jnp.concatenate([part.reshape(-1) for part in small_grads])
    count = flat.shape[0]
    flat = jnp.pad(flat, (0, -count % 1024)).reshape(-1, 128)
    flat = doubling_sum(flat, "seq").reshape(-1)
    small_sums, at = [], 0
    for part in small_grads:
        small_sums.append(flat[at : at + part.size].reshape(part.shape))
        at += part.size

    summed_grads = (
        small_sums[0],
        jnp.stack([early_sums[1], x_sum], axis=1),
        bc_all.reshape(bc_weight_grad.shape).astype(F32),
        small_sums[1].T,
        small_sums[2],
        small_sums[3],
        small_sums[4],
        small_sums[5],
        None,
    )
    params = (
        norm_gain,
        proj_zx,
        proj_bc,
        proj_step,
        conv_inner,
        conv_bc,
        head_params,
        gate_gain,
        proj_out,
    )
    means = (
        norm_gain_mean,
        proj_zx_mean,
        proj_bc_mean,
        proj_step_mean,
        conv_inner_mean,
        conv_bc_mean,
        head_params_mean,
        gate_gain_mean,
        proj_out_mean,
    )
    squares = (
        norm_gain_square,
        proj_zx_square,
        proj_bc_square,
        proj_step_square,
        conv_inner_square,
        conv_bc_square,
        head_params_square,
        gate_gain_square,
        proj_out_square,
    )
    results = [block_out, input_grad]
    for weight, mean_old, square_old, gradient, step_rate, decay_weight in zip(
        params, means, squares, summed_grads, LEARNING_RATES, WEIGHT_DECAYS
    ):
        if gradient is None:
            updated = out_updated
        elif weight.ndim == 3:
            updated = adam_tiles(weight, mean_old, square_old, gradient, step_rate, decay_weight)
        else:
            updated = adam_update(weight, mean_old, square_old, gradient, step_rate, decay_weight)
        results.extend(updated)
    return tuple(results)


def solution(mesh):
    in_specs = (
        P(None, "seq", None),
        P(None, "seq", None),
        P(),
        P(),
        P(),
        P(),
        P(None, None, "head"),
        P(None, None, "head"),
        P(None, None, "head"),
        P(),
        P(),
        P(),
        P(None, "head"),
        P(None, "head"),
        P(None, "head"),
        P(None, "head"),
        P(None, "head"),
        P(None, "head"),
        P(),
        P(),
        P(),
        P(None, "head"),
        P(None, "head"),
        P(None, "head"),
        P("head"),
        P("head"),
        P("head"),
        P(None, "head"),
        P(None, "head"),
        P(None, "head"),
    )
    out_specs = (
        P(None, "seq", None),
        P(None, "seq", None),
        P(),
        P(),
        P(),
        P(None, None, "head"),
        P(None, None, "head"),
        P(None, None, "head"),
        P(),
        P(),
        P(),
        P(None, "head"),
        P(None, "head"),
        P(None, "head"),
        P(None, "head"),
        P(None, "head"),
        P(None, "head"),
        P(),
        P(),
        P(),
        P(None, "head"),
        P(None, "head"),
        P(None, "head"),
        P("head"),
        P("head"),
        P("head"),
        P(None, "head"),
        P(None, "head"),
        P(None, "head"),
    )
    return jax.shard_map(shards, mesh=mesh, in_specs=in_specs, out_specs=out_specs, check_vma=False)
```

```python
import functools

import jax
import jax.numpy as jnp
from jax import lax
from jax.experimental import pallas as pl
from jax.experimental.pallas import tpu as pltpu
from jax.sharding import PartitionSpec as P

INNER = 2048
CONV = 4
CHUNK = 128
GROUP = 2
STEP = 7


EPS = 1e-05
BETA_ONE = 0.9
BETA_TWO = 0.95
ADAM_EPS = 1e-08
LEARNING_RATES = (0.6, 0.09, 0.09, 0.09, 0.9, 0.9, 0.9, 0.6, 0.06)
WEIGHT_DECAYS = (0.0, 0.1, 0.1, 0.1, 0.0, 0.0, 0.0, 0.0, 0.1)
HIGHEST_PREC = lax.Precision.HIGHEST
F32 = jnp.float32
BF16 = jnp.bfloat16


def passed_along(block, axis, distance):
    devices = range(lax.axis_size(axis))
    route = [(i - distance, i) for i in devices if i - distance in devices]
    return lax.ppermute(block, axis, route)


def swapped(block, axis, mask):
    return lax.ppermute(block, axis, [(i, i ^ mask) for i in range(lax.axis_size(axis))])


def doubling_sum(part, axis):
    for k in range(lax.axis_size(axis).bit_length() - 1):
        part = part + swapped(part, axis, 1 << k)
    return part


def axis_masks(axis):
    return [1 << k for k in range(lax.axis_size(axis).bit_length() - 1)]


def near_bit(axis, mask):
    return (lax.axis_index(axis) // mask) % 2


def added(a, b):
    return (a.astype(F32) + b.astype(F32)).astype(BF16)


def halved(part, axis):
    for mask in axis_masks(axis)[:-1]:
        bit = near_bit(axis, mask)
        halves = part.reshape((2, part.shape[0] // 2) + part.shape[1:])
        sent = lax.dynamic_index_in_dim(halves, 1 - bit, 0, keepdims=False)
        kept = lax.dynamic_index_in_dim(halves, bit, 0, keepdims=False)
        part = added(kept, swapped(sent, axis, mask))
    return part


def joined(part, got, bit):
    first = jnp.where(bit == 0, part, got)
    second = jnp.where(bit == 0, got, part)
    return jnp.concatenate([first, second], axis=0)


def regathered(part, axis):
    masks = axis_masks(axis)[:-1]
    for mask in reversed(masks[1:]):
        part = joined(part, swapped(part, axis, mask), near_bit(axis, mask))
    return part, swapped(part, axis, masks[0])


def halving_sum(part, axis):
    part = halved(part, axis)
    part = added(part, swapped(part, axis, axis_masks(axis)[-1]))
    part, other = regathered(part, axis)
    return joined(part, other, near_bit(axis, 1))


def exchanged(blocks, axis):
    return lax.all_to_all(blocks, axis, 0, 0, tiled=True)


def to_blocks(state, count):
    return state.astype(BF16).reshape(count, -1, state.shape[-1])


def states_before(packed, height, axis):
    size = lax.axis_size(axis)
    got = exchanged(packed, axis).astype(F32)
    decays = got[:, height : height + 1] + got[:, height + 1 : height + 2]
    entering = [jnp.zeros(got[0, :height].shape, F32)]
    for k in range(size - 1):
        entering.append(decays[k] * entering[-1] + got[k, :height])
    return exchanged(jnp.stack(entering).astype(BF16), axis), decays


def states_after(state, decays, axis):
    size = lax.axis_size(axis)
    got = exchanged(to_blocks(state, size), axis).astype(F32)
    leaving = [jnp.zeros(got[0].shape, F32)]
    for k in range(size - 1, 0, -1):
        leaving.append(decays[k] * leaving[-1] + got[k])
    return exchanged(jnp.stack(leaving[::-1]).astype(BF16), axis)


def lane_tiles(a):
    rows, two, columns = a.shape
    return a.reshape(rows, two, columns // 128, 128).transpose(0, 2, 1, 3).reshape(rows, -1, 128)


def from_lane_tiles(a, shape):
    rows, two, columns = shape
    return a.reshape(rows, columns // 128, two, 128).transpose(0, 2, 1, 3).reshape(shape)


def dot(a, b, dims=((1,), (0,)), precision=None):
    return lax.dot_general(a, b, (dims, ((), ())), precision=precision, preferred_element_type=F32)


def alternately(bodies):
    bodies = list(bodies)
    while bodies:
        bodies = [body for body in bodies if next(body, bodies) is not bodies]


def expander(heads, width):
    row = lax.broadcasted_iota(jnp.int32, (heads, heads * width), 0)
    column = lax.broadcasted_iota(jnp.int32, (heads, heads * width), 1)
    inside = (column >= row * width) & (column < (row + 1) * width)
    return jnp.where(inside, 1.0, 0.0).astype(BF16)


def split_dot(a, b, dims):
    high = a.astype(BF16)
    low = (a - high.astype(F32)).astype(BF16)
    return dot(high, b, dims) + dot(low, b, dims)


def spread(a, expand):
    return split_dot(a, expand, ((1,), (0,)))


def head_sums(a, expand):
    return split_dot(a, expand, ((1,), (1,)))


def pair_rows(a):
    lane = lax.broadcasted_iota(jnp.int32, a.shape, 1)
    first = lane < a.shape[1] // 2
    zero = jnp.zeros_like(a)
    return jnp.concatenate([jnp.where(first, a, zero), jnp.where(first, zero, a)], axis=0)


def chunk_decays(decay):
    q = decay.shape[0]
    row = lax.broadcasted_iota(jnp.int32, (q, q), 0)
    column = lax.broadcasted_iota(jnp.int32, (q, q), 1)
    lower = jnp.where(row >= column, 1.0, 0.0).astype(F32)
    cum = dot(lower, decay, precision=HIGHEST_PREC)
    cum_t = dot(decay, lower, ((0,), (1,)), precision=HIGHEST_PREC)
    return cum, cum_t, row, column


def scan_kernel(x_ref, b_ref, c_ref, step_ref, decay_ref, enter_ref, y_ref, in_ref, state):
    group, _, heads = step_ref.shape
    width = x_ref.shape[2] // heads

    @pl.when(pl.program_id(1) == 0)
    def _():
        state[...] = enter_ref[...].astype(F32)

    expand = expander(heads, width)

    def body(i):
        cum, cum_t, row, column = chunk_decays(decay_ref[i])
        causal = row >= column
        q = cum.shape[0]
        total = cum[q - 1 : q, :]
        b, c = b_ref[i], c_ref[i]
        x = x_ref[i].astype(F32)
        step = step_ref[i]
        yield
        xs = (x * spread(step, expand)).astype(BF16)
        grown = spread(jnp.exp(cum), expand)
        xw = (x * spread(step * jnp.exp(total - cum), expand)).astype(BF16)
        yield
        scores = dot(c, b, ((1,), (1,)))
        before = state[i]
        in_ref[i, 0] = before
        from_state = grown * dot(c, before.astype(BF16))
        yield
        for pair in range(heads // 2):
            lanes = slice(pair * 2 * width, (pair + 1) * 2 * width)
            mixing = []
            for h in (2 * pair, 2 * pair + 1):
                between = cum[:, h : h + 1] - cum_t[h : h + 1, :]
                mixing.append((jnp.exp(jnp.where(causal, between, -1e30)) * scores).astype(BF16))
            within = dot(jnp.concatenate(mixing, axis=1), pair_rows(xs[:, lanes]))
            y_ref[i, :, lanes] = within + from_state[:, lanes]
            yield
        state[i] = grown[q - 1 : q, :] * before + dot(b, xw, ((0,), (0,)))

    alternately(body(i) for i in range(group))


def conv_back_step(act_grad, mixed, previous, taps, after):
    q = mixed.shape[0]
    shifted = conv_windows(mixed, previous)
    convolved = taps[CONV : CONV + 1]
    for k in range(CONV):
        convolved = convolved + taps[k : k + 1] * shifted[k]
    conv_grad = act_grad * silu_slope(convolved)
    extended = jnp.concatenate([conv_grad, after], axis=0)
    mixed_grad = taps[CONV - 1 : CONV] * conv_grad
    for k in range(CONV - 1):
        mixed_grad = mixed_grad + taps[k : k + 1] * extended[CONV - 1 - k : CONV - 1 - k + q]
    sums = [jnp.sum(conv_grad * part, axis=0, keepdims=True) for part in shifted]
    sums.append(jnp.sum(conv_grad, axis=0, keepdims=True))
    sums.append(jnp.zeros((8 - CONV - 1, mixed.shape[1]), F32))
    return conv_grad, mixed_grad, jnp.concatenate(sums, axis=0)


def rows_before(edge_ref, previous_ref, i, chunk):
    first = pl.program_id(1) == chunk
    return jnp.where(first, edge_ref[i].astype(F32), previous_ref[i].astype(F32))[8:]


def back_kernel(
    x_ref, b_ref, c_ref, step_ref, decay_ref, skip_ref, dy_ref, y_ref, in_ref, leave_ref,
    mixed_ref, previous_ref, edge_ref, taps_ref, slope_ref, rate_ref,
    mixed_grad_ref, dbc_ref, pre_ref, first_ref, last_ref, tap_sums_ref, head_sums_ref,
    grad, after
):
    group, _, heads = step_ref.shape
    width = x_ref.shape[2] // heads
    start = (pl.program_id(0) == 0) & (pl.program_id(1) == 0)

    @pl.when(start)
    def _():
        tap_sums_ref[...] = jnp.zeros_like(tap_sums_ref)
        head_sums_ref[...] = jnp.zeros_like(head_sums_ref)

    @pl.when(pl.program_id(1) == 0)
    def _():
        after[...] = jnp.zeros_like(after)
        grad[...] = leave_ref[...].astype(F32)

    expand = expander(heads, width)
    last_chunk = pl.program_id(1) == 0

    def body(i):
        cum, cum_t, row, column = chunk_decays(decay_ref[i])
        later = column >= row
        q = cum.shape[0]
        total = cum[q - 1 : q, :]
        b, c = b_ref[i], c_ref[i]
        x = x_ref[i].astype(F32)
        step_wide = spread(step_ref[i], expand)
        yield
        xs = (x * step_wide).astype(BF16)
        grown = spread(jnp.exp(cum), expand)
        waned = spread(jnp.exp(total - cum), expand)
        yield
        xw = (x * step_wide * waned).astype(BF16)
        dy = dy_ref[i]
        dy_low = dy.astype(BF16)
        edy = (dy * grown).astype(BF16)
        before = in_ref[i, 0]
        after_grad = grad[i]
        after_low = after_grad.astype(BF16)
        yield
        scores_t = dot(b, c, ((1,), (1,)))
        v_state = waned * dot(b, after_low)
        dscores_t = jnp.zeros((q, q), F32)
        v_parts = []
        yield
        for pair in range(heads // 2):
            lanes = slice(pair * 2 * width, (pair + 1) * 2 * width)
            dy_pair = pair_rows(dy_low[:, lanes])
            xs_pair = pair_rows(xs[:, lanes])
            dmix = dot(xs_pair, dy_low[:, lanes], ((1,), (1,)))
            mixing = []
            for k, h in enumerate((2 * pair, 2 * pair + 1)):
                between = cum_t[h : h + 1, :] - cum[:, h : h + 1]
                fade = jnp.exp(jnp.where(later, between, -1e30))
                mixing.append((fade * scores_t).astype(BF16))
                dscores_t = dscores_t + fade * dmix[k * q : (k + 1) * q]
            v_parts.append(dot(jnp.concatenate(mixing, axis=1), dy_pair))
            yield
        v = jnp.concatenate(v_parts, axis=1) + v_state
        xs_wide = xs.astype(F32)
        etotal = grown[q - 1 : q, :]
        end_row = jnp.sum(xs_wide * v_state, axis=0, keepdims=True) + jnp.sum(
            etotal * before * after_grad, axis=0, keepdims=True
        )
        crossing = dy_low.astype(F32) * y_ref[i] - xs_wide * v
        last = lax.broadcasted_iota(jnp.int32, crossing.shape, 0) == q - 1
        crossing = crossing + jnp.where(last, end_row, 0.0)
        upper = jnp.where(column >= row, 1.0, 0.0).astype(F32)
        yield
        decay_grad = dot(upper, head_sums(crossing, expand), precision=HIGHEST_PREC)
        pre_grad = (head_sums(x * v, expand) - rate_ref[...] * decay_grad) * slope_ref[i]
        pre_ref[i] = pre_grad.astype(BF16)
        sums = [
            jnp.sum(decay_grad * decay_ref[i], axis=0, keepdims=True),
            jnp.sum(pre_grad, axis=0, keepdims=True),
            jnp.sum(head_sums(x * dy, expand), axis=0, keepdims=True),
            jnp.zeros((5, heads), F32),
        ]
        head_sums_ref[...] += jnp.concatenate(sums, axis=0)
        yield
        dscores_low = dscores_t.astype(BF16)
        state = b.shape[1]
        dbc_ref[i, :, :state] = (
            dot(dscores_low, c) + dot(xw, after_low, ((1,), (1,)))
        ).astype(BF16)
        dbc_ref[i, :, state:] = (
            dot(dscores_low, b, ((0,), (0,))) + dot(edy, before.astype(BF16), ((1,), (1,)))
        ).astype(BF16)
        grad[i] = etotal * after_grad + dot(c, edy, ((0,), (0,)))
        yield
        dx = step_wide * v + skip_ref[0] * dy
        previous = rows_before(edge_ref, previous_ref, i, pl.num_programs(1) - 1)
        conv_grad, mixed_grad, tap_sums = conv_back_step(
            dx, mixed_ref[i].astype(F32), previous, taps_ref[...], after[i]
        )
        mixed_grad_ref[i] = mixed_grad.astype(BF16)
        first_ref[i] = conv_grad[:8]
        after[i] = conv_grad[:8]
        last_ref[i] = jnp.where(last_chunk, mixed_grad[q - 8 :], last_ref[i])
        tap_sums_ref[...] += tap_sums

    alternately(body(i) for i in range(group))


def act_blocks(inner, state, place):
    def part(lanes, at):
        return pl.BlockSpec((GROUP, CHUNK, lanes), lambda s, k: (s, place(k), at))

    return [part(inner, 0), part(state, inner // state), part(state, inner // state + 1)]


def conv_windows(mixed, previous):
    q = mixed.shape[0]
    window = jnp.concatenate([previous, mixed], axis=0)
    return [window[8 - CONV + 1 + k : 8 - CONV + 1 + k + q] for k in range(CONV)]


def first_kernel(
    mixed_ref, previous_ref, edge_ref, taps_ref, step_ref, decay_ref, act_ref, packed_ref, state, total
):
    chunk = pl.program_id(1)
    group, _, heads = step_ref.shape
    state_width, inner = state.shape[1:]

    @pl.when(chunk == 0)
    def _():
        state[...] = jnp.zeros_like(state)
        total[...] = jnp.zeros_like(total)

    expand = expander(heads, inner // heads)

    def body(i):
        previous = rows_before(edge_ref, previous_ref, i, 0)
        cum = chunk_decays(decay_ref[i])[0]
        q = cum.shape[0]
        last = cum[q - 1 : q, :]
        yield
        weights = spread(step_ref[i] * jnp.exp(last - cum), expand)
        kept = spread(jnp.exp(cum), expand)[q - 1 : q]
        yield
        convolved = taps_ref[CONV : CONV + 1]
        for k, part in enumerate(conv_windows(mixed_ref[i].astype(F32), previous)):
            convolved = convolved + taps_ref[k : k + 1] * part
        activated = jax.nn.silu(convolved).astype(BF16)
        act_ref[i] = activated
        yield
        xw = (activated[:, :inner].astype(F32) * weights).astype(BF16)
        b = activated[:, inner : inner + state_width]
        state[i] = kept * state[i] + dot(b, xw, ((0,), (0,)))
        total[i] = total[i] + last

    alternately(body(i) for i in range(group))

    @pl.when(chunk == pl.num_programs(1) - 1)
    def _():
        height = packed_ref.shape[2] - 16
        for i in range(group):
            decay = spread(jnp.exp(jnp.broadcast_to(total[i], (8, heads))), expand)[:1]
            high = decay.astype(BF16).astype(F32)
            tail = jnp.concatenate([high, decay - high, jnp.zeros((14, inner), F32)], axis=0)
            for part in range(packed_ref.shape[1]):
                rows = state[i, part * height : (part + 1) * height]
                packed_ref[i, part] = jnp.concatenate([rows, tail], axis=0).astype(BF16)


def conv_forward(mixed, edge, taps, step, decay, state, parts):
    seqs, length, lanes = mixed.shape
    heads, inner = step.shape[2], lanes - 2 * state
    chunks, tall = length // CHUNK, CHUNK // 16
    height = state // parts + 16

    def block(width):
        return pl.BlockSpec((GROUP, CHUNK, width), lambda s, k: (s, k, 0))

    return pl.pallas_call(
        first_kernel,
        grid=(seqs // GROUP, chunks),
        in_specs=[
            block(lanes),
            pl.BlockSpec((GROUP, 16, lanes), lambda s, k: (s, jnp.maximum(k * tall - 1, 0), 0)),
            pl.BlockSpec((GROUP, 16, lanes), lambda s, k: (s, 0, 0)),
            pl.BlockSpec((8, lanes), lambda s, k: (0, 0)),
            block(heads),
            block(heads),
        ],
        out_specs=[
            block(lanes),
            pl.BlockSpec((GROUP, parts, height, inner), lambda s, k: (s, 0, 0, 0)),
        ],
        out_shape=[
            jax.ShapeDtypeStruct(mixed.shape, BF16),
            jax.ShapeDtypeStruct((seqs, parts, height, inner), BF16),
        ],
        scratch_shapes=[pltpu.VMEM((GROUP, state, inner), F32), pltpu.VMEM((GROUP, 1, heads), F32)],
        compiler_params=pltpu.CompilerParams(vmem_limit_bytes=40 << 20),
        cost_estimate=load(9),
    )(mixed, mixed, edge, taps, step, decay)


def scan_forward(activated, step, decay, enter):
    seqs, length, heads = step.shape
    state, inner = enter.shape[1:]
    chunks = length // CHUNK

    def block(lanes):
        return pl.BlockSpec((GROUP, CHUNK, lanes), lambda s, k: (s, k, 0))

    return pl.pallas_call(
        scan_kernel,
        grid=(seqs // GROUP, chunks),
        in_specs=act_blocks(inner, state, lambda k: k)
        + [
            block(heads),
            block(heads),
            pl.BlockSpec((GROUP, state, inner), lambda s, k: (s, 0, 0)),
        ],
        out_specs=[
            block(inner),
            pl.BlockSpec((GROUP, 1, state, inner), lambda s, k: (s, k, 0, 0)),
        ],
        out_shape=[
            jax.ShapeDtypeStruct((seqs, length, inner), F32),
            jax.ShapeDtypeStruct((seqs, chunks, state, inner), F32),
        ],
        scratch_shapes=[pltpu.VMEM((GROUP, state, inner), F32)],
        compiler_params=pltpu.CompilerParams(vmem_limit_bytes=40 << 20),
        cost_estimate=load(13),
    )(activated, activated, activated, step, decay, enter)


def conv_blocks(chunks, lanes, at):
    tall = CHUNK // 16
    return [
        pl.BlockSpec((GROUP, CHUNK, lanes), lambda s, k, *_: (s, chunks - 1 - k, at)),
        pl.BlockSpec(
            (GROUP, 16, lanes), lambda s, k, *_: (s, jnp.maximum((chunks - 1 - k) * tall - 1, 0), at)
        ),
        pl.BlockSpec((GROUP, 16, lanes), lambda s, k, *_: (s, 0, at)),
        pl.BlockSpec((8, lanes), lambda s, k, *_: (0, at)),
    ]


def conv_outs(seqs, chunks, lanes):
    specs = [
        pl.BlockSpec((GROUP, CHUNK, lanes), lambda s, k, *_: (s, chunks - 1 - k, 0)),
        pl.BlockSpec((GROUP, 8, lanes), lambda s, k, *_: (s, 0, 0)),
        pl.BlockSpec((GROUP, 8, lanes), lambda s, k, *_: (s, 0, 0)),
        pl.BlockSpec((8, lanes), lambda s, k, *_: (0, 0)),
    ]
    shapes = [
        jax.ShapeDtypeStruct((seqs, chunks * CHUNK, lanes), BF16),
        jax.ShapeDtypeStruct((seqs, 8, lanes), F32),
        jax.ShapeDtypeStruct((seqs, 8, lanes), F32),
        jax.ShapeDtypeStruct((8, lanes), F32),
    ]
    return specs, shapes


def scan_backward(
    activated, step, decay, skip, dy, y, states, leave, mixed, edge, taps, slope, rate
):
    seqs, length, heads = step.shape
    state, inner = leave.shape[1:]
    chunks = length // CHUNK

    def block(lanes):
        return pl.BlockSpec((GROUP, CHUNK, lanes), lambda s, k: (s, chunks - 1 - k, 0))

    conv_specs, conv_shapes = conv_outs(seqs, chunks, inner)
    return pl.pallas_call(
        back_kernel,
        grid=(seqs // GROUP, chunks),
        in_specs=act_blocks(inner, state, lambda k: chunks - 1 - k)
        + [
            block(heads),
            block(heads),
            pl.BlockSpec((1, 1, inner), lambda s, k: (0, 0, 0)),
            block(inner),
            block(inner),
            pl.BlockSpec((GROUP, 1, state, inner), lambda s, k: (s, chunks - 1 - k, 0, 0)),
            pl.BlockSpec((GROUP, state, inner), lambda s, k: (s, 0, 0)),
        ]
        + conv_blocks(chunks, inner, 0)
        + [block(heads), pl.BlockSpec((1, heads), lambda s, k: (0, 0))],
        out_specs=[conv_specs[0], block(2 * state), block(heads)]
        + conv_specs[1:]
        + [pl.BlockSpec((8, heads), lambda s, k: (0, 0))],
        out_shape=[
            conv_shapes[0],
            jax.ShapeDtypeStruct((seqs, length, 2 * state), BF16),
            jax.ShapeDtypeStruct((seqs, length, heads), BF16),
        ]
        + conv_shapes[1:]
        + [jax.ShapeDtypeStruct((8, heads), F32)],
        scratch_shapes=[pltpu.VMEM((GROUP, state, inner), F32), pltpu.VMEM((GROUP, 8, inner), F32)],
        compiler_params=pltpu.CompilerParams(vmem_limit_bytes=40 << 20),
        cost_estimate=load(30),
    )(
        activated, activated, activated, step, decay, skip, dy, y, states, leave,
        mixed, mixed, edge, taps, slope, rate
    )


def bc_kernel(
    scalars_ref, part_ref, got_ref, mixed_ref, previous_ref, edge_ref, taps_ref,
    mixed_grad_ref, first_ref, last_ref, tap_sums_ref, after
):
    group, q, _ = mixed_ref.shape
    last_chunk = pl.program_id(1) == 0
    start = (pl.program_id(0) == 0) & last_chunk

    @pl.when(start)
    def _():
        tap_sums_ref[...] = jnp.zeros_like(tap_sums_ref)

    @pl.when(last_chunk)
    def _():
        after[...] = jnp.zeros_like(after)

    act_grad = picked(scalars_ref, part_ref, got_ref)

    def body(i):
        previous = rows_before(edge_ref, previous_ref, i, pl.num_programs(1) - 1)
        yield
        conv_grad, mixed_grad, tap_sums = conv_back_step(
            act_grad[i], mixed_ref[i].astype(F32), previous, taps_ref[...], after[i]
        )
        mixed_grad_ref[i] = mixed_grad.astype(BF16)
        first_ref[i] = conv_grad[:8]
        after[i] = conv_grad[:8]
        last_ref[i] = jnp.where(last_chunk, mixed_grad[q - 8 :], last_ref[i])
        tap_sums_ref[...] += tap_sums

    alternately(body(i) for i in range(group))


def bc_backward(scalars, part, got, mixed, edge, taps):
    seqs, length, _ = mixed.shape
    lanes = part.shape[1]
    chunks, at = length // CHUNK, mixed.shape[2] // lanes - 1
    halves = seqs // 2 // GROUP
    half = pl.BlockSpec((GROUP, CHUNK, lanes), lambda s, k, _: (s % halves, chunks - 1 - k, 0))
    conv_specs, conv_shapes = conv_outs(seqs, chunks, lanes)
    return pl.pallas_call(
        bc_kernel,
        grid_spec=pltpu.PrefetchScalarGridSpec(
            num_scalar_prefetch=1,
            grid=(seqs // GROUP, chunks),
            in_specs=[half, half] + conv_blocks(chunks, lanes, at),
            out_specs=conv_specs,
            scratch_shapes=[pltpu.VMEM((GROUP, 8, lanes), F32)],
        ),
        out_shape=conv_shapes,
        compiler_params=pltpu.CompilerParams(vmem_limit_bytes=40 << 20),
        cost_estimate=load(5),
    )(
        scalars,
        part.reshape(seqs // 2, length, lanes),
        got.reshape(seqs // 2, length, lanes),
        mixed,
        mixed,
        edge,
        taps,
    )


def joined_edges(mixed_grad, first, last, taps):
    rows = []
    for j in range(CONV - 1):
        rows.append(sum(taps[k] * first[:, j - k] for k in range(j + 1)))
    edge_grad = passed_along(jnp.stack(rows, axis=1), "seq", -1)
    fixed = last + jnp.pad(edge_grad, ((0, 0), (8 - CONV + 1, 0), (0, 0)))
    return lax.dynamic_update_slice(mixed_grad, fixed.astype(BF16), (0, mixed_grad.shape[1] - 8, 0))


def normed_kernel(gate_ref, x_ref, step_ref, z_weight_ref, x_weight_ref, step_weight_ref, out_ref):
    nt = ((1,), (1,))
    total = dot(gate_ref[...], z_weight_ref[...], nt) + dot(x_ref[...], x_weight_ref[...], nt)
    out_ref[...] = (total + dot(step_ref[...], step_weight_ref[...], nt)).astype(BF16)


def normed_products(gate_grad, x_grad, step_grad, z_weight, x_weight, step_weight):
    rows, width = gate_grad.shape[0], z_weight.shape[0]

    def block(a):
        return pl.BlockSpec((ROWS, a.shape[1]), lambda i: (i, 0))

    def whole(a):
        return pl.BlockSpec(a.shape, lambda i: (0, 0))

    args = (gate_grad, x_grad, step_grad, z_weight, x_weight, step_weight)
    return pl.pallas_call(
        normed_kernel,
        grid=(rows // ROWS,),
        in_specs=[block(a) for a in args[:3]] + [whole(a) for a in args[3:]],
        out_specs=pl.BlockSpec((ROWS, width), lambda i: (i, 0)),
        out_shape=jax.ShapeDtypeStruct((rows, width), BF16),
        compiler_params=pltpu.CompilerParams(vmem_limit_bytes=40 << 20),
        cost_estimate=load(6),
    )(*args)


def picked(scalars_ref, part_ref, got_ref):
    bit = scalars_ref[scalars_ref.shape[0] - 1]
    half = pl.num_programs(0) // 2
    own = (pl.program_id(0) // half) == bit
    return jnp.where(own, part_ref[...].astype(F32), got_ref[...].astype(F32))


def out_kernel(scalars_ref, part_ref, got_ref, tokens_ref, scale_ref, out_ref):
    projected = picked(scalars_ref, part_ref, got_ref)
    out_ref[...] = (tokens_ref[...].astype(F32) + scale_ref[...] * projected).astype(BF16)


def tail_kernel(
    local_len, scalars_ref, part_ref, got_ref, bc_ref, weight_ref, tokens_ref, back_ref, gain_ref,
    out_ref, gain_grad_ref
):
    step = pl.program_id(0)
    height = tokens_ref.shape[0]
    normed_grad = picked(scalars_ref, part_ref, got_ref) + dot(
        bc_ref[...], weight_ref[...], ((1,), (1,))
    )
    tokens = tokens_ref[...].astype(F32)
    inverse_rms = lax.rsqrt(jnp.mean(tokens * tokens, axis=-1, keepdims=True) + EPS)
    unit = tokens * inverse_rms

    @pl.when(step == 0)
    def _():
        gain_grad_ref[...] = jnp.zeros_like(gain_grad_ref)

    gain_grad_ref[...] += jnp.sum(normed_grad * unit, axis=0, keepdims=True)
    unit_grad = normed_grad * gain_ref[...]
    along = jnp.mean(unit_grad * unit, axis=-1, keepdims=True)
    row = step * height
    length = scalars_ref[row // local_len]
    start = scalars_ref[scalars_ref.shape[0] - 2] + row % local_len
    position = start + lax.broadcasted_iota(jnp.int32, tokens.shape, 0)
    back = jnp.where(position < length, back_ref[...].astype(F32), 0.0)
    out_ref[...] = back + inverse_rms * (unit_grad - unit * along)


ROWS = 256


def load(microseconds):
    return pl.CostEstimate(flops=0, transcendentals=0, bytes_accessed=int(microseconds * 3.69e6))


def merge_call(kernel, scalars, part, got, others, other_specs, out_specs, out_shape):
    rows, width = 2 * part.shape[0], part.shape[1]
    blocks = rows // ROWS
    half = pl.BlockSpec((ROWS, width), lambda i, s: (i % (blocks // 2), 0))
    return pl.pallas_call(
        kernel,
        grid_spec=pltpu.PrefetchScalarGridSpec(
            num_scalar_prefetch=1,
            grid=(blocks,),
            in_specs=[half, half] + other_specs,
            out_specs=out_specs,
        ),
        out_shape=out_shape,
        compiler_params=pltpu.CompilerParams(vmem_limit_bytes=40 << 20),
        cost_estimate=load(8),
    )(scalars, part, got, *others)


def row_block(lanes):
    return pl.BlockSpec((ROWS, lanes), lambda i, s: (i, 0))


def whole_block(shape):
    return pl.BlockSpec(shape, lambda i, s: (0, 0))


def adam_kernel(
    step_rate, decay_weight, gradient_ref, weight_ref, mean_ref, square_ref,
    mean_out, square_out, weight_out
):
    mean_out[...], square_out[...], weight_out[...] = adam_update(
        weight_ref[...],
        mean_ref[...],
        square_ref[...],
        gradient_ref[...].astype(F32),
        step_rate,
        decay_weight,
    )


def adam_tiles(weight, mean_old, square_old, gradient, step_rate, decay_weight):
    rows, _, columns = weight.shape
    tiles = pl.BlockSpec((128, columns // 64, 128), lambda i: (i, 0, 0))
    updated = pl.pallas_call(
        functools.partial(adam_kernel, step_rate, decay_weight),
        grid=(rows // 128,),
        in_specs=[tiles] * 4,
        out_specs=[tiles] * 3,
        out_shape=[jax.ShapeDtypeStruct((rows, columns // 64, 128), F32)] * 3,
        compiler_params=pltpu.CompilerParams(vmem_limit_bytes=40 << 20),
        cost_estimate=load(9),
    )(*map(lane_tiles, (gradient, weight, mean_old, square_old)))
    return [from_lane_tiles(part, weight.shape) for part in updated]


def silu_slope(values):
    sigmoid_part = jax.nn.sigmoid(values)
    return sigmoid_part * (1.0 + values * (1.0 - sigmoid_part))


def adam_update(weight, mean_old, square_old, gradient, step_rate, decay_weight):
    mean_new = BETA_ONE * mean_old + (1.0 - BETA_ONE) * gradient
    square_new = BETA_TWO * square_old + (1.0 - BETA_TWO) * gradient * gradient
    corrected_mean = mean_new / (1.0 - BETA_ONE**STEP)
    corrected_square = square_new / (1.0 - BETA_TWO**STEP)
    weight_new = weight - step_rate * (
        corrected_mean / (jnp.sqrt(corrected_square) + ADAM_EPS) + decay_weight * weight
    )
    return (mean_new, square_new, weight_new)


def shards(
    inputs,
    cotangent,
    lengths,
    norm_gain,
    norm_gain_mean,
    norm_gain_square,
    proj_zx,
    proj_zx_mean,
    proj_zx_square,
    proj_bc,
    proj_bc_mean,
    proj_bc_square,
    proj_step,
    proj_step_mean,
    proj_step_square,
    conv_inner,
    conv_inner_mean,
    conv_inner_square,
    conv_bc,
    conv_bc_mean,
    conv_bc_square,
    head_params,
    head_params_mean,
    head_params_square,
    gate_gain,
    gate_gain_mean,
    gate_gain_square,
    proj_out,
    proj_out_mean,
    proj_out_square,
):
    seq_count, local_len, model_width = inputs.shape
    local_inner = proj_zx.shape[2]
    state_width = proj_bc.shape[1] // 2
    local_heads = proj_step.shape[1]
    head_width = local_inner // local_heads
    rows = seq_count * local_len
    seq_size, seq_index = lax.axis_size("seq"), lax.axis_index("seq")

    def wide(a):
        selector = jnp.repeat(jnp.eye(local_heads, dtype=F32), head_width, axis=1)
        return jnp.einsum("...h,hc->...c", a, selector, precision=HIGHEST_PREC)

    positions = seq_index * local_len + jnp.arange(local_len)
    is_valid = (positions[None, :] < lengths[:, None]).astype(F32)
    tokens = inputs.astype(F32)
    inverse_rms = lax.rsqrt(jnp.mean(tokens * tokens, axis=-1, keepdims=True) + EPS)
    unit_tokens = tokens * inverse_rms
    normed = (unit_tokens * norm_gain).astype(BF16)
    z_weight = proj_zx[:, 0].astype(BF16)
    x_weight = proj_zx[:, 1].astype(BF16)
    bc_weight = proj_bc.astype(BF16)
    step_weight = proj_step.astype(BF16)
    out_weight = proj_out.astype(BF16)
    xbc_weight = jnp.concatenate([x_weight, bc_weight], axis=1)
    mixed_in = jnp.einsum("btd,dc->btc", normed, xbc_weight, preferred_element_type=F32).astype(BF16)
    edge_in = passed_along(mixed_in[:, local_len - CONV + 1 :], "seq", 1)
    raw_step = jnp.einsum("btd,dh->bth", normed, step_weight, preferred_element_type=F32)
    gate_input = jnp.einsum("btd,dc->btc", normed, z_weight, preferred_element_type=F32)
    conv_weight = jnp.concatenate([conv_inner, conv_bc], axis=-1)
    taps = jnp.pad(conv_weight, ((0, 8 - CONV - 1), (0, 0)))
    edge_rows = jnp.pad(edge_in, ((0, 0), (16 - CONV + 1, 0), (0, 0)))
    decay_log, step_bias, skip_gain = head_params[0], head_params[1], head_params[2]
    step_size = jax.nn.softplus(raw_step + step_bias)
    log_decay = -step_size * jnp.exp(decay_log)
    parts = seq_size // seq_count
    activated, packed = conv_forward(
        mixed_in, edge_rows, taps, step_size, log_decay, state_width, parts
    )
    entering, block_decays = states_before(
        packed.reshape((seq_size,) + packed.shape[2:]), state_width // parts, "seq"
    )
    entering = entering.reshape(seq_count, state_width, local_inner)
    x_values = activated[..., :local_inner]
    c_values = activated[..., local_inner + state_width :]
    earlier = jnp.tril(jnp.ones((local_len, local_len), F32))
    running = jnp.einsum("ts,bsh->bth", earlier, log_decay, precision=HIGHEST_PREC)

    scanned_raw, states = scan_forward(activated, step_size, log_decay, entering)
    skip_wide = jnp.repeat(skip_gain, head_width)[None, None]
    scanned = scanned_raw + skip_wide * x_values.astype(F32)
    gate_act = jax.nn.silu(gate_input)
    gated_values = scanned * gate_act
    square_sum = jnp.sum(gated_values * gated_values, axis=-1)
    scaled = (gated_values * gate_gain).astype(BF16)
    partial_out = jnp.einsum("bti,di->btd", scaled, out_weight, preferred_element_type=F32)
    out_cotangent = cotangent.astype(F32) * is_valid[..., None]
    partial_scale_grad = jnp.sum(out_cotangent * partial_out, axis=-1)
    square_total, scale_grad = lax.psum(jnp.stack([square_sum, partial_scale_grad]), "head")
    out_scale = lax.rsqrt(square_total / INNER + EPS)
    proj_grad = (out_scale[..., None] * out_cotangent).astype(BF16)
    square_grad = -0.5 * scale_grad * out_scale * out_scale * out_scale / INNER
    out_weight_grad = jnp.einsum("btd,bti->di", proj_grad, scaled, preferred_element_type=F32)
    scaled_grad = jnp.einsum("btd,di->bti", proj_grad, out_weight, preferred_element_type=F32)
    gate_gain_grad = jnp.sum(scaled_grad * gated_values, axis=(0, 1))
    gated_grad = scaled_grad * gate_gain + 2.0 * gated_values * square_grad[..., None]
    scanned_grad = gated_grad * gate_act
    gate_grad = (gated_grad * scanned * silu_slope(gate_input)).astype(BF16)
    local_back = jnp.einsum(
        "btn,btc->bnc",
        c_values,
        (scanned_grad * wide(jnp.exp(running))).astype(BF16),
        preferred_element_type=F32,
    )
    leaving = states_after(local_back, block_decays, "seq")
    projected = halved(partial_out.astype(BF16).reshape(rows, model_width), "head")
    leaving, projected = lax.optimization_barrier((leaving, projected))
    leaving = leaving.reshape(local_back.shape)
    z_weight_grad = jnp.einsum("btd,btc->dc", normed, gate_grad, preferred_element_type=F32)
    early_grads = jnp.concatenate([out_weight_grad, z_weight_grad], axis=0).astype(BF16)
    early_grads, _ = lax.optimization_barrier((early_grads, leaving))
    early_parts = exchanged(to_blocks(early_grads, seq_size), "seq")
    projected_far = swapped(projected, "head", axis_masks("head")[-1])
    x_raw, bc_grad, step_in_grad, x_first, x_last, x_tap_sums, head_totals = scan_backward(
        activated,
        step_size,
        log_decay,
        skip_wide,
        scanned_grad,
        scanned_raw,
        states,
        leaving,
        mixed_in,
        edge_rows,
        taps,
        jax.nn.sigmoid(raw_step + step_bias),
        jnp.exp(decay_log)[None],
    )
    x_raw, early_parts, projected_far = lax.optimization_barrier(
        (x_raw, early_parts, projected_far)
    )
    projected_half, projected_other = regathered(added(projected, projected_far), "head")
    early_own = jnp.sum(early_parts.astype(F32), axis=0).astype(BF16)
    early_all = lax.all_gather(early_own, "seq")
    bc_sum = halved(bc_grad.reshape(rows, 2 * state_width), "head")
    x_in_grad = joined_edges(x_raw, x_first, x_last, conv_weight[:, :local_inner])
    bc_far = swapped(bc_sum, "head", axis_masks("head")[-1])
    x_in_grad, bc_added = lax.optimization_barrier((x_in_grad, added(bc_sum, bc_far)))
    bc_half, bc_other = regathered(bc_added, "head")
    normed_partial = normed_products(
        gate_grad.reshape(rows, local_inner),
        x_in_grad.reshape(rows, local_inner),
        step_in_grad.reshape(rows, local_heads),
        z_weight,
        x_weight,
        step_weight,
    )
    x_weight_grad = jnp.einsum("btd,btc->dc", normed, x_in_grad, preferred_element_type=F32)
    normed_sum = halved(normed_partial, "head")
    x_blocks, bc_other, _ = lax.optimization_barrier(
        (to_blocks(x_weight_grad, seq_size), bc_other, normed_sum)
    )
    x_parts = exchanged(x_blocks, "seq")
    normed_far = swapped(normed_sum, "head", axis_masks("head")[-1])

    scalars = jnp.concatenate(
        [lengths, jnp.stack([seq_index * local_len, near_bit("head", 1)]).astype(jnp.int32)]
    )
    early_sums = early_all.reshape(2, model_width, local_inner)
    bc_raw_grad, bc_first, bc_last, bc_tap_sums = bc_backward(
        scalars,
        bc_half,
        bc_other,
        mixed_in,
        edge_rows,
        taps,
    )
    bc_in_grad = joined_edges(bc_raw_grad, bc_first, bc_last, conv_weight[:, local_inner:])
    bc_in_grad, x_parts = lax.optimization_barrier((bc_in_grad, x_parts))
    x_own = jnp.sum(x_parts.astype(F32), axis=0).astype(BF16)
    x_all = lax.all_gather(x_own, "seq")
    x_sum = x_all.reshape(model_width, local_inner)
    bc_weight_grad = jnp.einsum("btd,btc->dc", normed, bc_in_grad, preferred_element_type=F32)
    bc_blocks = to_blocks(bc_weight_grad, seq_size)
    bc_parts = exchanged(bc_blocks, "seq")
    flat_tokens = inputs.reshape(rows, model_width)
    block_out = merge_call(
        out_kernel,
        scalars,
        projected_half,
        projected_other,
        (flat_tokens, out_scale.reshape(rows, 1)),
        [row_block(model_width), row_block(1)],
        row_block(model_width),
        jax.ShapeDtypeStruct((rows, model_width), BF16),
    )
    out_updated = adam_update(
        proj_out,
        proj_out_mean,
        proj_out_square,
        early_sums[0].astype(F32),
        LEARNING_RATES[-1],
        WEIGHT_DECAYS[-1],
    )
    normed_far, block_out, out_updated, _ = lax.optimization_barrier(
        (normed_far, block_out, out_updated, bc_blocks)
    )
    block_out = block_out.reshape(inputs.shape)
    normed_half, normed_other = regathered(added(normed_sum, normed_far), "head")
    input_grad, norm_gain_grad = merge_call(
        functools.partial(tail_kernel, local_len),
        scalars,
        normed_half,
        normed_other,
        (
            bc_in_grad.reshape(rows, 2 * state_width),
            bc_weight,
            flat_tokens,
            cotangent.reshape(rows, model_width),
            norm_gain[None],
        ),
        [
            row_block(2 * state_width),
            whole_block(bc_weight.shape),
            row_block(model_width),
            row_block(model_width),
            whole_block((1, model_width)),
        ],
        [row_block(model_width), whole_block((1, model_width))],
        [
            jax.ShapeDtypeStruct((rows, model_width), F32),
            jax.ShapeDtypeStruct((1, model_width), F32),
        ],
    )
    input_grad = input_grad.reshape(inputs.shape)
    bc_own = jnp.sum(bc_parts.astype(F32), axis=0).astype(BF16)
    bc_all = exchanged(jnp.broadcast_to(bc_own[None], bc_parts.shape), "seq")
    step_weight_grad = jnp.einsum("btd,bth->hd", normed, step_in_grad, preferred_element_type=F32)
    conv_inner_grad = x_tap_sums[: CONV + 1]
    conv_bc_grad = bc_tap_sums[: CONV + 1]
    head_grad = head_totals[:3]
    small_grads = (
        norm_gain_grad[0],
        step_weight_grad,
        conv_inner_grad,
        conv_bc_grad,
        head_grad,
        gate_gain_grad,
    )
    flat = jnp.concatenate([part.reshape(-1) for part in small_grads])
    count = flat.shape[0]
    flat = jnp.pad(flat, (0, -count % 1024)).reshape(-1, 128)
    flat = doubling_sum(flat, "seq").reshape(-1)
    small_sums, at = [], 0
    for part in small_grads:
        small_sums.append(flat[at : at + part.size].reshape(part.shape))
        at += part.size

    summed_grads = (
        small_sums[0],
        jnp.stack([early_sums[1], x_sum], axis=1),
        bc_all.reshape(bc_weight_grad.shape).astype(F32),
        small_sums[1].T,
        small_sums[2],
        small_sums[3],
        small_sums[4],
        small_sums[5],
        None,
    )
    params = (
        norm_gain,
        proj_zx,
        proj_bc,
        proj_step,
        conv_inner,
        conv_bc,
        head_params,
        gate_gain,
        proj_out,
    )
    means = (
        norm_gain_mean,
        proj_zx_mean,
        proj_bc_mean,
        proj_step_mean,
        conv_inner_mean,
        conv_bc_mean,
        head_params_mean,
        gate_gain_mean,
        proj_out_mean,
    )
    squares = (
        norm_gain_square,
        proj_zx_square,
        proj_bc_square,
        proj_step_square,
        conv_inner_square,
        conv_bc_square,
        head_params_square,
        gate_gain_square,
        proj_out_square,
    )
    results = [block_out, input_grad]
    for weight, mean_old, square_old, gradient, step_rate, decay_weight in zip(
        params, means, squares, summed_grads, LEARNING_RATES, WEIGHT_DECAYS
    ):
        if gradient is None:
            updated = out_updated
        elif weight.ndim == 3:
            updated = adam_tiles(weight, mean_old, square_old, gradient, step_rate, decay_weight)
        else:
            updated = adam_update(weight, mean_old, square_old, gradient, step_rate, decay_weight)
        results.extend(updated)
    return tuple(results)


def solution(mesh):
    in_specs = (
        P(None, "seq", None),
        P(None, "seq", None),
        P(),
        P(),
        P(),
        P(),
        P(None, None, "head"),
        P(None, None, "head"),
        P(None, None, "head"),
        P(),
        P(),
        P(),
        P(None, "head"),
        P(None, "head"),
        P(None, "head"),
        P(None, "head"),
        P(None, "head"),
        P(None, "head"),
        P(),
        P(),
        P(),
        P(None, "head"),
        P(None, "head"),
        P(None, "head"),
        P("head"),
        P("head"),
        P("head"),
        P(None, "head"),
        P(None, "head"),
        P(None, "head"),
    )
    out_specs = (
        P(None, "seq", None),
        P(None, "seq", None),
        P(),
        P(),
        P(),
        P(None, None, "head"),
        P(None, None, "head"),
        P(None, None, "head"),
        P(),
        P(),
        P(),
        P(None, "head"),
        P(None, "head"),
        P(None, "head"),
        P(None, "head"),
        P(None, "head"),
        P(None, "head"),
        P(),
        P(),
        P(),
        P(None, "head"),
        P(None, "head"),
        P(None, "head"),
        P("head"),
        P("head"),
        P("head"),
        P(None, "head"),
        P(None, "head"),
        P(None, "head"),
    )
    return jax.shard_map(shards, mesh=mesh, in_specs=in_specs, out_specs=out_specs, check_vma=False)
```

```python
import functools

import jax
import jax.numpy as jnp
from jax import lax
from jax.experimental import pallas as pl
from jax.experimental.pallas import tpu as pltpu
from jax.sharding import PartitionSpec as P

INNER = 2048
CONV = 4
CHUNK = 128
GROUP = 2
STEP = 7


EPS = 1e-05
BETA_ONE = 0.9
BETA_TWO = 0.95
ADAM_EPS = 1e-08
LEARNING_RATES = (0.6, 0.09, 0.09, 0.09, 0.9, 0.9, 0.9, 0.6, 0.06)
WEIGHT_DECAYS = (0.0, 0.1, 0.1, 0.1, 0.0, 0.0, 0.0, 0.0, 0.1)
HIGHEST_PREC = lax.Precision.HIGHEST
F32 = jnp.float32
BF16 = jnp.bfloat16


def passed_along(block, axis, distance):
    devices = range(lax.axis_size(axis))
    route = [(i - distance, i) for i in devices if i - distance in devices]
    return lax.ppermute(block, axis, route)


def swapped(block, axis, mask):
    return lax.ppermute(block, axis, [(i, i ^ mask) for i in range(lax.axis_size(axis))])


def doubling_sum(part, axis):
    for k in range(lax.axis_size(axis).bit_length() - 1):
        part = part + swapped(part, axis, 1 << k)
    return part


def axis_masks(axis):
    return [1 << k for k in range(lax.axis_size(axis).bit_length() - 1)]


def near_bit(axis, mask):
    return (lax.axis_index(axis) // mask) % 2


def added(a, b):
    return (a.astype(F32) + b.astype(F32)).astype(BF16)


def halved(part, axis):
    for mask in axis_masks(axis)[:-1]:
        bit = near_bit(axis, mask)
        halves = part.reshape((2, part.shape[0] // 2) + part.shape[1:])
        sent = lax.dynamic_index_in_dim(halves, 1 - bit, 0, keepdims=False)
        kept = lax.dynamic_index_in_dim(halves, bit, 0, keepdims=False)
        part = added(kept, swapped(sent, axis, mask))
    return part


def joined(part, got, bit):
    first = jnp.where(bit == 0, part, got)
    second = jnp.where(bit == 0, got, part)
    return jnp.concatenate([first, second], axis=0)


def regathered(part, axis):
    masks = axis_masks(axis)[:-1]
    for mask in reversed(masks[1:]):
        part = joined(part, swapped(part, axis, mask), near_bit(axis, mask))
    return part, swapped(part, axis, masks[0])


def halving_sum(part, axis):
    part = halved(part, axis)
    part = added(part, swapped(part, axis, axis_masks(axis)[-1]))
    part, other = regathered(part, axis)
    return joined(part, other, near_bit(axis, 1))


def exchanged(blocks, axis):
    return lax.all_to_all(blocks, axis, 0, 0, tiled=True)


def to_blocks(state, count):
    return state.astype(BF16).reshape(count, -1, state.shape[-1])


def states_before(packed, height, axis):
    size = lax.axis_size(axis)
    got = exchanged(packed, axis).astype(F32)
    decays = got[:, height : height + 1] + got[:, height + 1 : height + 2]
    entering = [jnp.zeros(got[0, :height].shape, F32)]
    for k in range(size - 1):
        entering.append(decays[k] * entering[-1] + got[k, :height])
    return exchanged(jnp.stack(entering).astype(BF16), axis), decays


def states_after(state, decays, axis):
    size = lax.axis_size(axis)
    got = exchanged(to_blocks(state, size), axis).astype(F32)
    leaving = [jnp.zeros(got[0].shape, F32)]
    for k in range(size - 1, 0, -1):
        leaving.append(decays[k] * leaving[-1] + got[k])
    return exchanged(jnp.stack(leaving[::-1]).astype(BF16), axis)


def lane_tiles(a):
    rows, two, columns = a.shape
    return a.reshape(rows, two, columns // 128, 128).transpose(0, 2, 1, 3).reshape(rows, -1, 128)


def from_lane_tiles(a, shape):
    rows, two, columns = shape
    return a.reshape(rows, columns // 128, two, 128).transpose(0, 2, 1, 3).reshape(shape)


def dot(a, b, dims=((1,), (0,)), precision=None):
    return lax.dot_general(a, b, (dims, ((), ())), precision=precision, preferred_element_type=F32)


def alternately(bodies):
    bodies = list(bodies)
    while bodies:
        bodies = [body for body in bodies if next(body, bodies) is not bodies]


def expander(heads, width):
    row = lax.broadcasted_iota(jnp.int32, (heads, heads * width), 0)
    column = lax.broadcasted_iota(jnp.int32, (heads, heads * width), 1)
    inside = (column >= row * width) & (column < (row + 1) * width)
    return jnp.where(inside, 1.0, 0.0).astype(BF16)


def split_dot(a, b, dims):
    high = a.astype(BF16)
    low = (a - high.astype(F32)).astype(BF16)
    return dot(high, b, dims) + dot(low, b, dims)


def spread(a, expand):
    return split_dot(a, expand, ((1,), (0,)))


def head_sums(a, expand):
    return split_dot(a, expand, ((1,), (1,)))


def pair_rows(a):
    lane = lax.broadcasted_iota(jnp.int32, a.shape, 1)
    first = lane < a.shape[1] // 2
    zero = jnp.zeros_like(a)
    return jnp.concatenate([jnp.where(first, a, zero), jnp.where(first, zero, a)], axis=0)


def chunk_decays(decay):
    q = decay.shape[0]
    row = lax.broadcasted_iota(jnp.int32, (q, q), 0)
    column = lax.broadcasted_iota(jnp.int32, (q, q), 1)
    lower = jnp.where(row >= column, 1.0, 0.0).astype(F32)
    cum = dot(lower, decay, precision=HIGHEST_PREC)
    cum_t = dot(decay, lower, ((0,), (1,)), precision=HIGHEST_PREC)
    return cum, cum_t, row, column


def scan_kernel(x_ref, b_ref, c_ref, step_ref, decay_ref, enter_ref, y_ref, in_ref, state):
    group, _, heads = step_ref.shape
    width = x_ref.shape[2] // heads

    @pl.when(pl.program_id(1) == 0)
    def _():
        state[...] = enter_ref[...].astype(F32)

    expand = expander(heads, width)

    def body(i):
        cum, cum_t, row, column = chunk_decays(decay_ref[i])
        causal = row >= column
        q = cum.shape[0]
        total = cum[q - 1 : q, :]
        b, c = b_ref[i], c_ref[i]
        x = x_ref[i].astype(F32)
        step = step_ref[i]
        yield
        xs = (x * spread(step, expand)).astype(BF16)
        grown = spread(jnp.exp(cum), expand)
        xw = (x * spread(step * jnp.exp(total - cum), expand)).astype(BF16)
        yield
        scores = dot(c, b, ((1,), (1,)))
        before = state[i]
        in_ref[i, 0] = before
        from_state = grown * dot(c, before.astype(BF16))
        yield
        for pair in range(heads // 2):
            lanes = slice(pair * 2 * width, (pair + 1) * 2 * width)
            mixing = []
            for h in (2 * pair, 2 * pair + 1):
                between = cum[:, h : h + 1] - cum_t[h : h + 1, :]
                mixing.append((jnp.exp(jnp.where(causal, between, -1e30)) * scores).astype(BF16))
            within = dot(jnp.concatenate(mixing, axis=1), pair_rows(xs[:, lanes]))
            y_ref[i, :, lanes] = within + from_state[:, lanes]
            yield
        state[i] = grown[q - 1 : q, :] * before + dot(b, xw, ((0,), (0,)))

    alternately(body(i) for i in range(group))


def conv_back_step(act_grad, mixed, previous, taps, after):
    q = mixed.shape[0]
    shifted = conv_windows(mixed, previous)
    convolved = taps[CONV : CONV + 1]
    for k in range(CONV):
        convolved = convolved + taps[k : k + 1] * shifted[k]
    conv_grad = act_grad * silu_slope(convolved)
    extended = jnp.concatenate([conv_grad, after], axis=0)
    mixed_grad = taps[CONV - 1 : CONV] * conv_grad
    for k in range(CONV - 1):
        mixed_grad = mixed_grad + taps[k : k + 1] * extended[CONV - 1 - k : CONV - 1 - k + q]
    sums = [jnp.sum(conv_grad * part, axis=0, keepdims=True) for part in shifted]
    sums.append(jnp.sum(conv_grad, axis=0, keepdims=True))
    sums.append(jnp.zeros((8 - CONV - 1, mixed.shape[1]), F32))
    return conv_grad, mixed_grad, jnp.concatenate(sums, axis=0)


def rows_before(edge_ref, previous_ref, i, chunk):
    first = pl.program_id(1) == chunk
    return jnp.where(first, edge_ref[i].astype(F32), previous_ref[i].astype(F32))[8:]


def back_kernel(
    x_ref, b_ref, c_ref, step_ref, decay_ref, skip_ref, dy_ref, y_ref, in_ref, leave_ref,
    mixed_ref, previous_ref, edge_ref, taps_ref, slope_ref, rate_ref,
    mixed_grad_ref, dbc_ref, pre_ref, first_ref, last_ref, tap_sums_ref, head_sums_ref,
    grad, after
):
    group, _, heads = step_ref.shape
    width = x_ref.shape[2] // heads
    start = (pl.program_id(0) == 0) & (pl.program_id(1) == 0)

    @pl.when(start)
    def _():
        tap_sums_ref[...] = jnp.zeros_like(tap_sums_ref)
        head_sums_ref[...] = jnp.zeros_like(head_sums_ref)

    @pl.when(pl.program_id(1) == 0)
    def _():
        after[...] = jnp.zeros_like(after)
        grad[...] = leave_ref[...].astype(F32)

    expand = expander(heads, width)
    last_chunk = pl.program_id(1) == 0

    def body(i):
        cum, cum_t, row, column = chunk_decays(decay_ref[i])
        later = column >= row
        q = cum.shape[0]
        total = cum[q - 1 : q, :]
        b, c = b_ref[i], c_ref[i]
        x = x_ref[i].astype(F32)
        step_wide = spread(step_ref[i], expand)
        yield
        xs = (x * step_wide).astype(BF16)
        grown = spread(jnp.exp(cum), expand)
        waned = spread(jnp.exp(total - cum), expand)
        yield
        xw = (x * step_wide * waned).astype(BF16)
        dy = dy_ref[i]
        dy_low = dy.astype(BF16)
        edy = (dy * grown).astype(BF16)
        before = in_ref[i, 0]
        after_grad = grad[i]
        after_low = after_grad.astype(BF16)
        yield
        scores_t = dot(b, c, ((1,), (1,)))
        v_state = waned * dot(b, after_low)
        dscores_t = jnp.zeros((q, q), F32)
        v_parts = []
        yield
        for pair in range(heads // 2):
            lanes = slice(pair * 2 * width, (pair + 1) * 2 * width)
            dy_pair = pair_rows(dy_low[:, lanes])
            xs_pair = pair_rows(xs[:, lanes])
            dmix = dot(xs_pair, dy_low[:, lanes], ((1,), (1,)))
            mixing = []
            for k, h in enumerate((2 * pair, 2 * pair + 1)):
                between = cum_t[h : h + 1, :] - cum[:, h : h + 1]
                fade = jnp.exp(jnp.where(later, between, -1e30))
                mixing.append((fade * scores_t).astype(BF16))
                dscores_t = dscores_t + fade * dmix[k * q : (k + 1) * q]
            v_parts.append(dot(jnp.concatenate(mixing, axis=1), dy_pair))
            yield
        v = jnp.concatenate(v_parts, axis=1) + v_state
        xs_wide = xs.astype(F32)
        etotal = grown[q - 1 : q, :]
        end_row = jnp.sum(xs_wide * v_state, axis=0, keepdims=True) + jnp.sum(
            etotal * before * after_grad, axis=0, keepdims=True
        )
        crossing = dy_low.astype(F32) * y_ref[i] - xs_wide * v
        last = lax.broadcasted_iota(jnp.int32, crossing.shape, 0) == q - 1
        crossing = crossing + jnp.where(last, end_row, 0.0)
        upper = jnp.where(column >= row, 1.0, 0.0).astype(F32)
        yield
        decay_grad = dot(upper, head_sums(crossing, expand), precision=HIGHEST_PREC)
        pre_grad = (head_sums(x * v, expand) - rate_ref[...] * decay_grad) * slope_ref[i]
        pre_ref[i] = pre_grad.astype(BF16)
        sums = [
            jnp.sum(decay_grad * decay_ref[i], axis=0, keepdims=True),
            jnp.sum(pre_grad, axis=0, keepdims=True),
            jnp.sum(head_sums(x * dy, expand), axis=0, keepdims=True),
            jnp.zeros((5, heads), F32),
        ]
        head_sums_ref[...] += jnp.concatenate(sums, axis=0)
        yield
        dscores_low = dscores_t.astype(BF16)
        state = b.shape[1]
        dbc_ref[i, :, :state] = (
            dot(dscores_low, c) + dot(xw, after_low, ((1,), (1,)))
        ).astype(BF16)
        dbc_ref[i, :, state:] = (
            dot(dscores_low, b, ((0,), (0,))) + dot(edy, before.astype(BF16), ((1,), (1,)))
        ).astype(BF16)
        grad[i] = etotal * after_grad + dot(c, edy, ((0,), (0,)))
        yield
        dx = step_wide * v + skip_ref[0] * dy
        previous = rows_before(edge_ref, previous_ref, i, pl.num_programs(1) - 1)
        conv_grad, mixed_grad, tap_sums = conv_back_step(
            dx, mixed_ref[i].astype(F32), previous, taps_ref[...], after[i]
        )
        mixed_grad_ref[i] = mixed_grad.astype(BF16)
        first_ref[i] = conv_grad[:8]
        after[i] = conv_grad[:8]
        last_ref[i] = jnp.where(last_chunk, mixed_grad[q - 8 :], last_ref[i])
        tap_sums_ref[...] += tap_sums

    alternately(body(i) for i in range(group))


def act_blocks(inner, state, place):
    def part(lanes, at):
        return pl.BlockSpec((GROUP, CHUNK, lanes), lambda s, k: (s, place(k), at))

    return [part(inner, 0), part(state, inner // state), part(state, inner // state + 1)]


def conv_windows(mixed, previous):
    q = mixed.shape[0]
    window = jnp.concatenate([previous, mixed], axis=0)
    return [window[8 - CONV + 1 + k : 8 - CONV + 1 + k + q] for k in range(CONV)]


def first_kernel(
    mixed_ref, previous_ref, edge_ref, taps_ref, step_ref, decay_ref, act_ref, packed_ref, state, total
):
    chunk = pl.program_id(1)
    group, _, heads = step_ref.shape
    state_width, inner = state.shape[1:]

    @pl.when(chunk == 0)
    def _():
        state[...] = jnp.zeros_like(state)
        total[...] = jnp.zeros_like(total)

    expand = expander(heads, inner // heads)

    def body(i):
        previous = rows_before(edge_ref, previous_ref, i, 0)
        cum = chunk_decays(decay_ref[i])[0]
        q = cum.shape[0]
        last = cum[q - 1 : q, :]
        yield
        weights = spread(step_ref[i] * jnp.exp(last - cum), expand)
        kept = spread(jnp.exp(cum), expand)[q - 1 : q]
        yield
        convolved = taps_ref[CONV : CONV + 1]
        for k, part in enumerate(conv_windows(mixed_ref[i].astype(F32), previous)):
            convolved = convolved + taps_ref[k : k + 1] * part
        activated = jax.nn.silu(convolved).astype(BF16)
        act_ref[i] = activated
        yield
        xw = (activated[:, :inner].astype(F32) * weights).astype(BF16)
        b = activated[:, inner : inner + state_width]
        state[i] = kept * state[i] + dot(b, xw, ((0,), (0,)))
        total[i] = total[i] + last

    alternately(body(i) for i in range(group))

    @pl.when(chunk == pl.num_programs(1) - 1)
    def _():
        height = packed_ref.shape[2] - 16
        for i in range(group):
            decay = spread(jnp.exp(jnp.broadcast_to(total[i], (8, heads))), expand)[:1]
            high = decay.astype(BF16).astype(F32)
            tail = jnp.concatenate([high, decay - high, jnp.zeros((14, inner), F32)], axis=0)
            for part in range(packed_ref.shape[1]):
                rows = state[i, part * height : (part + 1) * height]
                packed_ref[i, part] = jnp.concatenate([rows, tail], axis=0).astype(BF16)


def conv_forward(mixed, edge, taps, step, decay, state, parts):
    seqs, length, lanes = mixed.shape
    heads, inner = step.shape[2], lanes - 2 * state
    chunks, tall = length // CHUNK, CHUNK // 16
    height = state // parts + 16

    def block(width):
        return pl.BlockSpec((GROUP, CHUNK, width), lambda s, k: (s, k, 0))

    return pl.pallas_call(
        first_kernel,
        grid=(seqs // GROUP, chunks),
        in_specs=[
            block(lanes),
            pl.BlockSpec((GROUP, 16, lanes), lambda s, k: (s, jnp.maximum(k * tall - 1, 0), 0)),
            pl.BlockSpec((GROUP, 16, lanes), lambda s, k: (s, 0, 0)),
            pl.BlockSpec((8, lanes), lambda s, k: (0, 0)),
            block(heads),
            block(heads),
        ],
        out_specs=[
            block(lanes),
            pl.BlockSpec((GROUP, parts, height, inner), lambda s, k: (s, 0, 0, 0)),
        ],
        out_shape=[
            jax.ShapeDtypeStruct(mixed.shape, BF16),
            jax.ShapeDtypeStruct((seqs, parts, height, inner), BF16),
        ],
        scratch_shapes=[pltpu.VMEM((GROUP, state, inner), F32), pltpu.VMEM((GROUP, 1, heads), F32)],
        compiler_params=pltpu.CompilerParams(vmem_limit_bytes=40 << 20),
        cost_estimate=load(9),
    )(mixed, mixed, edge, taps, step, decay)


def scan_forward(activated, step, decay, enter):
    seqs, length, heads = step.shape
    state, inner = enter.shape[1:]
    chunks = length // CHUNK

    def block(lanes):
        return pl.BlockSpec((GROUP, CHUNK, lanes), lambda s, k: (s, k, 0))

    return pl.pallas_call(
        scan_kernel,
        grid=(seqs // GROUP, chunks),
        in_specs=act_blocks(inner, state, lambda k: k)
        + [
            block(heads),
            block(heads),
            pl.BlockSpec((GROUP, state, inner), lambda s, k: (s, 0, 0)),
        ],
        out_specs=[
            block(inner),
            pl.BlockSpec((GROUP, 1, state, inner), lambda s, k: (s, k, 0, 0)),
        ],
        out_shape=[
            jax.ShapeDtypeStruct((seqs, length, inner), F32),
            jax.ShapeDtypeStruct((seqs, chunks, state, inner), F32),
        ],
        scratch_shapes=[pltpu.VMEM((GROUP, state, inner), F32)],
        compiler_params=pltpu.CompilerParams(vmem_limit_bytes=40 << 20),
        cost_estimate=load(13),
    )(activated, activated, activated, step, decay, enter)


def conv_blocks(chunks, lanes, at):
    tall = CHUNK // 16
    return [
        pl.BlockSpec((GROUP, CHUNK, lanes), lambda s, k, *_: (s, chunks - 1 - k, at)),
        pl.BlockSpec(
            (GROUP, 16, lanes), lambda s, k, *_: (s, jnp.maximum((chunks - 1 - k) * tall - 1, 0), at)
        ),
        pl.BlockSpec((GROUP, 16, lanes), lambda s, k, *_: (s, 0, at)),
        pl.BlockSpec((8, lanes), lambda s, k, *_: (0, at)),
    ]


def conv_outs(seqs, chunks, lanes):
    specs = [
        pl.BlockSpec((GROUP, CHUNK, lanes), lambda s, k, *_: (s, chunks - 1 - k, 0)),
        pl.BlockSpec((GROUP, 8, lanes), lambda s, k, *_: (s, 0, 0)),
        pl.BlockSpec((GROUP, 8, lanes), lambda s, k, *_: (s, 0, 0)),
        pl.BlockSpec((8, lanes), lambda s, k, *_: (0, 0)),
    ]
    shapes = [
        jax.ShapeDtypeStruct((seqs, chunks * CHUNK, lanes), BF16),
        jax.ShapeDtypeStruct((seqs, 8, lanes), F32),
        jax.ShapeDtypeStruct((seqs, 8, lanes), F32),
        jax.ShapeDtypeStruct((8, lanes), F32),
    ]
    return specs, shapes


def scan_backward(
    activated, step, decay, skip, dy, y, states, leave, mixed, edge, taps, slope, rate
):
    seqs, length, heads = step.shape
    state, inner = leave.shape[1:]
    chunks = length // CHUNK

    def block(lanes):
        return pl.BlockSpec((GROUP, CHUNK, lanes), lambda s, k: (s, chunks - 1 - k, 0))

    conv_specs, conv_shapes = conv_outs(seqs, chunks, inner)
    return pl.pallas_call(
        back_kernel,
        grid=(seqs // GROUP, chunks),
        in_specs=act_blocks(inner, state, lambda k: chunks - 1 - k)
        + [
            block(heads),
            block(heads),
            pl.BlockSpec((1, 1, inner), lambda s, k: (0, 0, 0)),
            block(inner),
            block(inner),
            pl.BlockSpec((GROUP, 1, state, inner), lambda s, k: (s, chunks - 1 - k, 0, 0)),
            pl.BlockSpec((GROUP, state, inner), lambda s, k: (s, 0, 0)),
        ]
        + conv_blocks(chunks, inner, 0)
        + [block(heads), pl.BlockSpec((1, heads), lambda s, k: (0, 0))],
        out_specs=[conv_specs[0], block(2 * state), block(heads)]
        + conv_specs[1:]
        + [pl.BlockSpec((8, heads), lambda s, k: (0, 0))],
        out_shape=[
            conv_shapes[0],
            jax.ShapeDtypeStruct((seqs, length, 2 * state), BF16),
            jax.ShapeDtypeStruct((seqs, length, heads), BF16),
        ]
        + conv_shapes[1:]
        + [jax.ShapeDtypeStruct((8, heads), F32)],
        scratch_shapes=[pltpu.VMEM((GROUP, state, inner), F32), pltpu.VMEM((GROUP, 8, inner), F32)],
        compiler_params=pltpu.CompilerParams(vmem_limit_bytes=40 << 20),
        cost_estimate=load(30),
    )(
        activated, activated, activated, step, decay, skip, dy, y, states, leave,
        mixed, mixed, edge, taps, slope, rate
    )


def bc_kernel(
    scalars_ref, part_ref, got_ref, mixed_ref, previous_ref, edge_ref, taps_ref,
    mixed_grad_ref, first_ref, last_ref, tap_sums_ref, after
):
    group, q, _ = mixed_ref.shape
    last_chunk = pl.program_id(1) == 0
    start = (pl.program_id(0) == 0) & last_chunk

    @pl.when(start)
    def _():
        tap_sums_ref[...] = jnp.zeros_like(tap_sums_ref)

    @pl.when(last_chunk)
    def _():
        after[...] = jnp.zeros_like(after)

    act_grad = picked(scalars_ref, part_ref, got_ref)

    def body(i):
        previous = rows_before(edge_ref, previous_ref, i, pl.num_programs(1) - 1)
        yield
        conv_grad, mixed_grad, tap_sums = conv_back_step(
            act_grad[i], mixed_ref[i].astype(F32), previous, taps_ref[...], after[i]
        )
        mixed_grad_ref[i] = mixed_grad.astype(BF16)
        first_ref[i] = conv_grad[:8]
        after[i] = conv_grad[:8]
        last_ref[i] = jnp.where(last_chunk, mixed_grad[q - 8 :], last_ref[i])
        tap_sums_ref[...] += tap_sums

    alternately(body(i) for i in range(group))


def bc_backward(scalars, part, got, mixed, edge, taps):
    seqs, length, _ = mixed.shape
    lanes = part.shape[1]
    chunks, at = length // CHUNK, mixed.shape[2] // lanes - 1
    halves = seqs // 2 // GROUP
    half = pl.BlockSpec((GROUP, CHUNK, lanes), lambda s, k, _: (s % halves, chunks - 1 - k, 0))
    conv_specs, conv_shapes = conv_outs(seqs, chunks, lanes)
    return pl.pallas_call(
        bc_kernel,
        grid_spec=pltpu.PrefetchScalarGridSpec(
            num_scalar_prefetch=1,
            grid=(seqs // GROUP, chunks),
            in_specs=[half, half] + conv_blocks(chunks, lanes, at),
            out_specs=conv_specs,
            scratch_shapes=[pltpu.VMEM((GROUP, 8, lanes), F32)],
        ),
        out_shape=conv_shapes,
        compiler_params=pltpu.CompilerParams(vmem_limit_bytes=40 << 20),
        cost_estimate=load(5),
    )(
        scalars,
        part.reshape(seqs // 2, length, lanes),
        got.reshape(seqs // 2, length, lanes),
        mixed,
        mixed,
        edge,
        taps,
    )


def joined_edges(mixed_grad, first, last, taps):
    rows = []
    for j in range(CONV - 1):
        rows.append(sum(taps[k] * first[:, j - k] for k in range(j + 1)))
    edge_grad = passed_along(jnp.stack(rows, axis=1), "seq", -1)
    fixed = last + jnp.pad(edge_grad, ((0, 0), (8 - CONV + 1, 0), (0, 0)))
    return lax.dynamic_update_slice(mixed_grad, fixed.astype(BF16), (0, mixed_grad.shape[1] - 8, 0))


def normed_kernel(gate_ref, x_ref, step_ref, z_weight_ref, x_weight_ref, step_weight_ref, out_ref):
    nt = ((1,), (1,))
    total = dot(gate_ref[...], z_weight_ref[...], nt) + dot(x_ref[...], x_weight_ref[...], nt)
    out_ref[...] = (total + dot(step_ref[...], step_weight_ref[...], nt)).astype(BF16)


def normed_products(gate_grad, x_grad, step_grad, z_weight, x_weight, step_weight):
    rows, width = gate_grad.shape[0], z_weight.shape[0]

    def block(a):
        return pl.BlockSpec((ROWS, a.shape[1]), lambda i: (i, 0))

    def whole(a):
        return pl.BlockSpec(a.shape, lambda i: (0, 0))

    args = (gate_grad, x_grad, step_grad, z_weight, x_weight, step_weight)
    return pl.pallas_call(
        normed_kernel,
        grid=(rows // ROWS,),
        in_specs=[block(a) for a in args[:3]] + [whole(a) for a in args[3:]],
        out_specs=pl.BlockSpec((ROWS, width), lambda i: (i, 0)),
        out_shape=jax.ShapeDtypeStruct((rows, width), BF16),
        compiler_params=pltpu.CompilerParams(vmem_limit_bytes=40 << 20),
        cost_estimate=load(6),
    )(*args)


def picked(scalars_ref, part_ref, got_ref):
    bit = scalars_ref[scalars_ref.shape[0] - 1]
    half = pl.num_programs(0) // 2
    own = (pl.program_id(0) // half) == bit
    return jnp.where(own, part_ref[...].astype(F32), got_ref[...].astype(F32))


def out_kernel(scalars_ref, part_ref, got_ref, tokens_ref, scale_ref, out_ref):
    projected = picked(scalars_ref, part_ref, got_ref)
    out_ref[...] = (tokens_ref[...].astype(F32) + scale_ref[...] * projected).astype(BF16)


def tail_kernel(
    local_len, scalars_ref, part_ref, got_ref, bc_ref, weight_ref, tokens_ref, back_ref, gain_ref,
    out_ref, gain_grad_ref
):
    step = pl.program_id(0)
    height = tokens_ref.shape[0]
    normed_grad = picked(scalars_ref, part_ref, got_ref) + dot(
        bc_ref[...], weight_ref[...], ((1,), (1,))
    )
    tokens = tokens_ref[...].astype(F32)
    inverse_rms = lax.rsqrt(jnp.mean(tokens * tokens, axis=-1, keepdims=True) + EPS)
    unit = tokens * inverse_rms

    @pl.when(step == 0)
    def _():
        gain_grad_ref[...] = jnp.zeros_like(gain_grad_ref)

    gain_grad_ref[...] += jnp.sum(normed_grad * unit, axis=0, keepdims=True)
    unit_grad = normed_grad * gain_ref[...]
    along = jnp.mean(unit_grad * unit, axis=-1, keepdims=True)
    row = step * height
    length = scalars_ref[row // local_len]
    start = scalars_ref[scalars_ref.shape[0] - 2] + row % local_len
    position = start + lax.broadcasted_iota(jnp.int32, tokens.shape, 0)
    back = jnp.where(position < length, back_ref[...].astype(F32), 0.0)
    out_ref[...] = back + inverse_rms * (unit_grad - unit * along)


ROWS = 256


def load(microseconds):
    return pl.CostEstimate(flops=0, transcendentals=0, bytes_accessed=int(microseconds * 3.69e6))


def merge_call(kernel, scalars, part, got, others, other_specs, out_specs, out_shape):
    rows, width = 2 * part.shape[0], part.shape[1]
    blocks = rows // ROWS
    half = pl.BlockSpec((ROWS, width), lambda i, s: (i % (blocks // 2), 0))
    return pl.pallas_call(
        kernel,
        grid_spec=pltpu.PrefetchScalarGridSpec(
            num_scalar_prefetch=1,
            grid=(blocks,),
            in_specs=[half, half] + other_specs,
            out_specs=out_specs,
        ),
        out_shape=out_shape,
        compiler_params=pltpu.CompilerParams(vmem_limit_bytes=40 << 20),
        cost_estimate=load(8),
    )(scalars, part, got, *others)


def row_block(lanes):
    return pl.BlockSpec((ROWS, lanes), lambda i, s: (i, 0))


def whole_block(shape):
    return pl.BlockSpec(shape, lambda i, s: (0, 0))


def adam_kernel(
    step_rate, decay_weight, gradient_ref, weight_ref, mean_ref, square_ref,
    mean_out, square_out, weight_out
):
    mean_out[...], square_out[...], weight_out[...] = adam_update(
        weight_ref[...],
        mean_ref[...],
        square_ref[...],
        gradient_ref[...].astype(F32),
        step_rate,
        decay_weight,
    )


def adam_tiles(weight, mean_old, square_old, gradient, step_rate, decay_weight):
    rows, _, columns = weight.shape
    tiles = pl.BlockSpec((128, columns // 64, 128), lambda i: (i, 0, 0))
    updated = pl.pallas_call(
        functools.partial(adam_kernel, step_rate, decay_weight),
        grid=(rows // 128,),
        in_specs=[tiles] * 4,
        out_specs=[tiles] * 3,
        out_shape=[jax.ShapeDtypeStruct((rows, columns // 64, 128), F32)] * 3,
        compiler_params=pltpu.CompilerParams(vmem_limit_bytes=40 << 20),
        cost_estimate=load(9),
    )(*map(lane_tiles, (gradient, weight, mean_old, square_old)))
    return [from_lane_tiles(part, weight.shape) for part in updated]


def silu_slope(values):
    sigmoid_part = jax.nn.sigmoid(values)
    return sigmoid_part * (1.0 + values * (1.0 - sigmoid_part))


def adam_update(weight, mean_old, square_old, gradient, step_rate, decay_weight):
    mean_new = BETA_ONE * mean_old + (1.0 - BETA_ONE) * gradient
    square_new = BETA_TWO * square_old + (1.0 - BETA_TWO) * gradient * gradient
    corrected_mean = mean_new / (1.0 - BETA_ONE**STEP)
    corrected_square = square_new / (1.0 - BETA_TWO**STEP)
    weight_new = weight - step_rate * (
        corrected_mean / (jnp.sqrt(corrected_square) + ADAM_EPS) + decay_weight * weight
    )
    return (mean_new, square_new, weight_new)


def shards(
    inputs,
    cotangent,
    lengths,
    norm_gain,
    norm_gain_mean,
    norm_gain_square,
    proj_zx,
    proj_zx_mean,
    proj_zx_square,
    proj_bc,
    proj_bc_mean,
    proj_bc_square,
    proj_step,
    proj_step_mean,
    proj_step_square,
    conv_inner,
    conv_inner_mean,
    conv_inner_square,
    conv_bc,
    conv_bc_mean,
    conv_bc_square,
    head_params,
    head_params_mean,
    head_params_square,
    gate_gain,
    gate_gain_mean,
    gate_gain_square,
    proj_out,
    proj_out_mean,
    proj_out_square,
):
    seq_count, local_len, model_width = inputs.shape
    local_inner = proj_zx.shape[2]
    state_width = proj_bc.shape[1] // 2
    local_heads = proj_step.shape[1]
    head_width = local_inner // local_heads
    rows = seq_count * local_len
    seq_size, seq_index = lax.axis_size("seq"), lax.axis_index("seq")

    def wide(a):
        selector = jnp.repeat(jnp.eye(local_heads, dtype=F32), head_width, axis=1)
        return jnp.einsum("...h,hc->...c", a, selector, precision=HIGHEST_PREC)

    positions = seq_index * local_len + jnp.arange(local_len)
    is_valid = (positions[None, :] < lengths[:, None]).astype(F32)
    tokens = inputs.astype(F32)
    inverse_rms = lax.rsqrt(jnp.mean(tokens * tokens, axis=-1, keepdims=True) + EPS)
    unit_tokens = tokens * inverse_rms
    normed = (unit_tokens * norm_gain).astype(BF16)
    z_weight = proj_zx[:, 0].astype(BF16)
    x_weight = proj_zx[:, 1].astype(BF16)
    bc_weight = proj_bc.astype(BF16)
    step_weight = proj_step.astype(BF16)
    out_weight = proj_out.astype(BF16)
    xbc_weight = jnp.concatenate([x_weight, bc_weight], axis=1)
    mixed_in = jnp.einsum("btd,dc->btc", normed, xbc_weight, preferred_element_type=F32).astype(BF16)
    edge_in = passed_along(mixed_in[:, local_len - CONV + 1 :], "seq", 1)
    raw_step = jnp.einsum("btd,dh->bth", normed, step_weight, preferred_element_type=F32)
    gate_input = jnp.einsum("btd,dc->btc", normed, z_weight, preferred_element_type=F32)
    conv_weight = jnp.concatenate([conv_inner, conv_bc], axis=-1)
    taps = jnp.pad(conv_weight, ((0, 8 - CONV - 1), (0, 0)))
    edge_rows = jnp.pad(edge_in, ((0, 0), (16 - CONV + 1, 0), (0, 0)))
    decay_log, step_bias, skip_gain = head_params[0], head_params[1], head_params[2]
    step_size = jax.nn.softplus(raw_step + step_bias)
    log_decay = -step_size * jnp.exp(decay_log)
    parts = seq_size // seq_count
    activated, packed = conv_forward(
        mixed_in, edge_rows, taps, step_size, log_decay, state_width, parts
    )
    entering, block_decays = states_before(
        packed.reshape((seq_size,) + packed.shape[2:]), state_width // parts, "seq"
    )
    entering = entering.reshape(seq_count, state_width, local_inner)
    x_values = activated[..., :local_inner]
    c_values = activated[..., local_inner + state_width :]
    earlier = jnp.tril(jnp.ones((local_len, local_len), F32))
    running = jnp.einsum("ts,bsh->bth", earlier, log_decay, precision=HIGHEST_PREC)

    scanned_raw, states = scan_forward(activated, step_size, log_decay, entering)
    skip_wide = jnp.repeat(skip_gain, head_width)[None, None]
    scanned = scanned_raw + skip_wide * x_values.astype(F32)
    gate_act = jax.nn.silu(gate_input)
    gated_values = scanned * gate_act
    square_sum = jnp.sum(gated_values * gated_values, axis=-1)
    scaled = (gated_values * gate_gain).astype(BF16)
    partial_out = jnp.einsum("bti,di->btd", scaled, out_weight, preferred_element_type=F32)
    out_cotangent = cotangent.astype(F32) * is_valid[..., None]
    partial_scale_grad = jnp.sum(out_cotangent * partial_out, axis=-1)
    square_total, scale_grad = lax.psum(jnp.stack([square_sum, partial_scale_grad]), "head")
    out_scale = lax.rsqrt(square_total / INNER + EPS)
    proj_grad = (out_scale[..., None] * out_cotangent).astype(BF16)
    square_grad = -0.5 * scale_grad * out_scale * out_scale * out_scale / INNER
    out_weight_grad = jnp.einsum("btd,bti->di", proj_grad, scaled, preferred_element_type=F32)
    scaled_grad = jnp.einsum("btd,di->bti", proj_grad, out_weight, preferred_element_type=F32)
    gate_gain_grad = jnp.sum(scaled_grad * gated_values, axis=(0, 1))
    gated_grad = scaled_grad * gate_gain + 2.0 * gated_values * square_grad[..., None]
    scanned_grad = gated_grad * gate_act
    gate_grad = (gated_grad * scanned * silu_slope(gate_input)).astype(BF16)
    local_back = jnp.einsum(
        "btn,btc->bnc",
        c_values,
        (scanned_grad * wide(jnp.exp(running))).astype(BF16),
        preferred_element_type=F32,
    )
    leaving = states_after(local_back, block_decays, "seq")
    projected = halved(partial_out.astype(BF16).reshape(rows, model_width), "head")
    leaving, projected = lax.optimization_barrier((leaving, projected))
    leaving = leaving.reshape(local_back.shape)
    z_weight_grad = jnp.einsum("btd,btc->dc", normed, gate_grad, preferred_element_type=F32)
    early_grads = jnp.concatenate([out_weight_grad, z_weight_grad], axis=0).astype(BF16)
    early_grads, _ = lax.optimization_barrier((early_grads, leaving))
    early_parts = exchanged(to_blocks(early_grads, seq_size), "seq")
    projected_far = swapped(projected, "head", axis_masks("head")[-1])
    x_raw, bc_grad, step_in_grad, x_first, x_last, x_tap_sums, head_totals = scan_backward(
        activated,
        step_size,
        log_decay,
        skip_wide,
        scanned_grad,
        scanned_raw,
        states,
        leaving,
        mixed_in,
        edge_rows,
        taps,
        jax.nn.sigmoid(raw_step + step_bias),
        jnp.exp(decay_log)[None],
    )
    x_raw, early_parts, projected_far = lax.optimization_barrier(
        (x_raw, early_parts, projected_far)
    )
    projected_half, projected_other = regathered(added(projected, projected_far), "head")
    early_own = jnp.sum(early_parts.astype(F32), axis=0).astype(BF16)
    early_all = lax.all_gather(early_own, "seq")
    bc_sum = halved(bc_grad.reshape(rows, 2 * state_width), "head")
    x_in_grad = joined_edges(x_raw, x_first, x_last, conv_weight[:, :local_inner])
    bc_far = swapped(bc_sum, "head", axis_masks("head")[-1])
    normed_partial = normed_products(
        gate_grad.reshape(rows, local_inner),
        x_in_grad.reshape(rows, local_inner),
        step_in_grad.reshape(rows, local_heads),
        z_weight,
        x_weight,
        step_weight,
    )
    x_in_late, bc_added = lax.optimization_barrier((x_in_grad, added(bc_sum, bc_far)))
    bc_half, bc_other = regathered(bc_added, "head")
    x_weight_grad = jnp.einsum("btd,btc->dc", normed, x_in_late, preferred_element_type=F32)
    normed_sum = halved(normed_partial, "head")
    x_blocks, bc_other, _ = lax.optimization_barrier(
        (to_blocks(x_weight_grad, seq_size), bc_other, normed_sum)
    )
    x_parts = exchanged(x_blocks, "seq")
    normed_far = swapped(normed_sum, "head", axis_masks("head")[-1])

    scalars = jnp.concatenate(
        [lengths, jnp.stack([seq_index * local_len, near_bit("head", 1)]).astype(jnp.int32)]
    )
    bc_raw_grad, bc_first, bc_last, bc_tap_sums = bc_backward(
        scalars,
        bc_half,
        bc_other,
        mixed_in,
        edge_rows,
        taps,
    )
    bc_in_grad = joined_edges(bc_raw_grad, bc_first, bc_last, conv_weight[:, local_inner:])
    bc_in_grad, x_parts = lax.optimization_barrier((bc_in_grad, x_parts))
    x_own = jnp.sum(x_parts.astype(F32), axis=0).astype(BF16)
    x_all = lax.all_gather(x_own, "seq")
    x_sum = x_all.reshape(model_width, local_inner)
    bc_weight_grad = jnp.einsum("btd,btc->dc", normed, bc_in_grad, preferred_element_type=F32)
    bc_blocks = to_blocks(bc_weight_grad, seq_size)
    bc_parts = exchanged(bc_blocks, "seq")
    early_all, _ = lax.optimization_barrier((early_all, bc_blocks))
    early_sums = early_all.reshape(2, model_width, local_inner)
    flat_tokens = inputs.reshape(rows, model_width)
    block_out = merge_call(
        out_kernel,
        scalars,
        projected_half,
        projected_other,
        (flat_tokens, out_scale.reshape(rows, 1)),
        [row_block(model_width), row_block(1)],
        row_block(model_width),
        jax.ShapeDtypeStruct((rows, model_width), BF16),
    )
    out_updated = adam_update(
        proj_out,
        proj_out_mean,
        proj_out_square,
        early_sums[0].astype(F32),
        LEARNING_RATES[-1],
        WEIGHT_DECAYS[-1],
    )
    normed_far, block_out, out_updated, _ = lax.optimization_barrier(
        (normed_far, block_out, out_updated, bc_blocks)
    )
    block_out = block_out.reshape(inputs.shape)
    normed_added = added(normed_sum, normed_far)
    bc_parts, _ = lax.optimization_barrier((bc_parts, normed_added))
    normed_half, normed_other = regathered(normed_added, "head")
    input_grad, norm_gain_grad = merge_call(
        functools.partial(tail_kernel, local_len),
        scalars,
        normed_half,
        normed_other,
        (
            bc_in_grad.reshape(rows, 2 * state_width),
            bc_weight,
            flat_tokens,
            cotangent.reshape(rows, model_width),
            norm_gain[None],
        ),
        [
            row_block(2 * state_width),
            whole_block(bc_weight.shape),
            row_block(model_width),
            row_block(model_width),
            whole_block((1, model_width)),
        ],
        [row_block(model_width), whole_block((1, model_width))],
        [
            jax.ShapeDtypeStruct((rows, model_width), F32),
            jax.ShapeDtypeStruct((1, model_width), F32),
        ],
    )
    input_grad = input_grad.reshape(inputs.shape)
    bc_own = jnp.sum(bc_parts.astype(F32), axis=0).astype(BF16)
    bc_all = exchanged(jnp.broadcast_to(bc_own[None], bc_parts.shape), "seq")
    step_weight_grad = jnp.einsum("btd,bth->hd", normed, step_in_grad, preferred_element_type=F32)
    conv_inner_grad = x_tap_sums[: CONV + 1]
    conv_bc_grad = bc_tap_sums[: CONV + 1]
    head_grad = head_totals[:3]
    small_grads = (
        norm_gain_grad[0],
        step_weight_grad,
        conv_inner_grad,
        conv_bc_grad,
        head_grad,
        gate_gain_grad,
    )
    flat = jnp.concatenate([part.reshape(-1) for part in small_grads])
    count = flat.shape[0]
    flat = jnp.pad(flat, (0, -count % 1024)).reshape(-1, 128)
    flat = doubling_sum(flat, "seq").reshape(-1)
    small_sums, at = [], 0
    for part in small_grads:
        small_sums.append(flat[at : at + part.size].reshape(part.shape))
        at += part.size

    summed_grads = (
        small_sums[0],
        jnp.stack([early_sums[1], x_sum], axis=1),
        bc_all.reshape(bc_weight_grad.shape).astype(F32),
        small_sums[1].T,
        small_sums[2],
        small_sums[3],
        small_sums[4],
        small_sums[5],
        None,
    )
    params = (
        norm_gain,
        proj_zx,
        proj_bc,
        proj_step,
        conv_inner,
        conv_bc,
        head_params,
        gate_gain,
        proj_out,
    )
    means = (
        norm_gain_mean,
        proj_zx_mean,
        proj_bc_mean,
        proj_step_mean,
        conv_inner_mean,
        conv_bc_mean,
        head_params_mean,
        gate_gain_mean,
        proj_out_mean,
    )
    squares = (
        norm_gain_square,
        proj_zx_square,
        proj_bc_square,
        proj_step_square,
        conv_inner_square,
        conv_bc_square,
        head_params_square,
        gate_gain_square,
        proj_out_square,
    )
    results = [block_out, input_grad]
    for weight, mean_old, square_old, gradient, step_rate, decay_weight in zip(
        params, means, squares, summed_grads, LEARNING_RATES, WEIGHT_DECAYS
    ):
        if gradient is None:
            updated = out_updated
        elif weight.ndim == 3:
            updated = adam_tiles(weight, mean_old, square_old, gradient, step_rate, decay_weight)
        else:
            updated = adam_update(weight, mean_old, square_old, gradient, step_rate, decay_weight)
        results.extend(updated)
    return tuple(results)


def solution(mesh):
    in_specs = (
        P(None, "seq", None),
        P(None, "seq", None),
        P(),
        P(),
        P(),
        P(),
        P(None, None, "head"),
        P(None, None, "head"),
        P(None, None, "head"),
        P(),
        P(),
        P(),
        P(None, "head"),
        P(None, "head"),
        P(None, "head"),
        P(None, "head"),
        P(None, "head"),
        P(None, "head"),
        P(),
        P(),
        P(),
        P(None, "head"),
        P(None, "head"),
        P(None, "head"),
        P("head"),
        P("head"),
        P("head"),
        P(None, "head"),
        P(None, "head"),
        P(None, "head"),
    )
    out_specs = (
        P(None, "seq", None),
        P(None, "seq", None),
        P(),
        P(),
        P(),
        P(None, None, "head"),
        P(None, None, "head"),
        P(None, None, "head"),
        P(),
        P(),
        P(),
        P(None, "head"),
        P(None, "head"),
        P(None, "head"),
        P(None, "head"),
        P(None, "head"),
        P(None, "head"),
        P(),
        P(),
        P(),
        P(None, "head"),
        P(None, "head"),
        P(None, "head"),
        P("head"),
        P("head"),
        P("head"),
        P(None, "head"),
        P(None, "head"),
        P(None, "head"),
    )
    return jax.shard_map(shards, mesh=mesh, in_specs=in_specs, out_specs=out_specs, check_vma=False)
```

```python
import functools

import jax
import jax.numpy as jnp
from jax import lax
from jax.experimental import pallas as pl
from jax.experimental.pallas import tpu as pltpu
from jax.sharding import PartitionSpec as P

INNER = 2048
CONV = 4
CHUNK = 128
GROUP = 2
STEP = 7


EPS = 1e-05
BETA_ONE = 0.9
BETA_TWO = 0.95
ADAM_EPS = 1e-08
LEARNING_RATES = (0.6, 0.09, 0.09, 0.09, 0.9, 0.9, 0.9, 0.6, 0.06)
WEIGHT_DECAYS = (0.0, 0.1, 0.1, 0.1, 0.0, 0.0, 0.0, 0.0, 0.1)
HIGHEST_PREC = lax.Precision.HIGHEST
F32 = jnp.float32
BF16 = jnp.bfloat16


def passed_along(block, axis, distance):
    devices = range(lax.axis_size(axis))
    route = [(i - distance, i) for i in devices if i - distance in devices]
    return lax.ppermute(block, axis, route)


def swapped(block, axis, mask):
    return lax.ppermute(block, axis, [(i, i ^ mask) for i in range(lax.axis_size(axis))])


def doubling_sum(part, axis):
    for k in range(lax.axis_size(axis).bit_length() - 1):
        part = part + swapped(part, axis, 1 << k)
    return part


def axis_masks(axis):
    return [1 << k for k in range(lax.axis_size(axis).bit_length() - 1)]


def near_bit(axis, mask):
    return (lax.axis_index(axis) // mask) % 2


def added(a, b):
    return (a.astype(F32) + b.astype(F32)).astype(BF16)


def halved(part, axis):
    for mask in axis_masks(axis)[:-1]:
        bit = near_bit(axis, mask)
        halves = part.reshape((2, part.shape[0] // 2) + part.shape[1:])
        sent = lax.dynamic_index_in_dim(halves, 1 - bit, 0, keepdims=False)
        kept = lax.dynamic_index_in_dim(halves, bit, 0, keepdims=False)
        part = added(kept, swapped(sent, axis, mask))
    return part


def joined(part, got, bit):
    first = jnp.where(bit == 0, part, got)
    second = jnp.where(bit == 0, got, part)
    return jnp.concatenate([first, second], axis=0)


def regathered(part, axis):
    masks = axis_masks(axis)[:-1]
    for mask in reversed(masks[1:]):
        part = joined(part, swapped(part, axis, mask), near_bit(axis, mask))
    return part, swapped(part, axis, masks[0])


def halving_sum(part, axis):
    part = halved(part, axis)
    part = added(part, swapped(part, axis, axis_masks(axis)[-1]))
    part, other = regathered(part, axis)
    return joined(part, other, near_bit(axis, 1))


def exchanged(blocks, axis):
    return lax.all_to_all(blocks, axis, 0, 0, tiled=True)


def to_blocks(state, count):
    return state.astype(BF16).reshape(count, -1, state.shape[-1])


def states_before(packed, height, axis):
    size = lax.axis_size(axis)
    got = exchanged(packed, axis).astype(F32)
    decays = got[:, height : height + 1] + got[:, height + 1 : height + 2]
    entering = [jnp.zeros(got[0, :height].shape, F32)]
    for k in range(size - 1):
        entering.append(decays[k] * entering[-1] + got[k, :height])
    return exchanged(jnp.stack(entering).astype(BF16), axis), decays


def states_after(state, decays, axis):
    size = lax.axis_size(axis)
    got = exchanged(to_blocks(state, size), axis).astype(F32)
    leaving = [jnp.zeros(got[0].shape, F32)]
    for k in range(size - 1, 0, -1):
        leaving.append(decays[k] * leaving[-1] + got[k])
    return exchanged(jnp.stack(leaving[::-1]).astype(BF16), axis)


def lane_tiles(a):
    rows, two, columns = a.shape
    return a.reshape(rows, two, columns // 128, 128).transpose(0, 2, 1, 3).reshape(rows, -1, 128)


def from_lane_tiles(a, shape):
    rows, two, columns = shape
    return a.reshape(rows, columns // 128, two, 128).transpose(0, 2, 1, 3).reshape(shape)


def dot(a, b, dims=((1,), (0,)), precision=None):
    return lax.dot_general(a, b, (dims, ((), ())), precision=precision, preferred_element_type=F32)


def alternately(bodies):
    bodies = list(bodies)
    while bodies:
        bodies = [body for body in bodies if next(body, bodies) is not bodies]


def expander(heads, width):
    row = lax.broadcasted_iota(jnp.int32, (heads, heads * width), 0)
    column = lax.broadcasted_iota(jnp.int32, (heads, heads * width), 1)
    inside = (column >= row * width) & (column < (row + 1) * width)
    return jnp.where(inside, 1.0, 0.0).astype(BF16)


def split_dot(a, b, dims):
    high = a.astype(BF16)
    low = (a - high.astype(F32)).astype(BF16)
    return dot(high, b, dims) + dot(low, b, dims)


def spread(a, expand):
    return split_dot(a, expand, ((1,), (0,)))


def head_sums(a, expand):
    return split_dot(a, expand, ((1,), (1,)))


def pair_rows(a):
    lane = lax.broadcasted_iota(jnp.int32, a.shape, 1)
    first = lane < a.shape[1] // 2
    zero = jnp.zeros_like(a)
    return jnp.concatenate([jnp.where(first, a, zero), jnp.where(first, zero, a)], axis=0)


def chunk_decays(decay):
    q = decay.shape[0]
    row = lax.broadcasted_iota(jnp.int32, (q, q), 0)
    column = lax.broadcasted_iota(jnp.int32, (q, q), 1)
    lower = jnp.where(row >= column, 1.0, 0.0).astype(F32)
    cum = dot(lower, decay, precision=HIGHEST_PREC)
    cum_t = dot(decay, lower, ((0,), (1,)), precision=HIGHEST_PREC)
    return cum, cum_t, row, column


def scan_kernel(x_ref, b_ref, c_ref, step_ref, decay_ref, enter_ref, y_ref, in_ref, state):
    group, _, heads = step_ref.shape
    width = x_ref.shape[2] // heads

    @pl.when(pl.program_id(1) == 0)
    def _():
        state[...] = enter_ref[...].astype(F32)

    expand = expander(heads, width)

    def body(i):
        cum, cum_t, row, column = chunk_decays(decay_ref[i])
        causal = row >= column
        q = cum.shape[0]
        total = cum[q - 1 : q, :]
        b, c = b_ref[i], c_ref[i]
        x = x_ref[i].astype(F32)
        step = step_ref[i]
        yield
        xs = (x * spread(step, expand)).astype(BF16)
        grown = spread(jnp.exp(cum), expand)
        xw = (x * spread(step * jnp.exp(total - cum), expand)).astype(BF16)
        yield
        scores = dot(c, b, ((1,), (1,)))
        before = state[i]
        in_ref[i, 0] = before
        from_state = grown * dot(c, before.astype(BF16))
        yield
        for pair in range(heads // 2):
            lanes = slice(pair * 2 * width, (pair + 1) * 2 * width)
            mixing = []
            for h in (2 * pair, 2 * pair + 1):
                between = cum[:, h : h + 1] - cum_t[h : h + 1, :]
                mixing.append((jnp.exp(jnp.where(causal, between, -1e30)) * scores).astype(BF16))
            within = dot(jnp.concatenate(mixing, axis=1), pair_rows(xs[:, lanes]))
            y_ref[i, :, lanes] = within + from_state[:, lanes]
            yield
        state[i] = grown[q - 1 : q, :] * before + dot(b, xw, ((0,), (0,)))

    alternately(body(i) for i in range(group))


def conv_back_step(act_grad, mixed, previous, taps, after):
    q = mixed.shape[0]
    shifted = conv_windows(mixed, previous)
    convolved = taps[CONV : CONV + 1]
    for k in range(CONV):
        convolved = convolved + taps[k : k + 1] * shifted[k]
    conv_grad = act_grad * silu_slope(convolved)
    extended = jnp.concatenate([conv_grad, after], axis=0)
    mixed_grad = taps[CONV - 1 : CONV] * conv_grad
    for k in range(CONV - 1):
        mixed_grad = mixed_grad + taps[k : k + 1] * extended[CONV - 1 - k : CONV - 1 - k + q]
    sums = [jnp.sum(conv_grad * part, axis=0, keepdims=True) for part in shifted]
    sums.append(jnp.sum(conv_grad, axis=0, keepdims=True))
    sums.append(jnp.zeros((8 - CONV - 1, mixed.shape[1]), F32))
    return conv_grad, mixed_grad, jnp.concatenate(sums, axis=0)


def rows_before(edge_ref, previous_ref, i, chunk):
    first = pl.program_id(1) == chunk
    return jnp.where(first, edge_ref[i].astype(F32), previous_ref[i].astype(F32))[8:]


def back_kernel(
    x_ref, b_ref, c_ref, step_ref, decay_ref, skip_ref, dy_ref, y_ref, in_ref, leave_ref,
    mixed_ref, previous_ref, edge_ref, taps_ref, slope_ref, rate_ref,
    mixed_grad_ref, dbc_ref, pre_ref, first_ref, last_ref, tap_sums_ref, head_sums_ref,
    grad, after
):
    group, _, heads = step_ref.shape
    width = x_ref.shape[2] // heads
    start = (pl.program_id(0) == 0) & (pl.program_id(1) == 0)

    @pl.when(start)
    def _():
        tap_sums_ref[...] = jnp.zeros_like(tap_sums_ref)
        head_sums_ref[...] = jnp.zeros_like(head_sums_ref)

    @pl.when(pl.program_id(1) == 0)
    def _():
        after[...] = jnp.zeros_like(after)
        grad[...] = leave_ref[...].astype(F32)

    expand = expander(heads, width)
    last_chunk = pl.program_id(1) == 0

    def body(i):
        cum, cum_t, row, column = chunk_decays(decay_ref[i])
        later = column >= row
        q = cum.shape[0]
        total = cum[q - 1 : q, :]
        b, c = b_ref[i], c_ref[i]
        x = x_ref[i].astype(F32)
        step_wide = spread(step_ref[i], expand)
        yield
        xs = (x * step_wide).astype(BF16)
        grown = spread(jnp.exp(cum), expand)
        waned = spread(jnp.exp(total - cum), expand)
        yield
        xw = (x * step_wide * waned).astype(BF16)
        dy = dy_ref[i]
        dy_low = dy.astype(BF16)
        edy = (dy * grown).astype(BF16)
        before = in_ref[i, 0]
        after_grad = grad[i]
        after_low = after_grad.astype(BF16)
        yield
        scores_t = dot(b, c, ((1,), (1,)))
        v_state = waned * dot(b, after_low)
        dscores_t = jnp.zeros((q, q), F32)
        v_parts = []
        yield
        for pair in range(heads // 2):
            lanes = slice(pair * 2 * width, (pair + 1) * 2 * width)
            dy_pair = pair_rows(dy_low[:, lanes])
            xs_pair = pair_rows(xs[:, lanes])
            dmix = dot(xs_pair, dy_low[:, lanes], ((1,), (1,)))
            mixing = []
            for k, h in enumerate((2 * pair, 2 * pair + 1)):
                between = cum_t[h : h + 1, :] - cum[:, h : h + 1]
                fade = jnp.exp(jnp.where(later, between, -1e30))
                mixing.append((fade * scores_t).astype(BF16))
                dscores_t = dscores_t + fade * dmix[k * q : (k + 1) * q]
            v_parts.append(dot(jnp.concatenate(mixing, axis=1), dy_pair))
            yield
        v = jnp.concatenate(v_parts, axis=1) + v_state
        xs_wide = xs.astype(F32)
        etotal = grown[q - 1 : q, :]
        end_row = jnp.sum(xs_wide * v_state, axis=0, keepdims=True) + jnp.sum(
            etotal * before * after_grad, axis=0, keepdims=True
        )
        crossing = dy_low.astype(F32) * y_ref[i] - xs_wide * v
        last = lax.broadcasted_iota(jnp.int32, crossing.shape, 0) == q - 1
        crossing = crossing + jnp.where(last, end_row, 0.0)
        upper = jnp.where(column >= row, 1.0, 0.0).astype(F32)
        yield
        decay_grad = dot(upper, head_sums(crossing, expand), precision=HIGHEST_PREC)
        pre_grad = (head_sums(x * v, expand) - rate_ref[...] * decay_grad) * slope_ref[i]
        pre_ref[i] = pre_grad.astype(BF16)
        sums = [
            jnp.sum(decay_grad * decay_ref[i], axis=0, keepdims=True),
            jnp.sum(pre_grad, axis=0, keepdims=True),
            jnp.sum(head_sums(x * dy, expand), axis=0, keepdims=True),
            jnp.zeros((5, heads), F32),
        ]
        head_sums_ref[...] += jnp.concatenate(sums, axis=0)
        yield
        dscores_low = dscores_t.astype(BF16)
        state = b.shape[1]
        dbc_ref[i, :, :state] = (
            dot(dscores_low, c) + dot(xw, after_low, ((1,), (1,)))
        ).astype(BF16)
        dbc_ref[i, :, state:] = (
            dot(dscores_low, b, ((0,), (0,))) + dot(edy, before.astype(BF16), ((1,), (1,)))
        ).astype(BF16)
        grad[i] = etotal * after_grad + dot(c, edy, ((0,), (0,)))
        yield
        dx = step_wide * v + skip_ref[0] * dy
        previous = rows_before(edge_ref, previous_ref, i, pl.num_programs(1) - 1)
        conv_grad, mixed_grad, tap_sums = conv_back_step(
            dx, mixed_ref[i].astype(F32), previous, taps_ref[...], after[i]
        )
        mixed_grad_ref[i] = mixed_grad.astype(BF16)
        first_ref[i] = conv_grad[:8]
        after[i] = conv_grad[:8]
        last_ref[i] = jnp.where(last_chunk, mixed_grad[q - 8 :], last_ref[i])
        tap_sums_ref[...] += tap_sums

    alternately(body(i) for i in range(group))


def act_blocks(inner, state, place):
    def part(lanes, at):
        return pl.BlockSpec((GROUP, CHUNK, lanes), lambda s, k: (s, place(k), at))

    return [part(inner, 0), part(state, inner // state), part(state, inner // state + 1)]


def conv_windows(mixed, previous):
    q = mixed.shape[0]
    window = jnp.concatenate([previous, mixed], axis=0)
    return [window[8 - CONV + 1 + k : 8 - CONV + 1 + k + q] for k in range(CONV)]


def first_kernel(
    mixed_ref, previous_ref, edge_ref, taps_ref, step_ref, decay_ref, act_ref, packed_ref, state, total
):
    chunk = pl.program_id(1)
    group, _, heads = step_ref.shape
    state_width, inner = state.shape[1:]

    @pl.when(chunk == 0)
    def _():
        state[...] = jnp.zeros_like(state)
        total[...] = jnp.zeros_like(total)

    expand = expander(heads, inner // heads)

    def body(i):
        previous = rows_before(edge_ref, previous_ref, i, 0)
        cum = chunk_decays(decay_ref[i])[0]
        q = cum.shape[0]
        last = cum[q - 1 : q, :]
        yield
        weights = spread(step_ref[i] * jnp.exp(last - cum), expand)
        kept = spread(jnp.exp(cum), expand)[q - 1 : q]
        yield
        convolved = taps_ref[CONV : CONV + 1]
        for k, part in enumerate(conv_windows(mixed_ref[i].astype(F32), previous)):
            convolved = convolved + taps_ref[k : k + 1] * part
        activated = jax.nn.silu(convolved).astype(BF16)
        act_ref[i] = activated
        yield
        xw = (activated[:, :inner].astype(F32) * weights).astype(BF16)
        b = activated[:, inner : inner + state_width]
        state[i] = kept * state[i] + dot(b, xw, ((0,), (0,)))
        total[i] = total[i] + last

    alternately(body(i) for i in range(group))

    @pl.when(chunk == pl.num_programs(1) - 1)
    def _():
        height = packed_ref.shape[2] - 16
        for i in range(group):
            decay = spread(jnp.exp(jnp.broadcast_to(total[i], (8, heads))), expand)[:1]
            high = decay.astype(BF16).astype(F32)
            tail = jnp.concatenate([high, decay - high, jnp.zeros((14, inner), F32)], axis=0)
            for part in range(packed_ref.shape[1]):
                rows = state[i, part * height : (part + 1) * height]
                packed_ref[i, part] = jnp.concatenate([rows, tail], axis=0).astype(BF16)


def conv_forward(mixed, edge, taps, step, decay, state, parts):
    seqs, length, lanes = mixed.shape
    heads, inner = step.shape[2], lanes - 2 * state
    chunks, tall = length // CHUNK, CHUNK // 16
    height = state // parts + 16

    def block(width):
        return pl.BlockSpec((GROUP, CHUNK, width), lambda s, k: (s, k, 0))

    return pl.pallas_call(
        first_kernel,
        grid=(seqs // GROUP, chunks),
        in_specs=[
            block(lanes),
            pl.BlockSpec((GROUP, 16, lanes), lambda s, k: (s, jnp.maximum(k * tall - 1, 0), 0)),
            pl.BlockSpec((GROUP, 16, lanes), lambda s, k: (s, 0, 0)),
            pl.BlockSpec((8, lanes), lambda s, k: (0, 0)),
            block(heads),
            block(heads),
        ],
        out_specs=[
            block(lanes),
            pl.BlockSpec((GROUP, parts, height, inner), lambda s, k: (s, 0, 0, 0)),
        ],
        out_shape=[
            jax.ShapeDtypeStruct(mixed.shape, BF16),
            jax.ShapeDtypeStruct((seqs, parts, height, inner), BF16),
        ],
        scratch_shapes=[pltpu.VMEM((GROUP, state, inner), F32), pltpu.VMEM((GROUP, 1, heads), F32)],
        compiler_params=pltpu.CompilerParams(vmem_limit_bytes=40 << 20),
        cost_estimate=load(9),
    )(mixed, mixed, edge, taps, step, decay)


def scan_forward(activated, step, decay, enter):
    seqs, length, heads = step.shape
    state, inner = enter.shape[1:]
    chunks = length // CHUNK

    def block(lanes):
        return pl.BlockSpec((GROUP, CHUNK, lanes), lambda s, k: (s, k, 0))

    return pl.pallas_call(
        scan_kernel,
        grid=(seqs // GROUP, chunks),
        in_specs=act_blocks(inner, state, lambda k: k)
        + [
            block(heads),
            block(heads),
            pl.BlockSpec((GROUP, state, inner), lambda s, k: (s, 0, 0)),
        ],
        out_specs=[
            block(inner),
            pl.BlockSpec((GROUP, 1, state, inner), lambda s, k: (s, k, 0, 0)),
        ],
        out_shape=[
            jax.ShapeDtypeStruct((seqs, length, inner), F32),
            jax.ShapeDtypeStruct((seqs, chunks, state, inner), F32),
        ],
        scratch_shapes=[pltpu.VMEM((GROUP, state, inner), F32)],
        compiler_params=pltpu.CompilerParams(vmem_limit_bytes=40 << 20),
        cost_estimate=load(13),
    )(activated, activated, activated, step, decay, enter)


def conv_blocks(chunks, lanes, at):
    tall = CHUNK // 16
    return [
        pl.BlockSpec((GROUP, CHUNK, lanes), lambda s, k, *_: (s, chunks - 1 - k, at)),
        pl.BlockSpec(
            (GROUP, 16, lanes), lambda s, k, *_: (s, jnp.maximum((chunks - 1 - k) * tall - 1, 0), at)
        ),
        pl.BlockSpec((GROUP, 16, lanes), lambda s, k, *_: (s, 0, at)),
        pl.BlockSpec((8, lanes), lambda s, k, *_: (0, at)),
    ]


def conv_outs(seqs, chunks, lanes):
    specs = [
        pl.BlockSpec((GROUP, CHUNK, lanes), lambda s, k, *_: (s, chunks - 1 - k, 0)),
        pl.BlockSpec((GROUP, 8, lanes), lambda s, k, *_: (s, 0, 0)),
        pl.BlockSpec((GROUP, 8, lanes), lambda s, k, *_: (s, 0, 0)),
        pl.BlockSpec((8, lanes), lambda s, k, *_: (0, 0)),
    ]
    shapes = [
        jax.ShapeDtypeStruct((seqs, chunks * CHUNK, lanes), BF16),
        jax.ShapeDtypeStruct((seqs, 8, lanes), F32),
        jax.ShapeDtypeStruct((seqs, 8, lanes), F32),
        jax.ShapeDtypeStruct((8, lanes), F32),
    ]
    return specs, shapes


def scan_backward(
    activated, step, decay, skip, dy, y, states, leave, mixed, edge, taps, slope, rate
):
    seqs, length, heads = step.shape
    state, inner = leave.shape[1:]
    chunks = length // CHUNK

    def block(lanes):
        return pl.BlockSpec((GROUP, CHUNK, lanes), lambda s, k: (s, chunks - 1 - k, 0))

    conv_specs, conv_shapes = conv_outs(seqs, chunks, inner)
    return pl.pallas_call(
        back_kernel,
        grid=(seqs // GROUP, chunks),
        in_specs=act_blocks(inner, state, lambda k: chunks - 1 - k)
        + [
            block(heads),
            block(heads),
            pl.BlockSpec((1, 1, inner), lambda s, k: (0, 0, 0)),
            block(inner),
            block(inner),
            pl.BlockSpec((GROUP, 1, state, inner), lambda s, k: (s, chunks - 1 - k, 0, 0)),
            pl.BlockSpec((GROUP, state, inner), lambda s, k: (s, 0, 0)),
        ]
        + conv_blocks(chunks, inner, 0)
        + [block(heads), pl.BlockSpec((1, heads), lambda s, k: (0, 0))],
        out_specs=[conv_specs[0], block(2 * state), block(heads)]
        + conv_specs[1:]
        + [pl.BlockSpec((8, heads), lambda s, k: (0, 0))],
        out_shape=[
            conv_shapes[0],
            jax.ShapeDtypeStruct((seqs, length, 2 * state), BF16),
            jax.ShapeDtypeStruct((seqs, length, heads), BF16),
        ]
        + conv_shapes[1:]
        + [jax.ShapeDtypeStruct((8, heads), F32)],
        scratch_shapes=[pltpu.VMEM((GROUP, state, inner), F32), pltpu.VMEM((GROUP, 8, inner), F32)],
        compiler_params=pltpu.CompilerParams(vmem_limit_bytes=40 << 20),
        cost_estimate=load(30),
    )(
        activated, activated, activated, step, decay, skip, dy, y, states, leave,
        mixed, mixed, edge, taps, slope, rate
    )


def bc_kernel(
    scalars_ref, part_ref, got_ref, mixed_ref, previous_ref, edge_ref, taps_ref,
    mixed_grad_ref, first_ref, last_ref, tap_sums_ref, after
):
    group, q, _ = mixed_ref.shape
    last_chunk = pl.program_id(1) == 0
    start = (pl.program_id(0) == 0) & last_chunk

    @pl.when(start)
    def _():
        tap_sums_ref[...] = jnp.zeros_like(tap_sums_ref)

    @pl.when(last_chunk)
    def _():
        after[...] = jnp.zeros_like(after)

    act_grad = picked(scalars_ref, part_ref, got_ref)

    def body(i):
        previous = rows_before(edge_ref, previous_ref, i, pl.num_programs(1) - 1)
        yield
        conv_grad, mixed_grad, tap_sums = conv_back_step(
            act_grad[i], mixed_ref[i].astype(F32), previous, taps_ref[...], after[i]
        )
        mixed_grad_ref[i] = mixed_grad.astype(BF16)
        first_ref[i] = conv_grad[:8]
        after[i] = conv_grad[:8]
        last_ref[i] = jnp.where(last_chunk, mixed_grad[q - 8 :], last_ref[i])
        tap_sums_ref[...] += tap_sums

    alternately(body(i) for i in range(group))


def bc_backward(scalars, part, got, mixed, edge, taps):
    seqs, length, _ = mixed.shape
    lanes = part.shape[1]
    chunks, at = length // CHUNK, mixed.shape[2] // lanes - 1
    halves = seqs // 2 // GROUP
    half = pl.BlockSpec((GROUP, CHUNK, lanes), lambda s, k, _: (s % halves, chunks - 1 - k, 0))
    conv_specs, conv_shapes = conv_outs(seqs, chunks, lanes)
    return pl.pallas_call(
        bc_kernel,
        grid_spec=pltpu.PrefetchScalarGridSpec(
            num_scalar_prefetch=1,
            grid=(seqs // GROUP, chunks),
            in_specs=[half, half] + conv_blocks(chunks, lanes, at),
            out_specs=conv_specs,
            scratch_shapes=[pltpu.VMEM((GROUP, 8, lanes), F32)],
        ),
        out_shape=conv_shapes,
        compiler_params=pltpu.CompilerParams(vmem_limit_bytes=40 << 20),
        cost_estimate=load(5),
    )(
        scalars,
        part.reshape(seqs // 2, length, lanes),
        got.reshape(seqs // 2, length, lanes),
        mixed,
        mixed,
        edge,
        taps,
    )


def joined_edges(mixed_grad, first, last, taps):
    rows = []
    for j in range(CONV - 1):
        rows.append(sum(taps[k] * first[:, j - k] for k in range(j + 1)))
    edge_grad = passed_along(jnp.stack(rows, axis=1), "seq", -1)
    fixed = last + jnp.pad(edge_grad, ((0, 0), (8 - CONV + 1, 0), (0, 0)))
    return lax.dynamic_update_slice(mixed_grad, fixed.astype(BF16), (0, mixed_grad.shape[1] - 8, 0))


def normed_kernel(gate_ref, x_ref, step_ref, z_weight_ref, x_weight_ref, step_weight_ref, out_ref):
    nt = ((1,), (1,))
    total = dot(gate_ref[...], z_weight_ref[...], nt) + dot(x_ref[...], x_weight_ref[...], nt)
    out_ref[...] = (total + dot(step_ref[...], step_weight_ref[...], nt)).astype(BF16)


def normed_products(gate_grad, x_grad, step_grad, z_weight, x_weight, step_weight):
    rows, width = gate_grad.shape[0], z_weight.shape[0]

    def block(a):
        return pl.BlockSpec((ROWS, a.shape[1]), lambda i: (i, 0))

    def whole(a):
        return pl.BlockSpec(a.shape, lambda i: (0, 0))

    args = (gate_grad, x_grad, step_grad, z_weight, x_weight, step_weight)
    return pl.pallas_call(
        normed_kernel,
        grid=(rows // ROWS,),
        in_specs=[block(a) for a in args[:3]] + [whole(a) for a in args[3:]],
        out_specs=pl.BlockSpec((ROWS, width), lambda i: (i, 0)),
        out_shape=jax.ShapeDtypeStruct((rows, width), BF16),
        compiler_params=pltpu.CompilerParams(vmem_limit_bytes=40 << 20),
        cost_estimate=load(6),
    )(*args)


def picked(scalars_ref, part_ref, got_ref):
    bit = scalars_ref[scalars_ref.shape[0] - 1]
    half = pl.num_programs(0) // 2
    own = (pl.program_id(0) // half) == bit
    return jnp.where(own, part_ref[...].astype(F32), got_ref[...].astype(F32))


def out_kernel(scalars_ref, part_ref, got_ref, tokens_ref, scale_ref, out_ref):
    projected = picked(scalars_ref, part_ref, got_ref)
    out_ref[...] = (tokens_ref[...].astype(F32) + scale_ref[...] * projected).astype(BF16)


def tail_kernel(
    local_len, scalars_ref, part_ref, got_ref, bc_ref, weight_ref, tokens_ref, back_ref, gain_ref,
    out_ref, gain_grad_ref
):
    step = pl.program_id(0)
    height = tokens_ref.shape[0]
    normed_grad = picked(scalars_ref, part_ref, got_ref) + dot(
        bc_ref[...], weight_ref[...], ((1,), (1,))
    )
    tokens = tokens_ref[...].astype(F32)
    inverse_rms = lax.rsqrt(jnp.mean(tokens * tokens, axis=-1, keepdims=True) + EPS)
    unit = tokens * inverse_rms

    @pl.when(step == 0)
    def _():
        gain_grad_ref[...] = jnp.zeros_like(gain_grad_ref)

    gain_grad_ref[...] += jnp.sum(normed_grad * unit, axis=0, keepdims=True)
    unit_grad = normed_grad * gain_ref[...]
    along = jnp.mean(unit_grad * unit, axis=-1, keepdims=True)
    row = step * height
    length = scalars_ref[row // local_len]
    start = scalars_ref[scalars_ref.shape[0] - 2] + row % local_len
    position = start + lax.broadcasted_iota(jnp.int32, tokens.shape, 0)
    back = jnp.where(position < length, back_ref[...].astype(F32), 0.0)
    out_ref[...] = back + inverse_rms * (unit_grad - unit * along)


ROWS = 256


def load(microseconds):
    return pl.CostEstimate(flops=0, transcendentals=0, bytes_accessed=int(microseconds * 3.69e6))


def merge_call(kernel, scalars, part, got, others, other_specs, out_specs, out_shape):
    rows, width = 2 * part.shape[0], part.shape[1]
    blocks = rows // ROWS
    half = pl.BlockSpec((ROWS, width), lambda i, s: (i % (blocks // 2), 0))
    return pl.pallas_call(
        kernel,
        grid_spec=pltpu.PrefetchScalarGridSpec(
            num_scalar_prefetch=1,
            grid=(blocks,),
            in_specs=[half, half] + other_specs,
            out_specs=out_specs,
        ),
        out_shape=out_shape,
        compiler_params=pltpu.CompilerParams(vmem_limit_bytes=40 << 20),
        cost_estimate=load(8),
    )(scalars, part, got, *others)


def row_block(lanes):
    return pl.BlockSpec((ROWS, lanes), lambda i, s: (i, 0))


def whole_block(shape):
    return pl.BlockSpec(shape, lambda i, s: (0, 0))


def adam_kernel(
    step_rate, decay_weight, gradient_ref, weight_ref, mean_ref, square_ref,
    mean_out, square_out, weight_out
):
    mean_out[...], square_out[...], weight_out[...] = adam_update(
        weight_ref[...],
        mean_ref[...],
        square_ref[...],
        gradient_ref[...].astype(F32),
        step_rate,
        decay_weight,
    )


def adam_tiles(weight, mean_old, square_old, gradient, step_rate, decay_weight):
    rows, _, columns = weight.shape
    tiles = pl.BlockSpec((128, columns // 64, 128), lambda i: (i, 0, 0))
    updated = pl.pallas_call(
        functools.partial(adam_kernel, step_rate, decay_weight),
        grid=(rows // 128,),
        in_specs=[tiles] * 4,
        out_specs=[tiles] * 3,
        out_shape=[jax.ShapeDtypeStruct((rows, columns // 64, 128), F32)] * 3,
        compiler_params=pltpu.CompilerParams(vmem_limit_bytes=40 << 20),
        cost_estimate=load(9),
    )(*map(lane_tiles, (gradient, weight, mean_old, square_old)))
    return [from_lane_tiles(part, weight.shape) for part in updated]


def silu_slope(values):
    sigmoid_part = jax.nn.sigmoid(values)
    return sigmoid_part * (1.0 + values * (1.0 - sigmoid_part))


def adam_update(weight, mean_old, square_old, gradient, step_rate, decay_weight):
    mean_new = BETA_ONE * mean_old + (1.0 - BETA_ONE) * gradient
    square_new = BETA_TWO * square_old + (1.0 - BETA_TWO) * gradient * gradient
    corrected_mean = mean_new / (1.0 - BETA_ONE**STEP)
    corrected_square = square_new / (1.0 - BETA_TWO**STEP)
    weight_new = weight - step_rate * (
        corrected_mean / (jnp.sqrt(corrected_square) + ADAM_EPS) + decay_weight * weight
    )
    return (mean_new, square_new, weight_new)


def shards(
    inputs,
    cotangent,
    lengths,
    norm_gain,
    norm_gain_mean,
    norm_gain_square,
    proj_zx,
    proj_zx_mean,
    proj_zx_square,
    proj_bc,
    proj_bc_mean,
    proj_bc_square,
    proj_step,
    proj_step_mean,
    proj_step_square,
    conv_inner,
    conv_inner_mean,
    conv_inner_square,
    conv_bc,
    conv_bc_mean,
    conv_bc_square,
    head_params,
    head_params_mean,
    head_params_square,
    gate_gain,
    gate_gain_mean,
    gate_gain_square,
    proj_out,
    proj_out_mean,
    proj_out_square,
):
    seq_count, local_len, model_width = inputs.shape
    local_inner = proj_zx.shape[2]
    state_width = proj_bc.shape[1] // 2
    local_heads = proj_step.shape[1]
    head_width = local_inner // local_heads
    rows = seq_count * local_len
    seq_size, seq_index = lax.axis_size("seq"), lax.axis_index("seq")

    def wide(a):
        selector = jnp.repeat(jnp.eye(local_heads, dtype=F32), head_width, axis=1)
        return jnp.einsum("...h,hc->...c", a, selector, precision=HIGHEST_PREC)

    positions = seq_index * local_len + jnp.arange(local_len)
    is_valid = (positions[None, :] < lengths[:, None]).astype(F32)
    tokens = inputs.astype(F32)
    inverse_rms = lax.rsqrt(jnp.mean(tokens * tokens, axis=-1, keepdims=True) + EPS)
    unit_tokens = tokens * inverse_rms
    normed = (unit_tokens * norm_gain).astype(BF16)
    z_weight = proj_zx[:, 0].astype(BF16)
    x_weight = proj_zx[:, 1].astype(BF16)
    bc_weight = proj_bc.astype(BF16)
    step_weight = proj_step.astype(BF16)
    out_weight = proj_out.astype(BF16)
    xbc_weight = jnp.concatenate([x_weight, bc_weight], axis=1)
    mixed_in = jnp.einsum("btd,dc->btc", normed, xbc_weight, preferred_element_type=F32).astype(BF16)
    edge_in = passed_along(mixed_in[:, local_len - CONV + 1 :], "seq", 1)
    raw_step = jnp.einsum("btd,dh->bth", normed, step_weight, preferred_element_type=F32)
    gate_input = jnp.einsum("btd,dc->btc", normed, z_weight, preferred_element_type=F32)
    conv_weight = jnp.concatenate([conv_inner, conv_bc], axis=-1)
    taps = jnp.pad(conv_weight, ((0, 8 - CONV - 1), (0, 0)))
    edge_rows = jnp.pad(edge_in, ((0, 0), (16 - CONV + 1, 0), (0, 0)))
    decay_log, step_bias, skip_gain = head_params[0], head_params[1], head_params[2]
    step_size = jax.nn.softplus(raw_step + step_bias)
    log_decay = -step_size * jnp.exp(decay_log)
    parts = seq_size // seq_count
    activated, packed = conv_forward(
        mixed_in, edge_rows, taps, step_size, log_decay, state_width, parts
    )
    entering, block_decays = states_before(
        packed.reshape((seq_size,) + packed.shape[2:]), state_width // parts, "seq"
    )
    entering = entering.reshape(seq_count, state_width, local_inner)
    x_values = activated[..., :local_inner]
    c_values = activated[..., local_inner + state_width :]
    earlier = jnp.tril(jnp.ones((local_len, local_len), F32))
    running = jnp.einsum("ts,bsh->bth", earlier, log_decay, precision=HIGHEST_PREC)

    scanned_raw, states = scan_forward(activated, step_size, log_decay, entering)
    skip_wide = jnp.repeat(skip_gain, head_width)[None, None]
    scanned = scanned_raw + skip_wide * x_values.astype(F32)
    gate_act = jax.nn.silu(gate_input)
    gated_values = scanned * gate_act
    square_sum = jnp.sum(gated_values * gated_values, axis=-1)
    scaled = (gated_values * gate_gain).astype(BF16)
    partial_out = jnp.einsum("bti,di->btd", scaled, out_weight, preferred_element_type=F32)
    out_cotangent = cotangent.astype(F32) * is_valid[..., None]
    partial_scale_grad = jnp.sum(out_cotangent * partial_out, axis=-1)
    square_total, scale_grad = lax.psum(jnp.stack([square_sum, partial_scale_grad]), "head")
    out_scale = lax.rsqrt(square_total / INNER + EPS)
    proj_grad = (out_scale[..., None] * out_cotangent).astype(BF16)
    square_grad = -0.5 * scale_grad * out_scale * out_scale * out_scale / INNER
    out_weight_grad = jnp.einsum("btd,bti->di", proj_grad, scaled, preferred_element_type=F32)
    scaled_grad = jnp.einsum("btd,di->bti", proj_grad, out_weight, preferred_element_type=F32)
    gate_gain_grad = jnp.sum(scaled_grad * gated_values, axis=(0, 1))
    gated_grad = scaled_grad * gate_gain + 2.0 * gated_values * square_grad[..., None]
    scanned_grad = gated_grad * gate_act
    gate_grad = (gated_grad * scanned * silu_slope(gate_input)).astype(BF16)
    local_back = jnp.einsum(
        "btn,btc->bnc",
        c_values,
        (scanned_grad * wide(jnp.exp(running))).astype(BF16),
        preferred_element_type=F32,
    )
    leaving = states_after(local_back, block_decays, "seq")
    projected = halved(partial_out.astype(BF16).reshape(rows, model_width), "head")
    leaving, projected = lax.optimization_barrier((leaving, projected))
    leaving = leaving.reshape(local_back.shape)
    z_weight_grad = jnp.einsum("btd,btc->dc", normed, gate_grad, preferred_element_type=F32)
    early_grads = jnp.concatenate([out_weight_grad, z_weight_grad], axis=0).astype(BF16)
    early_grads, _ = lax.optimization_barrier((early_grads, leaving))
    early_parts = exchanged(to_blocks(early_grads, seq_size), "seq")
    projected_far = swapped(projected, "head", axis_masks("head")[-1])
    x_raw, bc_grad, step_in_grad, x_first, x_last, x_tap_sums, head_totals = scan_backward(
        activated,
        step_size,
        log_decay,
        skip_wide,
        scanned_grad,
        scanned_raw,
        states,
        leaving,
        mixed_in,
        edge_rows,
        taps,
        jax.nn.sigmoid(raw_step + step_bias),
        jnp.exp(decay_log)[None],
    )
    x_raw, early_parts, projected_far = lax.optimization_barrier(
        (x_raw, early_parts, projected_far)
    )
    projected_half, projected_other = regathered(added(projected, projected_far), "head")
    early_own = jnp.sum(early_parts.astype(F32), axis=0).astype(BF16)
    bc_sum = halved(bc_grad.reshape(rows, 2 * state_width), "head")
    x_in_grad = joined_edges(x_raw, x_first, x_last, conv_weight[:, :local_inner])
    bc_far = swapped(bc_sum, "head", axis_masks("head")[-1])
    x_in_grad, bc_added, early_own = lax.optimization_barrier(
        (x_in_grad, added(bc_sum, bc_far), early_own)
    )
    early_all = lax.all_gather(early_own, "seq")
    bc_half, bc_other = regathered(bc_added, "head")
    normed_partial = normed_products(
        gate_grad.reshape(rows, local_inner),
        x_in_grad.reshape(rows, local_inner),
        step_in_grad.reshape(rows, local_heads),
        z_weight,
        x_weight,
        step_weight,
    )
    x_weight_grad = jnp.einsum("btd,btc->dc", normed, x_in_grad, preferred_element_type=F32)
    normed_sum = halved(normed_partial, "head")
    x_blocks, bc_other, _ = lax.optimization_barrier(
        (to_blocks(x_weight_grad, seq_size), bc_other, normed_sum)
    )
    x_parts = exchanged(x_blocks, "seq")
    normed_far = swapped(normed_sum, "head", axis_masks("head")[-1])

    scalars = jnp.concatenate(
        [lengths, jnp.stack([seq_index * local_len, near_bit("head", 1)]).astype(jnp.int32)]
    )
    bc_raw_grad, bc_first, bc_last, bc_tap_sums = bc_backward(
        scalars,
        bc_half,
        bc_other,
        mixed_in,
        edge_rows,
        taps,
    )
    bc_in_grad = joined_edges(bc_raw_grad, bc_first, bc_last, conv_weight[:, local_inner:])
    x_own = jnp.sum(x_parts.astype(F32), axis=0).astype(BF16)
    bc_weight_grad = jnp.einsum("btd,btc->dc", normed, bc_in_grad, preferred_element_type=F32)
    bc_blocks = to_blocks(bc_weight_grad, seq_size)
    bc_parts = exchanged(bc_blocks, "seq")
    early_all, _ = lax.optimization_barrier((early_all, bc_blocks))
    early_sums = early_all.reshape(2, model_width, local_inner)
    flat_tokens = inputs.reshape(rows, model_width)
    block_out = merge_call(
        out_kernel,
        scalars,
        projected_half,
        projected_other,
        (flat_tokens, out_scale.reshape(rows, 1)),
        [row_block(model_width), row_block(1)],
        row_block(model_width),
        jax.ShapeDtypeStruct((rows, model_width), BF16),
    )
    out_updated = adam_update(
        proj_out,
        proj_out_mean,
        proj_out_square,
        early_sums[0].astype(F32),
        LEARNING_RATES[-1],
        WEIGHT_DECAYS[-1],
    )
    normed_far, block_out, out_updated, _, x_own = lax.optimization_barrier(
        (normed_far, block_out, out_updated, bc_blocks, x_own)
    )
    x_all = lax.all_gather(x_own, "seq")
    x_sum = x_all.reshape(model_width, local_inner)
    block_out = block_out.reshape(inputs.shape)
    normed_half, normed_other = regathered(added(normed_sum, normed_far), "head")
    input_grad, norm_gain_grad = merge_call(
        functools.partial(tail_kernel, local_len),
        scalars,
        normed_half,
        normed_other,
        (
            bc_in_grad.reshape(rows, 2 * state_width),
            bc_weight,
            flat_tokens,
            cotangent.reshape(rows, model_width),
            norm_gain[None],
        ),
        [
            row_block(2 * state_width),
            whole_block(bc_weight.shape),
            row_block(model_width),
            row_block(model_width),
            whole_block((1, model_width)),
        ],
        [row_block(model_width), whole_block((1, model_width))],
        [
            jax.ShapeDtypeStruct((rows, model_width), F32),
            jax.ShapeDtypeStruct((1, model_width), F32),
        ],
    )
    bc_parts, input_grad = lax.optimization_barrier((bc_parts, input_grad))
    input_grad = input_grad.reshape(inputs.shape)
    bc_own = jnp.sum(bc_parts.astype(F32), axis=0).astype(BF16)
    bc_all = exchanged(jnp.broadcast_to(bc_own[None], bc_parts.shape), "seq")
    step_weight_grad = jnp.einsum("btd,bth->hd", normed, step_in_grad, preferred_element_type=F32)
    conv_inner_grad = x_tap_sums[: CONV + 1]
    conv_bc_grad = bc_tap_sums[: CONV + 1]
    head_grad = head_totals[:3]
    small_grads = (
        norm_gain_grad[0],
        step_weight_grad,
        conv_inner_grad,
        conv_bc_grad,
        head_grad,
        gate_gain_grad,
    )
    flat = jnp.concatenate([part.reshape(-1) for part in small_grads])
    count = flat.shape[0]
    flat = jnp.pad(flat, (0, -count % 1024)).reshape(-1, 128)
    flat = doubling_sum(flat, "seq").reshape(-1)
    small_sums, at = [], 0
    for part in small_grads:
        small_sums.append(flat[at : at + part.size].reshape(part.shape))
        at += part.size

    summed_grads = (
        small_sums[0],
        jnp.stack([early_sums[1], x_sum], axis=1),
        bc_all.reshape(bc_weight_grad.shape).astype(F32),
        small_sums[1].T,
        small_sums[2],
        small_sums[3],
        small_sums[4],
        small_sums[5],
        None,
    )
    params = (
        norm_gain,
        proj_zx,
        proj_bc,
        proj_step,
        conv_inner,
        conv_bc,
        head_params,
        gate_gain,
        proj_out,
    )
    means = (
        norm_gain_mean,
        proj_zx_mean,
        proj_bc_mean,
        proj_step_mean,
        conv_inner_mean,
        conv_bc_mean,
        head_params_mean,
        gate_gain_mean,
        proj_out_mean,
    )
    squares = (
        norm_gain_square,
        proj_zx_square,
        proj_bc_square,
        proj_step_square,
        conv_inner_square,
        conv_bc_square,
        head_params_square,
        gate_gain_square,
        proj_out_square,
    )
    results = [block_out, input_grad]
    for weight, mean_old, square_old, gradient, step_rate, decay_weight in zip(
        params, means, squares, summed_grads, LEARNING_RATES, WEIGHT_DECAYS
    ):
        if gradient is None:
            updated = out_updated
        elif weight.ndim == 3:
            updated = adam_tiles(weight, mean_old, square_old, gradient, step_rate, decay_weight)
        else:
            updated = adam_update(weight, mean_old, square_old, gradient, step_rate, decay_weight)
        results.extend(updated)
    return tuple(results)


def solution(mesh):
    in_specs = (
        P(None, "seq", None),
        P(None, "seq", None),
        P(),
        P(),
        P(),
        P(),
        P(None, None, "head"),
        P(None, None, "head"),
        P(None, None, "head"),
        P(),
        P(),
        P(),
        P(None, "head"),
        P(None, "head"),
        P(None, "head"),
        P(None, "head"),
        P(None, "head"),
        P(None, "head"),
        P(),
        P(),
        P(),
        P(None, "head"),
        P(None, "head"),
        P(None, "head"),
        P("head"),
        P("head"),
        P("head"),
        P(None, "head"),
        P(None, "head"),
        P(None, "head"),
    )
    out_specs = (
        P(None, "seq", None),
        P(None, "seq", None),
        P(),
        P(),
        P(),
        P(None, None, "head"),
        P(None, None, "head"),
        P(None, None, "head"),
        P(),
        P(),
        P(),
        P(None, "head"),
        P(None, "head"),
        P(None, "head"),
        P(None, "head"),
        P(None, "head"),
        P(None, "head"),
        P(),
        P(),
        P(),
        P(None, "head"),
        P(None, "head"),
        P(None, "head"),
        P("head"),
        P("head"),
        P("head"),
        P(None, "head"),
        P(None, "head"),
        P(None, "head"),
    )
    return jax.shard_map(shards, mesh=mesh, in_specs=in_specs, out_specs=out_specs, check_vma=False)
```

```python
import functools

import jax
import jax.numpy as jnp
from jax import lax
from jax.experimental import pallas as pl
from jax.experimental.pallas import tpu as pltpu
from jax.sharding import PartitionSpec as P

INNER = 2048
CONV = 4
CHUNK = 128
GROUP = 2
STEP = 7


EPS = 1e-05
BETA_ONE = 0.9
BETA_TWO = 0.95
ADAM_EPS = 1e-08
LEARNING_RATES = (0.6, 0.09, 0.09, 0.09, 0.9, 0.9, 0.9, 0.6, 0.06)
WEIGHT_DECAYS = (0.0, 0.1, 0.1, 0.1, 0.0, 0.0, 0.0, 0.0, 0.1)
HIGHEST_PREC = lax.Precision.HIGHEST
F32 = jnp.float32
BF16 = jnp.bfloat16


def passed_along(block, axis, distance):
    devices = range(lax.axis_size(axis))
    route = [(i - distance, i) for i in devices if i - distance in devices]
    return lax.ppermute(block, axis, route)


def swapped(block, axis, mask):
    return lax.ppermute(block, axis, [(i, i ^ mask) for i in range(lax.axis_size(axis))])


def doubling_sum(part, axis):
    for k in range(lax.axis_size(axis).bit_length() - 1):
        part = part + swapped(part, axis, 1 << k)
    return part


def axis_masks(axis):
    return [1 << k for k in range(lax.axis_size(axis).bit_length() - 1)]


def near_bit(axis, mask):
    return (lax.axis_index(axis) // mask) % 2


def added(a, b):
    return (a.astype(F32) + b.astype(F32)).astype(BF16)


def halved(part, axis):
    for mask in axis_masks(axis)[:-1]:
        bit = near_bit(axis, mask)
        halves = part.reshape((2, part.shape[0] // 2) + part.shape[1:])
        sent = lax.dynamic_index_in_dim(halves, 1 - bit, 0, keepdims=False)
        kept = lax.dynamic_index_in_dim(halves, bit, 0, keepdims=False)
        part = added(kept, swapped(sent, axis, mask))
    return part


def joined(part, got, bit):
    first = jnp.where(bit == 0, part, got)
    second = jnp.where(bit == 0, got, part)
    return jnp.concatenate([first, second], axis=0)


def regathered(part, axis):
    masks = axis_masks(axis)[:-1]
    for mask in reversed(masks[1:]):
        part = joined(part, swapped(part, axis, mask), near_bit(axis, mask))
    return part, swapped(part, axis, masks[0])


def halving_sum(part, axis):
    part = halved(part, axis)
    part = added(part, swapped(part, axis, axis_masks(axis)[-1]))
    part, other = regathered(part, axis)
    return joined(part, other, near_bit(axis, 1))


def exchanged(blocks, axis):
    return lax.all_to_all(blocks, axis, 0, 0, tiled=True)


def to_blocks(state, count):
    return state.astype(BF16).reshape(count, -1, state.shape[-1])


def states_before(packed, height, axis):
    size = lax.axis_size(axis)
    got = exchanged(packed, axis).astype(F32)
    decays = got[:, height : height + 1] + got[:, height + 1 : height + 2]
    entering = [jnp.zeros(got[0, :height].shape, F32)]
    for k in range(size - 1):
        entering.append(decays[k] * entering[-1] + got[k, :height])
    return exchanged(jnp.stack(entering).astype(BF16), axis), decays


def states_after(state, decays, axis):
    size = lax.axis_size(axis)
    got = exchanged(to_blocks(state, size), axis).astype(F32)
    leaving = [jnp.zeros(got[0].shape, F32)]
    for k in range(size - 1, 0, -1):
        leaving.append(decays[k] * leaving[-1] + got[k])
    return exchanged(jnp.stack(leaving[::-1]).astype(BF16), axis)


def lane_tiles(a):
    rows, two, columns = a.shape
    return a.reshape(rows, two, columns // 128, 128).transpose(0, 2, 1, 3).reshape(rows, -1, 128)


def from_lane_tiles(a, shape):
    rows, two, columns = shape
    return a.reshape(rows, columns // 128, two, 128).transpose(0, 2, 1, 3).reshape(shape)


def dot(a, b, dims=((1,), (0,)), precision=None):
    return lax.dot_general(a, b, (dims, ((), ())), precision=precision, preferred_element_type=F32)


def alternately(bodies):
    bodies = list(bodies)
    while bodies:
        bodies = [body for body in bodies if next(body, bodies) is not bodies]


def expander(heads, width):
    row = lax.broadcasted_iota(jnp.int32, (heads, heads * width), 0)
    column = lax.broadcasted_iota(jnp.int32, (heads, heads * width), 1)
    inside = (column >= row * width) & (column < (row + 1) * width)
    return jnp.where(inside, 1.0, 0.0).astype(BF16)


def split_dot(a, b, dims):
    high = a.astype(BF16)
    low = (a - high.astype(F32)).astype(BF16)
    return dot(high, b, dims) + dot(low, b, dims)


def spread(a, expand):
    return split_dot(a, expand, ((1,), (0,)))


def head_sums(a, expand):
    return split_dot(a, expand, ((1,), (1,)))


def pair_rows(a):
    lane = lax.broadcasted_iota(jnp.int32, a.shape, 1)
    first = lane < a.shape[1] // 2
    zero = jnp.zeros_like(a)
    return jnp.concatenate([jnp.where(first, a, zero), jnp.where(first, zero, a)], axis=0)


def chunk_decays(decay):
    q = decay.shape[0]
    row = lax.broadcasted_iota(jnp.int32, (q, q), 0)
    column = lax.broadcasted_iota(jnp.int32, (q, q), 1)
    lower = jnp.where(row >= column, 1.0, 0.0).astype(F32)
    cum = dot(lower, decay, precision=HIGHEST_PREC)
    cum_t = dot(decay, lower, ((0,), (1,)), precision=HIGHEST_PREC)
    return cum, cum_t, row, column


def scan_kernel(x_ref, b_ref, c_ref, step_ref, decay_ref, enter_ref, y_ref, in_ref, state):
    group, _, heads = step_ref.shape
    width = x_ref.shape[2] // heads

    @pl.when(pl.program_id(1) == 0)
    def _():
        state[...] = enter_ref[...].astype(F32)

    expand = expander(heads, width)

    def body(i):
        cum, cum_t, row, column = chunk_decays(decay_ref[i])
        causal = row >= column
        q = cum.shape[0]
        total = cum[q - 1 : q, :]
        b, c = b_ref[i], c_ref[i]
        x = x_ref[i].astype(F32)
        step = step_ref[i]
        yield
        xs = (x * spread(step, expand)).astype(BF16)
        grown = spread(jnp.exp(cum), expand)
        xw = (x * spread(step * jnp.exp(total - cum), expand)).astype(BF16)
        yield
        scores = dot(c, b, ((1,), (1,)))
        before = state[i]
        in_ref[i, 0] = before
        from_state = grown * dot(c, before.astype(BF16))
        yield
        for pair in range(heads // 2):
            lanes = slice(pair * 2 * width, (pair + 1) * 2 * width)
            mixing = []
            for h in (2 * pair, 2 * pair + 1):
                between = cum[:, h : h + 1] - cum_t[h : h + 1, :]
                mixing.append((jnp.exp(jnp.where(causal, between, -1e30)) * scores).astype(BF16))
            within = dot(jnp.concatenate(mixing, axis=1), pair_rows(xs[:, lanes]))
            y_ref[i, :, lanes] = within + from_state[:, lanes]
            yield
        state[i] = grown[q - 1 : q, :] * before + dot(b, xw, ((0,), (0,)))

    alternately(body(i) for i in range(group))


def conv_back_step(act_grad, mixed, previous, taps, after):
    q = mixed.shape[0]
    shifted = conv_windows(mixed, previous)
    convolved = taps[CONV : CONV + 1]
    for k in range(CONV):
        convolved = convolved + taps[k : k + 1] * shifted[k]
    conv_grad = act_grad * silu_slope(convolved)
    extended = jnp.concatenate([conv_grad, after], axis=0)
    mixed_grad = taps[CONV - 1 : CONV] * conv_grad
    for k in range(CONV - 1):
        mixed_grad = mixed_grad + taps[k : k + 1] * extended[CONV - 1 - k : CONV - 1 - k + q]
    sums = [jnp.sum(conv_grad * part, axis=0, keepdims=True) for part in shifted]
    sums.append(jnp.sum(conv_grad, axis=0, keepdims=True))
    sums.append(jnp.zeros((8 - CONV - 1, mixed.shape[1]), F32))
    return conv_grad, mixed_grad, jnp.concatenate(sums, axis=0)


def rows_before(edge_ref, previous_ref, i, chunk):
    first = pl.program_id(1) == chunk
    return jnp.where(first, edge_ref[i].astype(F32), previous_ref[i].astype(F32))[8:]


def back_kernel(
    x_ref, b_ref, c_ref, step_ref, decay_ref, skip_ref, dy_ref, y_ref, in_ref, leave_ref,
    mixed_ref, previous_ref, edge_ref, taps_ref, slope_ref, rate_ref,
    mixed_grad_ref, dbc_ref, pre_ref, first_ref, last_ref, tap_sums_ref, head_sums_ref,
    grad, after
):
    group, _, heads = step_ref.shape
    width = x_ref.shape[2] // heads
    start = (pl.program_id(0) == 0) & (pl.program_id(1) == 0)

    @pl.when(start)
    def _():
        tap_sums_ref[...] = jnp.zeros_like(tap_sums_ref)
        head_sums_ref[...] = jnp.zeros_like(head_sums_ref)

    @pl.when(pl.program_id(1) == 0)
    def _():
        after[...] = jnp.zeros_like(after)
        grad[...] = leave_ref[...].astype(F32)

    expand = expander(heads, width)
    last_chunk = pl.program_id(1) == 0

    def body(i):
        cum, cum_t, row, column = chunk_decays(decay_ref[i])
        later = column >= row
        q = cum.shape[0]
        total = cum[q - 1 : q, :]
        b, c = b_ref[i], c_ref[i]
        x = x_ref[i].astype(F32)
        step_wide = spread(step_ref[i], expand)
        yield
        xs = (x * step_wide).astype(BF16)
        grown = spread(jnp.exp(cum), expand)
        waned = spread(jnp.exp(total - cum), expand)
        yield
        xw = (x * step_wide * waned).astype(BF16)
        dy = dy_ref[i]
        dy_low = dy.astype(BF16)
        edy = (dy * grown).astype(BF16)
        before = in_ref[i, 0]
        after_grad = grad[i]
        after_low = after_grad.astype(BF16)
        yield
        scores_t = dot(b, c, ((1,), (1,)))
        v_state = waned * dot(b, after_low)
        dscores_t = jnp.zeros((q, q), F32)
        v_parts = []
        yield
        for pair in range(heads // 2):
            lanes = slice(pair * 2 * width, (pair + 1) * 2 * width)
            dy_pair = pair_rows(dy_low[:, lanes])
            xs_pair = pair_rows(xs[:, lanes])
            dmix = dot(xs_pair, dy_low[:, lanes], ((1,), (1,)))
            mixing = []
            for k, h in enumerate((2 * pair, 2 * pair + 1)):
                between = cum_t[h : h + 1, :] - cum[:, h : h + 1]
                fade = jnp.exp(jnp.where(later, between, -1e30))
                mixing.append((fade * scores_t).astype(BF16))
                dscores_t = dscores_t + fade * dmix[k * q : (k + 1) * q]
            v_parts.append(dot(jnp.concatenate(mixing, axis=1), dy_pair))
            yield
        v = jnp.concatenate(v_parts, axis=1) + v_state
        xs_wide = xs.astype(F32)
        etotal = grown[q - 1 : q, :]
        end_row = jnp.sum(xs_wide * v_state, axis=0, keepdims=True) + jnp.sum(
            etotal * before * after_grad, axis=0, keepdims=True
        )
        crossing = dy_low.astype(F32) * y_ref[i] - xs_wide * v
        last = lax.broadcasted_iota(jnp.int32, crossing.shape, 0) == q - 1
        crossing = crossing + jnp.where(last, end_row, 0.0)
        upper = jnp.where(column >= row, 1.0, 0.0).astype(F32)
        yield
        decay_grad = dot(upper, head_sums(crossing, expand), precision=HIGHEST_PREC)
        pre_grad = (head_sums(x * v, expand) - rate_ref[...] * decay_grad) * slope_ref[i]
        pre_ref[i] = pre_grad.astype(BF16)
        sums = [
            jnp.sum(decay_grad * decay_ref[i], axis=0, keepdims=True),
            jnp.sum(pre_grad, axis=0, keepdims=True),
            jnp.sum(head_sums(x * dy, expand), axis=0, keepdims=True),
            jnp.zeros((5, heads), F32),
        ]
        head_sums_ref[...] += jnp.concatenate(sums, axis=0)
        yield
        dscores_low = dscores_t.astype(BF16)
        state = b.shape[1]
        dbc_ref[i, :, :state] = (
            dot(dscores_low, c) + dot(xw, after_low, ((1,), (1,)))
        ).astype(BF16)
        dbc_ref[i, :, state:] = (
            dot(dscores_low, b, ((0,), (0,))) + dot(edy, before.astype(BF16), ((1,), (1,)))
        ).astype(BF16)
        grad[i] = etotal * after_grad + dot(c, edy, ((0,), (0,)))
        yield
        dx = step_wide * v + skip_ref[0] * dy
        previous = rows_before(edge_ref, previous_ref, i, pl.num_programs(1) - 1)
        conv_grad, mixed_grad, tap_sums = conv_back_step(
            dx, mixed_ref[i].astype(F32), previous, taps_ref[...], after[i]
        )
        mixed_grad_ref[i] = mixed_grad.astype(BF16)
        first_ref[i] = conv_grad[:8]
        after[i] = conv_grad[:8]
        last_ref[i] = jnp.where(last_chunk, mixed_grad[q - 8 :], last_ref[i])
        tap_sums_ref[...] += tap_sums

    alternately(body(i) for i in range(group))


def act_blocks(inner, state, place):
    def part(lanes, at):
        return pl.BlockSpec((GROUP, CHUNK, lanes), lambda s, k: (s, place(k), at))

    return [part(inner, 0), part(state, inner // state), part(state, inner // state + 1)]


def conv_windows(mixed, previous):
    q = mixed.shape[0]
    window = jnp.concatenate([previous, mixed], axis=0)
    return [window[8 - CONV + 1 + k : 8 - CONV + 1 + k + q] for k in range(CONV)]


def first_kernel(
    mixed_ref, previous_ref, edge_ref, taps_ref, step_ref, decay_ref, act_ref, packed_ref, state, total
):
    chunk = pl.program_id(1)
    group, _, heads = step_ref.shape
    state_width, inner = state.shape[1:]

    @pl.when(chunk == 0)
    def _():
        state[...] = jnp.zeros_like(state)
        total[...] = jnp.zeros_like(total)

    expand = expander(heads, inner // heads)

    def body(i):
        previous = rows_before(edge_ref, previous_ref, i, 0)
        cum = chunk_decays(decay_ref[i])[0]
        q = cum.shape[0]
        last = cum[q - 1 : q, :]
        yield
        weights = spread(step_ref[i] * jnp.exp(last - cum), expand)
        kept = spread(jnp.exp(cum), expand)[q - 1 : q]
        yield
        convolved = taps_ref[CONV : CONV + 1]
        for k, part in enumerate(conv_windows(mixed_ref[i].astype(F32), previous)):
            convolved = convolved + taps_ref[k : k + 1] * part
        activated = jax.nn.silu(convolved).astype(BF16)
        act_ref[i] = activated
        yield
        xw = (activated[:, :inner].astype(F32) * weights).astype(BF16)
        b = activated[:, inner : inner + state_width]
        state[i] = kept * state[i] + dot(b, xw, ((0,), (0,)))
        total[i] = total[i] + last

    alternately(body(i) for i in range(group))

    @pl.when(chunk == pl.num_programs(1) - 1)
    def _():
        height = packed_ref.shape[2] - 16
        for i in range(group):
            decay = spread(jnp.exp(jnp.broadcast_to(total[i], (8, heads))), expand)[:1]
            high = decay.astype(BF16).astype(F32)
            tail = jnp.concatenate([high, decay - high, jnp.zeros((14, inner), F32)], axis=0)
            for part in range(packed_ref.shape[1]):
                rows = state[i, part * height : (part + 1) * height]
                packed_ref[i, part] = jnp.concatenate([rows, tail], axis=0).astype(BF16)


def conv_forward(mixed, edge, taps, step, decay, state, parts):
    seqs, length, lanes = mixed.shape
    heads, inner = step.shape[2], lanes - 2 * state
    chunks, tall = length // CHUNK, CHUNK // 16
    height = state // parts + 16

    def block(width):
        return pl.BlockSpec((GROUP, CHUNK, width), lambda s, k: (s, k, 0))

    return pl.pallas_call(
        first_kernel,
        grid=(seqs // GROUP, chunks),
        in_specs=[
            block(lanes),
            pl.BlockSpec((GROUP, 16, lanes), lambda s, k: (s, jnp.maximum(k * tall - 1, 0), 0)),
            pl.BlockSpec((GROUP, 16, lanes), lambda s, k: (s, 0, 0)),
            pl.BlockSpec((8, lanes), lambda s, k: (0, 0)),
            block(heads),
            block(heads),
        ],
        out_specs=[
            block(lanes),
            pl.BlockSpec((GROUP, parts, height, inner), lambda s, k: (s, 0, 0, 0)),
        ],
        out_shape=[
            jax.ShapeDtypeStruct(mixed.shape, BF16),
            jax.ShapeDtypeStruct((seqs, parts, height, inner), BF16),
        ],
        scratch_shapes=[pltpu.VMEM((GROUP, state, inner), F32), pltpu.VMEM((GROUP, 1, heads), F32)],
        compiler_params=pltpu.CompilerParams(vmem_limit_bytes=40 << 20),
        cost_estimate=load(9),
    )(mixed, mixed, edge, taps, step, decay)


def scan_forward(activated, step, decay, enter):
    seqs, length, heads = step.shape
    state, inner = enter.shape[1:]
    chunks = length // CHUNK

    def block(lanes):
        return pl.BlockSpec((GROUP, CHUNK, lanes), lambda s, k: (s, k, 0))

    return pl.pallas_call(
        scan_kernel,
        grid=(seqs // GROUP, chunks),
        in_specs=act_blocks(inner, state, lambda k: k)
        + [
            block(heads),
            block(heads),
            pl.BlockSpec((GROUP, state, inner), lambda s, k: (s, 0, 0)),
        ],
        out_specs=[
            block(inner),
            pl.BlockSpec((GROUP, 1, state, inner), lambda s, k: (s, k, 0, 0)),
        ],
        out_shape=[
            jax.ShapeDtypeStruct((seqs, length, inner), F32),
            jax.ShapeDtypeStruct((seqs, chunks, state, inner), F32),
        ],
        scratch_shapes=[pltpu.VMEM((GROUP, state, inner), F32)],
        compiler_params=pltpu.CompilerParams(vmem_limit_bytes=40 << 20),
        cost_estimate=load(13),
    )(activated, activated, activated, step, decay, enter)


def conv_blocks(chunks, lanes, at):
    tall = CHUNK // 16
    return [
        pl.BlockSpec((GROUP, CHUNK, lanes), lambda s, k, *_: (s, chunks - 1 - k, at)),
        pl.BlockSpec(
            (GROUP, 16, lanes), lambda s, k, *_: (s, jnp.maximum((chunks - 1 - k) * tall - 1, 0), at)
        ),
        pl.BlockSpec((GROUP, 16, lanes), lambda s, k, *_: (s, 0, at)),
        pl.BlockSpec((8, lanes), lambda s, k, *_: (0, at)),
    ]


def conv_outs(seqs, chunks, lanes):
    specs = [
        pl.BlockSpec((GROUP, CHUNK, lanes), lambda s, k, *_: (s, chunks - 1 - k, 0)),
        pl.BlockSpec((GROUP, 8, lanes), lambda s, k, *_: (s, 0, 0)),
        pl.BlockSpec((GROUP, 8, lanes), lambda s, k, *_: (s, 0, 0)),
        pl.BlockSpec((8, lanes), lambda s, k, *_: (0, 0)),
    ]
    shapes = [
        jax.ShapeDtypeStruct((seqs, chunks * CHUNK, lanes), BF16),
        jax.ShapeDtypeStruct((seqs, 8, lanes), F32),
        jax.ShapeDtypeStruct((seqs, 8, lanes), F32),
        jax.ShapeDtypeStruct((8, lanes), F32),
    ]
    return specs, shapes


def scan_backward(
    activated, step, decay, skip, dy, y, states, leave, mixed, edge, taps, slope, rate
):
    seqs, length, heads = step.shape
    state, inner = leave.shape[1:]
    chunks = length // CHUNK

    def block(lanes):
        return pl.BlockSpec((GROUP, CHUNK, lanes), lambda s, k: (s, chunks - 1 - k, 0))

    conv_specs, conv_shapes = conv_outs(seqs, chunks, inner)
    return pl.pallas_call(
        back_kernel,
        grid=(seqs // GROUP, chunks),
        in_specs=act_blocks(inner, state, lambda k: chunks - 1 - k)
        + [
            block(heads),
            block(heads),
            pl.BlockSpec((1, 1, inner), lambda s, k: (0, 0, 0)),
            block(inner),
            block(inner),
            pl.BlockSpec((GROUP, 1, state, inner), lambda s, k: (s, chunks - 1 - k, 0, 0)),
            pl.BlockSpec((GROUP, state, inner), lambda s, k: (s, 0, 0)),
        ]
        + conv_blocks(chunks, inner, 0)
        + [block(heads), pl.BlockSpec((1, heads), lambda s, k: (0, 0))],
        out_specs=[conv_specs[0], block(2 * state), block(heads)]
        + conv_specs[1:]
        + [pl.BlockSpec((8, heads), lambda s, k: (0, 0))],
        out_shape=[
            conv_shapes[0],
            jax.ShapeDtypeStruct((seqs, length, 2 * state), BF16),
            jax.ShapeDtypeStruct((seqs, length, heads), BF16),
        ]
        + conv_shapes[1:]
        + [jax.ShapeDtypeStruct((8, heads), F32)],
        scratch_shapes=[pltpu.VMEM((GROUP, state, inner), F32), pltpu.VMEM((GROUP, 8, inner), F32)],
        compiler_params=pltpu.CompilerParams(vmem_limit_bytes=40 << 20),
        cost_estimate=load(30),
    )(
        activated, activated, activated, step, decay, skip, dy, y, states, leave,
        mixed, mixed, edge, taps, slope, rate
    )


def bc_kernel(
    scalars_ref, part_ref, got_ref, mixed_ref, previous_ref, edge_ref, taps_ref,
    mixed_grad_ref, first_ref, last_ref, tap_sums_ref, after
):
    group, q, _ = mixed_ref.shape
    last_chunk = pl.program_id(1) == 0
    start = (pl.program_id(0) == 0) & last_chunk

    @pl.when(start)
    def _():
        tap_sums_ref[...] = jnp.zeros_like(tap_sums_ref)

    @pl.when(last_chunk)
    def _():
        after[...] = jnp.zeros_like(after)

    act_grad = picked(scalars_ref, part_ref, got_ref)

    def body(i):
        previous = rows_before(edge_ref, previous_ref, i, pl.num_programs(1) - 1)
        yield
        conv_grad, mixed_grad, tap_sums = conv_back_step(
            act_grad[i], mixed_ref[i].astype(F32), previous, taps_ref[...], after[i]
        )
        mixed_grad_ref[i] = mixed_grad.astype(BF16)
        first_ref[i] = conv_grad[:8]
        after[i] = conv_grad[:8]
        last_ref[i] = jnp.where(last_chunk, mixed_grad[q - 8 :], last_ref[i])
        tap_sums_ref[...] += tap_sums

    alternately(body(i) for i in range(group))


def bc_backward(scalars, part, got, mixed, edge, taps):
    seqs, length, _ = mixed.shape
    lanes = part.shape[1]
    chunks, at = length // CHUNK, mixed.shape[2] // lanes - 1
    halves = seqs // 2 // GROUP
    half = pl.BlockSpec((GROUP, CHUNK, lanes), lambda s, k, _: (s % halves, chunks - 1 - k, 0))
    conv_specs, conv_shapes = conv_outs(seqs, chunks, lanes)
    return pl.pallas_call(
        bc_kernel,
        grid_spec=pltpu.PrefetchScalarGridSpec(
            num_scalar_prefetch=1,
            grid=(seqs // GROUP, chunks),
            in_specs=[half, half] + conv_blocks(chunks, lanes, at),
            out_specs=conv_specs,
            scratch_shapes=[pltpu.VMEM((GROUP, 8, lanes), F32)],
        ),
        out_shape=conv_shapes,
        compiler_params=pltpu.CompilerParams(vmem_limit_bytes=40 << 20),
        cost_estimate=load(5),
    )(
        scalars,
        part.reshape(seqs // 2, length, lanes),
        got.reshape(seqs // 2, length, lanes),
        mixed,
        mixed,
        edge,
        taps,
    )


def joined_edges(mixed_grad, first, last, taps):
    rows = []
    for j in range(CONV - 1):
        rows.append(sum(taps[k] * first[:, j - k] for k in range(j + 1)))
    edge_grad = passed_along(jnp.stack(rows, axis=1), "seq", -1)
    fixed = last + jnp.pad(edge_grad, ((0, 0), (8 - CONV + 1, 0), (0, 0)))
    return lax.dynamic_update_slice(mixed_grad, fixed.astype(BF16), (0, mixed_grad.shape[1] - 8, 0))


def normed_kernel(gate_ref, x_ref, step_ref, z_weight_ref, x_weight_ref, step_weight_ref, out_ref):
    nt = ((1,), (1,))
    total = dot(gate_ref[...], z_weight_ref[...], nt) + dot(x_ref[...], x_weight_ref[...], nt)
    out_ref[...] = (total + dot(step_ref[...], step_weight_ref[...], nt)).astype(BF16)


def normed_products(gate_grad, x_grad, step_grad, z_weight, x_weight, step_weight):
    rows, width = gate_grad.shape[0], z_weight.shape[0]

    def block(a):
        return pl.BlockSpec((ROWS, a.shape[1]), lambda i: (i, 0))

    def whole(a):
        return pl.BlockSpec(a.shape, lambda i: (0, 0))

    args = (gate_grad, x_grad, step_grad, z_weight, x_weight, step_weight)
    return pl.pallas_call(
        normed_kernel,
        grid=(rows // ROWS,),
        in_specs=[block(a) for a in args[:3]] + [whole(a) for a in args[3:]],
        out_specs=pl.BlockSpec((ROWS, width), lambda i: (i, 0)),
        out_shape=jax.ShapeDtypeStruct((rows, width), BF16),
        compiler_params=pltpu.CompilerParams(vmem_limit_bytes=40 << 20),
        cost_estimate=load(6),
    )(*args)


def picked(scalars_ref, part_ref, got_ref):
    bit = scalars_ref[scalars_ref.shape[0] - 1]
    half = pl.num_programs(0) // 2
    own = (pl.program_id(0) // half) == bit
    return jnp.where(own, part_ref[...].astype(F32), got_ref[...].astype(F32))


def out_kernel(scalars_ref, part_ref, got_ref, tokens_ref, scale_ref, out_ref):
    projected = picked(scalars_ref, part_ref, got_ref)
    out_ref[...] = (tokens_ref[...].astype(F32) + scale_ref[...] * projected).astype(BF16)


def tail_kernel(
    local_len, scalars_ref, part_ref, got_ref, bc_ref, weight_ref, tokens_ref, back_ref, gain_ref,
    out_ref, gain_grad_ref
):
    step = pl.program_id(0)
    height = tokens_ref.shape[0]
    normed_grad = picked(scalars_ref, part_ref, got_ref) + dot(
        bc_ref[...], weight_ref[...], ((1,), (1,))
    )
    tokens = tokens_ref[...].astype(F32)
    inverse_rms = lax.rsqrt(jnp.mean(tokens * tokens, axis=-1, keepdims=True) + EPS)
    unit = tokens * inverse_rms

    @pl.when(step == 0)
    def _():
        gain_grad_ref[...] = jnp.zeros_like(gain_grad_ref)

    gain_grad_ref[...] += jnp.sum(normed_grad * unit, axis=0, keepdims=True)
    unit_grad = normed_grad * gain_ref[...]
    along = jnp.mean(unit_grad * unit, axis=-1, keepdims=True)
    row = step * height
    length = scalars_ref[row // local_len]
    start = scalars_ref[scalars_ref.shape[0] - 2] + row % local_len
    position = start + lax.broadcasted_iota(jnp.int32, tokens.shape, 0)
    back = jnp.where(position < length, back_ref[...].astype(F32), 0.0)
    out_ref[...] = back + inverse_rms * (unit_grad - unit * along)


ROWS = 256


def load(microseconds):
    return pl.CostEstimate(flops=0, transcendentals=0, bytes_accessed=int(microseconds * 3.69e6))


def merge_call(kernel, scalars, part, got, others, other_specs, out_specs, out_shape):
    rows, width = 2 * part.shape[0], part.shape[1]
    blocks = rows // ROWS
    half = pl.BlockSpec((ROWS, width), lambda i, s: (i % (blocks // 2), 0))
    return pl.pallas_call(
        kernel,
        grid_spec=pltpu.PrefetchScalarGridSpec(
            num_scalar_prefetch=1,
            grid=(blocks,),
            in_specs=[half, half] + other_specs,
            out_specs=out_specs,
        ),
        out_shape=out_shape,
        compiler_params=pltpu.CompilerParams(vmem_limit_bytes=40 << 20),
        cost_estimate=load(8),
    )(scalars, part, got, *others)


def row_block(lanes):
    return pl.BlockSpec((ROWS, lanes), lambda i, s: (i, 0))


def whole_block(shape):
    return pl.BlockSpec(shape, lambda i, s: (0, 0))


def adam_kernel(
    step_rate, decay_weight, gradient_ref, weight_ref, mean_ref, square_ref,
    mean_out, square_out, weight_out
):
    mean_out[...], square_out[...], weight_out[...] = adam_update(
        weight_ref[...],
        mean_ref[...],
        square_ref[...],
        gradient_ref[...].astype(F32),
        step_rate,
        decay_weight,
    )


def adam_tiles(weight, mean_old, square_old, gradient, step_rate, decay_weight):
    rows, _, columns = weight.shape
    tiles = pl.BlockSpec((128, columns // 64, 128), lambda i: (i, 0, 0))
    updated = pl.pallas_call(
        functools.partial(adam_kernel, step_rate, decay_weight),
        grid=(rows // 128,),
        in_specs=[tiles] * 4,
        out_specs=[tiles] * 3,
        out_shape=[jax.ShapeDtypeStruct((rows, columns // 64, 128), F32)] * 3,
        compiler_params=pltpu.CompilerParams(vmem_limit_bytes=40 << 20),
        cost_estimate=load(9),
    )(*map(lane_tiles, (gradient, weight, mean_old, square_old)))
    return [from_lane_tiles(part, weight.shape) for part in updated]


def silu_slope(values):
    sigmoid_part = jax.nn.sigmoid(values)
    return sigmoid_part * (1.0 + values * (1.0 - sigmoid_part))


def adam_update(weight, mean_old, square_old, gradient, step_rate, decay_weight):
    mean_new = BETA_ONE * mean_old + (1.0 - BETA_ONE) * gradient
    square_new = BETA_TWO * square_old + (1.0 - BETA_TWO) * gradient * gradient
    corrected_mean = mean_new / (1.0 - BETA_ONE**STEP)
    corrected_square = square_new / (1.0 - BETA_TWO**STEP)
    weight_new = weight - step_rate * (
        corrected_mean / (jnp.sqrt(corrected_square) + ADAM_EPS) + decay_weight * weight
    )
    return (mean_new, square_new, weight_new)


def shards(
    inputs,
    cotangent,
    lengths,
    norm_gain,
    norm_gain_mean,
    norm_gain_square,
    proj_zx,
    proj_zx_mean,
    proj_zx_square,
    proj_bc,
    proj_bc_mean,
    proj_bc_square,
    proj_step,
    proj_step_mean,
    proj_step_square,
    conv_inner,
    conv_inner_mean,
    conv_inner_square,
    conv_bc,
    conv_bc_mean,
    conv_bc_square,
    head_params,
    head_params_mean,
    head_params_square,
    gate_gain,
    gate_gain_mean,
    gate_gain_square,
    proj_out,
    proj_out_mean,
    proj_out_square,
):
    seq_count, local_len, model_width = inputs.shape
    local_inner = proj_zx.shape[2]
    state_width = proj_bc.shape[1] // 2
    local_heads = proj_step.shape[1]
    head_width = local_inner // local_heads
    rows = seq_count * local_len
    seq_size, seq_index = lax.axis_size("seq"), lax.axis_index("seq")

    def wide(a):
        selector = jnp.repeat(jnp.eye(local_heads, dtype=F32), head_width, axis=1)
        return jnp.einsum("...h,hc->...c", a, selector, precision=HIGHEST_PREC)

    positions = seq_index * local_len + jnp.arange(local_len)
    is_valid = (positions[None, :] < lengths[:, None]).astype(F32)
    tokens = inputs.astype(F32)
    inverse_rms = lax.rsqrt(jnp.mean(tokens * tokens, axis=-1, keepdims=True) + EPS)
    unit_tokens = tokens * inverse_rms
    normed = (unit_tokens * norm_gain).astype(BF16)
    z_weight = proj_zx[:, 0].astype(BF16)
    x_weight = proj_zx[:, 1].astype(BF16)
    bc_weight = proj_bc.astype(BF16)
    step_weight = proj_step.astype(BF16)
    out_weight = proj_out.astype(BF16)
    xbc_weight = jnp.concatenate([x_weight, bc_weight], axis=1)
    mixed_in = jnp.einsum("btd,dc->btc", normed, xbc_weight, preferred_element_type=F32).astype(BF16)
    edge_in = passed_along(mixed_in[:, local_len - CONV + 1 :], "seq", 1)
    raw_step = jnp.einsum("btd,dh->bth", normed, step_weight, preferred_element_type=F32)
    gate_input = jnp.einsum("btd,dc->btc", normed, z_weight, preferred_element_type=F32)
    conv_weight = jnp.concatenate([conv_inner, conv_bc], axis=-1)
    taps = jnp.pad(conv_weight, ((0, 8 - CONV - 1), (0, 0)))
    edge_rows = jnp.pad(edge_in, ((0, 0), (16 - CONV + 1, 0), (0, 0)))
    decay_log, step_bias, skip_gain = head_params[0], head_params[1], head_params[2]
    step_size = jax.nn.softplus(raw_step + step_bias)
    log_decay = -step_size * jnp.exp(decay_log)
    parts = seq_size // seq_count
    activated, packed = conv_forward(
        mixed_in, edge_rows, taps, step_size, log_decay, state_width, parts
    )
    entering, block_decays = states_before(
        packed.reshape((seq_size,) + packed.shape[2:]), state_width // parts, "seq"
    )
    entering = entering.reshape(seq_count, state_width, local_inner)
    x_values = activated[..., :local_inner]
    c_values = activated[..., local_inner + state_width :]
    earlier = jnp.tril(jnp.ones((local_len, local_len), F32))
    running = jnp.einsum("ts,bsh->bth", earlier, log_decay, precision=HIGHEST_PREC)

    scanned_raw, states = scan_forward(activated, step_size, log_decay, entering)
    skip_wide = jnp.repeat(skip_gain, head_width)[None, None]
    scanned = scanned_raw + skip_wide * x_values.astype(F32)
    gate_act = jax.nn.silu(gate_input)
    gated_values = scanned * gate_act
    square_sum = jnp.sum(gated_values * gated_values, axis=-1)
    scaled = (gated_values * gate_gain).astype(BF16)
    partial_out = jnp.einsum("bti,di->btd", scaled, out_weight, preferred_element_type=F32)
    out_cotangent = cotangent.astype(F32) * is_valid[..., None]
    partial_scale_grad = jnp.sum(out_cotangent * partial_out, axis=-1)
    square_total, scale_grad = lax.psum(jnp.stack([square_sum, partial_scale_grad]), "head")
    out_scale = lax.rsqrt(square_total / INNER + EPS)
    proj_grad = (out_scale[..., None] * out_cotangent).astype(BF16)
    square_grad = -0.5 * scale_grad * out_scale * out_scale * out_scale / INNER
    out_weight_grad = jnp.einsum("btd,bti->di", proj_grad, scaled, preferred_element_type=F32)
    scaled_grad = jnp.einsum("btd,di->bti", proj_grad, out_weight, preferred_element_type=F32)
    gate_gain_grad = jnp.sum(scaled_grad * gated_values, axis=(0, 1))
    gated_grad = scaled_grad * gate_gain + 2.0 * gated_values * square_grad[..., None]
    scanned_grad = gated_grad * gate_act
    gate_grad = (gated_grad * scanned * silu_slope(gate_input)).astype(BF16)
    local_back = jnp.einsum(
        "btn,btc->bnc",
        c_values,
        (scanned_grad * wide(jnp.exp(running))).astype(BF16),
        preferred_element_type=F32,
    )
    leaving = states_after(local_back, block_decays, "seq")
    projected = halved(partial_out.astype(BF16).reshape(rows, model_width), "head")
    leaving, projected = lax.optimization_barrier((leaving, projected))
    leaving = leaving.reshape(local_back.shape)
    z_weight_grad = jnp.einsum("btd,btc->dc", normed, gate_grad, preferred_element_type=F32)
    early_grads = jnp.concatenate([out_weight_grad, z_weight_grad], axis=0).astype(BF16)
    early_grads, _ = lax.optimization_barrier((early_grads, leaving))
    early_parts = exchanged(to_blocks(early_grads, seq_size), "seq")
    projected_far = swapped(projected, "head", axis_masks("head")[-1])
    x_raw, bc_grad, step_in_grad, x_first, x_last, x_tap_sums, head_totals = scan_backward(
        activated,
        step_size,
        log_decay,
        skip_wide,
        scanned_grad,
        scanned_raw,
        states,
        leaving,
        mixed_in,
        edge_rows,
        taps,
        jax.nn.sigmoid(raw_step + step_bias),
        jnp.exp(decay_log)[None],
    )
    x_raw, early_parts, projected_far = lax.optimization_barrier(
        (x_raw, early_parts, projected_far)
    )
    projected_half, projected_other = regathered(added(projected, projected_far), "head")
    early_own = jnp.sum(early_parts.astype(F32), axis=0).astype(BF16)
    bc_sum = halved(bc_grad.reshape(rows, 2 * state_width), "head")
    x_in_grad = joined_edges(x_raw, x_first, x_last, conv_weight[:, :local_inner])
    bc_far = swapped(bc_sum, "head", axis_masks("head")[-1])
    x_in_grad, bc_added, early_own = lax.optimization_barrier(
        (x_in_grad, added(bc_sum, bc_far), early_own)
    )
    early_all = lax.all_gather(early_own, "seq")
    bc_half, bc_other = regathered(bc_added, "head")
    normed_partial = normed_products(
        gate_grad.reshape(rows, local_inner),
        x_in_grad.reshape(rows, local_inner),
        step_in_grad.reshape(rows, local_heads),
        z_weight,
        x_weight,
        step_weight,
    )
    x_weight_grad = jnp.einsum("btd,btc->dc", normed, x_in_grad, preferred_element_type=F32)
    normed_sum = halved(normed_partial, "head")
    x_blocks, bc_other, _ = lax.optimization_barrier(
        (to_blocks(x_weight_grad, seq_size), bc_other, normed_sum)
    )
    x_parts = exchanged(x_blocks, "seq")
    normed_far = swapped(normed_sum, "head", axis_masks("head")[-1])

    scalars = jnp.concatenate(
        [lengths, jnp.stack([seq_index * local_len, near_bit("head", 1)]).astype(jnp.int32)]
    )
    bc_raw_grad, bc_first, bc_last, bc_tap_sums = bc_backward(
        scalars,
        bc_half,
        bc_other,
        mixed_in,
        edge_rows,
        taps,
    )
    bc_in_grad = joined_edges(bc_raw_grad, bc_first, bc_last, conv_weight[:, local_inner:])
    x_own = jnp.sum(x_parts.astype(F32), axis=0).astype(BF16)
    bc_weight_grad = jnp.einsum("btd,btc->dc", normed, bc_in_grad, preferred_element_type=F32)
    bc_blocks = to_blocks(bc_weight_grad, seq_size)
    bc_parts = exchanged(bc_blocks, "seq")
    early_all, _ = lax.optimization_barrier((early_all, bc_blocks))
    early_sums = early_all.reshape(2, model_width, local_inner)
    flat_tokens = inputs.reshape(rows, model_width)
    block_out = merge_call(
        out_kernel,
        scalars,
        projected_half,
        projected_other,
        (flat_tokens, out_scale.reshape(rows, 1)),
        [row_block(model_width), row_block(1)],
        row_block(model_width),
        jax.ShapeDtypeStruct((rows, model_width), BF16),
    )
    out_updated = adam_update(
        proj_out,
        proj_out_mean,
        proj_out_square,
        early_sums[0].astype(F32),
        LEARNING_RATES[-1],
        WEIGHT_DECAYS[-1],
    )
    normed_far, block_out, out_updated, _, x_own = lax.optimization_barrier(
        (normed_far, block_out, out_updated, bc_blocks, x_own)
    )
    x_all = lax.all_gather(x_own, "seq")
    x_sum = x_all.reshape(model_width, local_inner)
    block_out = block_out.reshape(inputs.shape)
    normed_half, normed_other = regathered(added(normed_sum, normed_far), "head")
    input_grad, norm_gain_grad = merge_call(
        functools.partial(tail_kernel, local_len),
        scalars,
        normed_half,
        normed_other,
        (
            bc_in_grad.reshape(rows, 2 * state_width),
            bc_weight,
            flat_tokens,
            cotangent.reshape(rows, model_width),
            norm_gain[None],
        ),
        [
            row_block(2 * state_width),
            whole_block(bc_weight.shape),
            row_block(model_width),
            row_block(model_width),
            whole_block((1, model_width)),
        ],
        [row_block(model_width), whole_block((1, model_width))],
        [
            jax.ShapeDtypeStruct((rows, model_width), F32),
            jax.ShapeDtypeStruct((1, model_width), F32),
        ],
    )
    bc_parts, input_grad = lax.optimization_barrier((bc_parts, input_grad))
    input_grad = input_grad.reshape(inputs.shape)
    bc_own = jnp.sum(bc_parts.astype(F32), axis=0).astype(BF16)
    x_sum, bc_own = lax.optimization_barrier((x_sum, bc_own))
    bc_all = exchanged(jnp.broadcast_to(bc_own[None], bc_parts.shape), "seq")
    step_weight_grad = jnp.einsum("btd,bth->hd", normed, step_in_grad, preferred_element_type=F32)
    conv_inner_grad = x_tap_sums[: CONV + 1]
    conv_bc_grad = bc_tap_sums[: CONV + 1]
    head_grad = head_totals[:3]
    small_grads = (
        norm_gain_grad[0],
        step_weight_grad,
        conv_inner_grad,
        conv_bc_grad,
        head_grad,
        gate_gain_grad,
    )
    flat = jnp.concatenate([part.reshape(-1) for part in small_grads])
    count = flat.shape[0]
    flat = jnp.pad(flat, (0, -count % 1024)).reshape(-1, 128)
    flat = doubling_sum(flat, "seq").reshape(-1)
    small_sums, at = [], 0
    for part in small_grads:
        small_sums.append(flat[at : at + part.size].reshape(part.shape))
        at += part.size

    summed_grads = (
        small_sums[0],
        jnp.stack([early_sums[1], x_sum], axis=1),
        bc_all.reshape(bc_weight_grad.shape).astype(F32),
        small_sums[1].T,
        small_sums[2],
        small_sums[3],
        small_sums[4],
        small_sums[5],
        None,
    )
    params = (
        norm_gain,
        proj_zx,
        proj_bc,
        proj_step,
        conv_inner,
        conv_bc,
        head_params,
        gate_gain,
        proj_out,
    )
    means = (
        norm_gain_mean,
        proj_zx_mean,
        proj_bc_mean,
        proj_step_mean,
        conv_inner_mean,
        conv_bc_mean,
        head_params_mean,
        gate_gain_mean,
        proj_out_mean,
    )
    squares = (
        norm_gain_square,
        proj_zx_square,
        proj_bc_square,
        proj_step_square,
        conv_inner_square,
        conv_bc_square,
        head_params_square,
        gate_gain_square,
        proj_out_square,
    )
    results = [block_out, input_grad]
    for weight, mean_old, square_old, gradient, step_rate, decay_weight in zip(
        params, means, squares, summed_grads, LEARNING_RATES, WEIGHT_DECAYS
    ):
        if gradient is None:
            updated = out_updated
        elif weight.ndim == 3:
            updated = adam_tiles(weight, mean_old, square_old, gradient, step_rate, decay_weight)
        else:
            updated = adam_update(weight, mean_old, square_old, gradient, step_rate, decay_weight)
        results.extend(updated)
    return tuple(results)


def solution(mesh):
    in_specs = (
        P(None, "seq", None),
        P(None, "seq", None),
        P(),
        P(),
        P(),
        P(),
        P(None, None, "head"),
        P(None, None, "head"),
        P(None, None, "head"),
        P(),
        P(),
        P(),
        P(None, "head"),
        P(None, "head"),
        P(None, "head"),
        P(None, "head"),
        P(None, "head"),
        P(None, "head"),
        P(),
        P(),
        P(),
        P(None, "head"),
        P(None, "head"),
        P(None, "head"),
        P("head"),
        P("head"),
        P("head"),
        P(None, "head"),
        P(None, "head"),
        P(None, "head"),
    )
    out_specs = (
        P(None, "seq", None),
        P(None, "seq", None),
        P(),
        P(),
        P(),
        P(None, None, "head"),
        P(None, None, "head"),
        P(None, None, "head"),
        P(),
        P(),
        P(),
        P(None, "head"),
        P(None, "head"),
        P(None, "head"),
        P(None, "head"),
        P(None, "head"),
        P(None, "head"),
        P(),
        P(),
        P(),
        P(None, "head"),
        P(None, "head"),
        P(None, "head"),
        P("head"),
        P("head"),
        P("head"),
        P(None, "head"),
        P(None, "head"),
        P(None, "head"),
    )
    return jax.shard_map(shards, mesh=mesh, in_specs=in_specs, out_specs=out_specs, check_vma=False)
```
